32 devices in a mesh: narrow: 4 (over y, core), wide: 8 (over z, x).
Axes of the slice: x: 2, y: 2, z: 4, core: 2. Of those that a mesh axis runs over, the one named last changes fastest.
Arguments:
- points: float32 [2, 4096], P(None, ('narrow', 'wide')), may hold values from 0 to 1
- quad_weight: float32 [4096], P(('narrow', 'wide')), may hold values from 7.324219e-05 to 0.0007324219
- basis: float32 [4, 2, 4096, 128], P(None, None, ('narrow', 'wide')), may hold values from -6 to 6
- jacobi: float32 [2, 4096], P(None, ('narrow', 'wide')), may hold values from 0.5 to 2
- near_panel: int32 [256, 12], P(('narrow', 'wide')), may hold values from 0 to 255, as said below
- near_count: int32 [256], P(('narrow', 'wide')), may hold values from 2 to 12, as said below
- near_block: bfloat16 [256, 12, 32, 32], P(('narrow', 'wide')), may hold values from -0.875 to 0.875
- agg_index: int32 [2, 4096], P(None, ('narrow', 'wide')), may hold values from 0 to 47
- coarse_inverse: float32 [4, 384, 1536], P(None, 'wide', 'narrow'), may hold values from -0.1 to 0.5
Outputs:
- new_block: float32 [2, 4096, 128], P(None, ('narrow', 'wide'))
- hessenberg: float32 [4, 128, 128], replicated
- upper_factor: float32 [128, 128], replicated
The draws below stay inside these ranges and needn't reach their ends.
Inputs may be any that keep to these rules, and one draw needn't show every extreme that they name: near_panel[p, 0] = p; every entry lies within 4 panels of p in panel order, and some entry lies exactly 4 panels away. `near_count`: slots at or beyond a panel's count are not used; some panel uses all 12.
All inputs are finite; a program needn't handle non-finite values.
Results may differ from the reference program's by a relative error of at most 0.0027.
The reference program's roundings to bfloat16 on the way count: a program that leaves them out, or rounds other values in their place, can miss the bound.
Values may be sent and summed in bfloat16 or wider, within the bound.
No kernel may reach another device: no remote copies, remote signals or barrier semaphores. Data moves between devices by JAX's collectives and lax.ppermute only.
A program may use at most 64 MiB of HBM per device.

```python
import math
import jax
import jax.numpy as jnp
from jax import lax

Q = 16
NRHS = 128
KB = 4
MAXN = 12
SPAN = 4
CB = 48
PTS_DEV = 128
PANELS = 256
POINTS = 4096
NC = 1536
N_NARROW = 4


def draw_near_panel(key, part):
    own = jnp.arange(PANELS, dtype=jnp.int32)[:, None]
    slot_index = jnp.arange(MAXN, dtype=jnp.int32)[None, :]
    first_key, second_key, third_key = jax.random.split(jax.random.fold_in(key, 11), 3)
    spread = jax.random.randint(first_key, (PANELS, MAXN), -SPAN, SPAN + 1)
    side_sign = 2 * jax.random.randint(second_key, (PANELS, 1), 0, 2) - 1
    chosen = jax.random.randint(third_key, (), SPAN, PANELS - SPAN)
    offset = jnp.where(slot_index == 0, 0, jnp.where(slot_index == 1, side_sign, spread))
    offset = jnp.where((slot_index == 2) & (own == chosen), SPAN, offset)
    return jnp.clip(own + offset, 0, PANELS - 1).astype(jnp.int32)


def draw_near_count(key, part):
    first_key, second_key = jax.random.split(jax.random.fold_in(key, 23), 2)
    counts = jax.random.randint(first_key, (PANELS,), 2, MAXN + 1)
    chosen = jax.random.randint(second_key, (), 0, PANELS)
    return jnp.where(jnp.arange(PANELS, dtype=jnp.int32) == chosen, MAXN, counts).astype(jnp.int32)


def draw_coarse_inverse(key, part):
    row_span = NC // N_NARROW
    first_key, second_key = jax.random.split(jax.random.fold_in(key, 37), 2)
    shape = (N_NARROW, row_span, NC)
    row_id = jnp.arange(N_NARROW, dtype=jnp.int32)[:, None, None] * row_span + jnp.arange(row_span, dtype=jnp.int32)[None, :, None]
    col_id = jnp.arange(NC, dtype=jnp.int32)[None, None, :]
    spread = jax.random.normal(first_key, shape, jnp.float32) * (0.2 / math.sqrt(NC))
    diagonal = jax.random.uniform(second_key, (N_NARROW, row_span, 1), jnp.float32, 0.1, 0.4)
    return jnp.where(row_id == col_id, diagonal + spread, spread).astype(jnp.float32)


def set_ends(result, stream_key, low, top_value):
    longest = result.shape.index(max(result.shape))
    spots = []
    for shift in (0, 1):
        where = [jax.random.randint(jax.random.fold_in(stream_key, axis), (), 0, length) for axis, length in enumerate(result.shape)]
        where[longest] = (where[longest] + shift) % result.shape[longest]
        spots.append(tuple(where))
    return result.at[spots[0]].set(low).at[spots[1]].set(top_value)


def level_of(own_key, shape, cuts, smallest, top_value):
    loudness, own = 1.0, jax.random.fold_in(own_key, 6)
    for dim, parts in cuts:
        heights = jnp.exp(jax.random.uniform(jax.random.fold_in(own, dim), (parts,), jnp.float32, smallest / len(cuts), top_value / len(cuts)))
        loudness = loudness * jnp.repeat(heights, shape[dim] // parts).reshape([-1 if axis == dim else 1 for axis in range(len(shape))])
    return loudness


def gaussian(own_key, extent, scale, bound, pieces=(), kind=jnp.bfloat16):
    factor_of = level_of(own_key, extent, pieces, -0.22, 0.18) if pieces else 1.0
    values = jax.random.normal(own_key, extent, jnp.float32) * scale * factor_of
    return jnp.minimum(jnp.maximum(values, -bound), bound).astype(kind)


def setup_inputs(seed: int = 0) -> dict:
    arg_keys = jax.random.split(jax.random.key(seed), 10)
    return {
        "points": jnp.clip(1.0 * jax.random.uniform(arg_keys[0], (2, POINTS), jnp.float32) ** level_of(arg_keys[0], (2, POINTS), ((1, 32),), -0.2, 0.2), 0.0, 1.0),
        "quad_weight": jnp.clip(jnp.exp(math.log(0.0007324219) - 2.3025851 * jax.random.uniform(arg_keys[1], (POINTS,), jnp.float32) ** level_of(arg_keys[1], (POINTS,), ((0, 32),), -0.2, 0.2)), 7.324219041038305e-05, 0.0007324219),
        "basis": gaussian(arg_keys[2], (KB, 2, POINTS, NRHS), 0.65, 6.0, ((2, 32),), jnp.float32),
        "jacobi": jnp.clip(jnp.exp(math.log(2.0) - 1.3862944 * jax.random.uniform(arg_keys[3], (2, POINTS), jnp.float32) ** level_of(arg_keys[3], (2, POINTS), ((1, 32),), -0.2, 0.2)), 0.5, 2.0),
        "near_panel": draw_near_panel(jax.random.fold_in(arg_keys[9], 71), 0),
        "near_count": draw_near_count(jax.random.fold_in(arg_keys[9], 71), 0),
        "near_block": gaussian(arg_keys[6], (PANELS, MAXN, 2 * Q, 2 * Q), 0.06, 0.875, ((0, 32),)),
        "agg_index": set_ends(jax.random.randint(arg_keys[7], (2, POINTS), 0, CB), jax.random.fold_in(arg_keys[7], 1), 0, CB - 1).astype(jnp.int32),
        "coarse_inverse": draw_coarse_inverse(jax.random.fold_in(arg_keys[9], 71), 0),
    }


NU = 0.3
DELTA2 = 1e-05
ELASTIC = 40.0
HIGH = lax.Precision.HIGHEST

def far_kernel(targets, sources, weights):
    delta_x = targets[0][:, None] - sources[0][None, :]
    delta_y = targets[1][:, None] - sources[1][None, :]
    square_dist = delta_x * delta_x + delta_y * delta_y + DELTA2
    factor = ELASTIC * weights[None, :]
    log_part = -0.5 * (3.0 - 4.0 * NU) * jnp.log(square_dist)
    g_xx = factor * (log_part + delta_x * delta_x / square_dist)
    g_xy = factor * (delta_x * delta_y / square_dist)
    g_yy = factor * (log_part + delta_y * delta_y / square_dist)
    first_row = jnp.stack([g_xx, g_xy], axis=1)
    second_row = jnp.stack([g_xy, g_yy], axis=1)
    stacked = jnp.stack([first_row, second_row], axis=0)
    return stacked.reshape(2 * targets.shape[1], 2 * sources.shape[1]).astype(jnp.bfloat16)

def reference(points, quad_weight, basis, jacobi, near_panel, near_count, near_block, agg_index, coarse_inverse):
    newest = basis[KB - 1]
    owner = (jnp.arange(POINTS, dtype=jnp.int32) // PTS_DEV).astype(jnp.int32)
    coarse_id = (owner[None, :] * CB + agg_index).astype(jnp.int32)
    coarse_rhs = jax.ops.segment_sum(newest.reshape(2 * POINTS, NRHS), coarse_id.reshape(2 * POINTS), num_segments=NC)
    inverse_full = coarse_inverse.reshape(NC, NC)
    coarse_sol = jnp.dot(inverse_full.astype(jnp.float32), coarse_rhs.astype(jnp.float32), precision=HIGH, preferred_element_type=jnp.float32)
    precond = (jacobi[:, :, None] * newest + coarse_sol[coarse_id]).astype(jnp.bfloat16)
    fields = precond.reshape(2 * POINTS, NRHS).astype(jnp.float32)
    target_size = math.gcd(POINTS, 512)

    def target_block(block_index):
        offset = block_index * target_size
        targets = lax.dynamic_slice_in_dim(points, offset, target_size, 1)
        kernel_rows = far_kernel(targets, points, quad_weight).astype(jnp.float32)
        product = jnp.dot(kernel_rows.astype(jnp.float32), fields.astype(jnp.float32), precision=HIGH, preferred_element_type=jnp.float32)
        return product.reshape(2, target_size, NRHS)
    far_blocks = lax.map(target_block, jnp.arange(POINTS // target_size, dtype=jnp.int32))
    far = jnp.transpose(far_blocks, (1, 0, 2, 3)).reshape(2, POINTS, NRHS)
    panel_fields = precond.reshape(2, PANELS, Q, NRHS)
    gathered = panel_fields[:, near_panel]
    slot_live = jnp.arange(MAXN, dtype=jnp.int32)[None, :] < near_count[:, None]
    gathered = jnp.where(slot_live[None, :, :, None, None], gathered, jnp.zeros((), gathered.dtype))
    gathered = jnp.transpose(gathered, (1, 2, 0, 3, 4)).reshape(PANELS, MAXN, 2 * Q, NRHS)
    near_terms = jnp.einsum('pkxy,pkyr->pxr', near_block.astype(jnp.float32), gathered.astype(jnp.float32), precision=HIGH)
    near = jnp.transpose(near_terms.reshape(PANELS, 2, Q, NRHS), (1, 0, 2, 3)).reshape(2, POINTS, NRHS)
    image = 0.5 * precond.astype(jnp.float32) + far + near
    weighted = basis * quad_weight[None, None, :, None]
    hessenberg = jnp.einsum('jair,aiw->jrw', weighted, image, precision=HIGH)
    remainder = image - jnp.einsum('jair,jrw->aiw', basis, hessenberg, precision=HIGH)
    gram_matrix = jnp.einsum('air,aiw->rw', remainder * quad_weight[None, :, None], remainder, precision=HIGH)
    lower_factor = jnp.linalg.cholesky(gram_matrix)
    flat = remainder.reshape(2 * POINTS, NRHS)
    solved = jax.scipy.linalg.solve_triangular(lower_factor, flat.T, lower=True)
    new_block = solved.T.reshape(2, POINTS, NRHS)
    return (new_block, hessenberg, lower_factor.T)
```

```python
import math

import jax
import jax.numpy as jnp
from jax import lax
from jax.sharding import PartitionSpec as P

SPAN = 4


NU = 0.3
DELTA2 = 1e-05
ELASTIC = 40.0
HIGH = lax.Precision.HIGHEST
AXES = ("narrow", "wide")


def gather_all(block, axis):
    count = lax.axis_size(axis)
    return lax.all_to_all(
        jnp.broadcast_to(block[None], (count,) + block.shape), axis, 0, 0, tiled=True
    )


def sum_scatter(parts, axis):
    return jnp.sum(lax.all_to_all(parts, axis, 0, 0, tiled=True), axis=0)


def sum_all(block, axis):
    count = lax.axis_size(axis)
    if block.shape[0] % count:
        return lax.psum(block, axis)
    rows = block.shape[0] // count
    mine = sum_scatter(block.reshape((count, rows) + block.shape[1:]), axis)
    return gather_all(mine, axis).reshape(block.shape)


def extended(block, sides, width):
    for axis, dim in sides:
        count = lax.axis_size(axis)
        forward = [(i, i + 1) for i in range(count - 1)]
        backward = [(target, source) for source, target in forward]
        low = lax.ppermute(
            lax.slice_in_dim(block, block.shape[dim] - width, None, axis=dim), axis, forward
        )
        high = lax.ppermute(lax.slice_in_dim(block, 0, width, axis=dim), axis, backward)
        block = jnp.concatenate([low, block, high], axis=dim)
    return block


def far_kernel(targets, sources, weights):
    delta_x = targets[0][:, None] - sources[0][None, :]
    delta_y = targets[1][:, None] - sources[1][None, :]
    square_dist = delta_x * delta_x + delta_y * delta_y + DELTA2
    factor = ELASTIC * weights[None, :]
    log_part = -0.5 * (3.0 - 4.0 * NU) * jnp.log(square_dist)
    g_xx = factor * (log_part + delta_x * delta_x / square_dist)
    g_xy = factor * (delta_x * delta_y / square_dist)
    g_yy = factor * (log_part + delta_y * delta_y / square_dist)
    return (
        g_xx.astype(jnp.bfloat16),
        g_xy.astype(jnp.bfloat16),
        g_yy.astype(jnp.bfloat16),
    )


def dot32(left, right):
    return jnp.dot(left, right, preferred_element_type=jnp.float32)


def body(
    points,
    quad_weight,
    basis,
    jacobi,
    near_panel,
    near_count,
    near_block,
    agg_index,
    coarse_inverse,
):
    block_total = basis.shape[0]
    point_count = basis.shape[2]
    rhs_count = basis.shape[3]
    coarse_count = coarse_inverse.shape[1]
    narrow_count = lax.axis_size("narrow")
    wide_count = lax.axis_size("wide")
    newest = basis[block_total - 1]
    member = (
        agg_index[:, :, None] == jnp.arange(coarse_count, dtype=jnp.int32)[None, None, :]
    ).astype(jnp.float32)
    coarse_rhs = jnp.einsum("apc,apr->cr", member, newest, precision=HIGH)
    coarse_part = jnp.einsum(
        "abc,cr->abr",
        coarse_inverse,
        gather_all(coarse_rhs, "wide").reshape(wide_count * coarse_count, rhs_count),
        precision=HIGH,
    )
    row_groups = coarse_inverse.shape[0]
    coarse_sol = sum_scatter(
        coarse_part.reshape(narrow_count, row_groups * coarse_count // narrow_count, rhs_count),
        "narrow",
    )
    lifted = jnp.einsum("apc,cr->apr", member, coarse_sol, precision=HIGH)
    precond = (jacobi[:, :, None] * newest + lifted).astype(jnp.bfloat16)
    source_info = jnp.concatenate([points, quad_weight[None, :]], axis=0)
    targets = gather_all(points, "narrow")
    targets = jnp.transpose(targets, (1, 0, 2)).reshape(2, narrow_count * point_count)
    source_all = gather_all(source_info, "wide")
    source_all = jnp.transpose(source_all, (1, 0, 2)).reshape(3, wide_count * point_count)
    g_xx, g_xy, g_yy = far_kernel(targets, source_all[0:2], source_all[2])
    fields = gather_all(precond, "wide")
    f_x = fields[:, 0].reshape(wide_count * point_count, rhs_count)
    f_y = fields[:, 1].reshape(wide_count * point_count, rhs_count)
    far_x = dot32(g_xx, f_x) + dot32(g_xy, f_y)
    far_y = dot32(g_xy, f_x) + dot32(g_yy, f_y)
    shape = (narrow_count, point_count, rhs_count)
    far_local = sum_scatter(
        jnp.stack([far_x.reshape(shape), far_y.reshape(shape)], axis=1), "narrow"
    )
    panels_dev = near_panel.shape[0]
    slot_total = near_panel.shape[1]
    nodes = near_block.shape[2] // 2
    padded = extended(precond, ((AXES, 1),), SPAN * nodes)
    panel_fields = padded.reshape(2, panels_dev + 2 * SPAN, nodes, rhs_count)
    local_index = near_panel - lax.axis_index(AXES) * panels_dev + SPAN
    gathered = panel_fields[:, local_index]
    slot_live = jnp.arange(slot_total, dtype=jnp.int32)[None, :] < near_count[:, None]
    gathered = jnp.where(slot_live[None, :, :, None, None], gathered, jnp.zeros((), gathered.dtype))
    gathered = jnp.transpose(gathered, (1, 2, 0, 3, 4)).reshape(
        panels_dev, slot_total, 2 * nodes, rhs_count
    )
    near_terms = jnp.einsum(
        "pkxy,pkyr->pxr", near_block, gathered, preferred_element_type=jnp.float32
    )
    near = jnp.transpose(near_terms.reshape(panels_dev, 2, nodes, rhs_count), (1, 0, 2, 3)).reshape(
        2, point_count, rhs_count
    )
    image = 0.5 * precond.astype(jnp.float32) + far_local + near
    weighted = basis * quad_weight[None, None, :, None]
    local_proj = jnp.einsum("jair,aiw->jrw", weighted, image, precision=HIGH)
    hessenberg = sum_all(
        local_proj.reshape(block_total * rhs_count, rhs_count), AXES
    ).reshape(block_total, rhs_count, rhs_count)
    remainder = image - jnp.einsum("jair,jrw->aiw", basis, hessenberg, precision=HIGH)
    gram_matrix = sum_all(
        jnp.einsum(
            "air,aiw->rw", remainder * quad_weight[None, :, None], remainder, precision=HIGH
        ),
        AXES,
    )
    lower_factor = jnp.linalg.cholesky(gram_matrix)
    flat = remainder.reshape(2 * point_count, rhs_count)
    solved = jax.scipy.linalg.solve_triangular(lower_factor, flat.T, lower=True)
    new_block = solved.T.reshape(2, point_count, rhs_count)
    return (new_block, hessenberg, lower_factor.T)


def solution(mesh):
    in_specs = (
        P(None, ("narrow", "wide")),
        P(("narrow", "wide")),
        P(None, None, ("narrow", "wide"), None),
        P(None, ("narrow", "wide")),
        P(("narrow", "wide"), None),
        P(("narrow", "wide")),
        P(("narrow", "wide"), None, None, None),
        P(None, ("narrow", "wide")),
        P(None, "wide", "narrow"),
    )
    out_specs = (P(None, ("narrow", "wide"), None), P(), P())
    return jax.shard_map(body, mesh=mesh, in_specs=in_specs, out_specs=out_specs, check_vma=False)
```

```python
import math

import jax
import jax.numpy as jnp
from jax import lax
from jax.experimental import pallas as pl
from jax.experimental.pallas import tpu as pltpu
from jax.sharding import PartitionSpec as P

SPAN = 4


NU = 0.3
DELTA2 = 1e-05
ELASTIC = 40.0
HIGH = lax.Precision.HIGHEST
AXES = ("narrow", "wide")


def gather_all(block, axis):
    count = lax.axis_size(axis)
    return lax.all_to_all(
        jnp.broadcast_to(block[None], (count,) + block.shape), axis, 0, 0, tiled=True
    )


def sum_scatter(parts, axis):
    return jnp.sum(lax.all_to_all(parts, axis, 0, 0, tiled=True), axis=0)


def sum_all(block, axis):
    count = lax.axis_size(axis)
    if block.shape[0] % count:
        return lax.psum(block, axis)
    rows = block.shape[0] // count
    mine = sum_scatter(block.reshape((count, rows) + block.shape[1:]), axis)
    return gather_all(mine, axis).reshape(block.shape)


def halo_fields(precond, fields, width):
    narrow_count = lax.axis_size("narrow")
    wide_count = lax.axis_size("wide")
    wide_index = lax.axis_index("wide")
    pairs = []
    for group in range(narrow_count - 1):
        left = group * wide_count + wide_count - 1
        pairs += [(left, left + 1), (left + 1, left)]
    first = precond[:, :width]
    last = precond[:, precond.shape[1] - width :]
    crossed = lax.ppermute(jnp.where(wide_index == 0, first, last), AXES, pairs)
    before = lax.dynamic_index_in_dim(fields, jnp.maximum(wide_index - 1, 0), 0, False)
    after = lax.dynamic_index_in_dim(fields, jnp.minimum(wide_index + 1, wide_count - 1), 0, False)
    low = jnp.where(wide_index == 0, crossed, before[:, before.shape[1] - width :])
    high = jnp.where(wide_index == wide_count - 1, crossed, after[:, :width])
    return jnp.concatenate([low, precond, high], axis=1)


def far_kernel(targets, sources, weights):
    delta_x = targets[0][:, None] - sources[0][None, :]
    delta_y = targets[1][:, None] - sources[1][None, :]
    square_dist = delta_x * delta_x + delta_y * delta_y + DELTA2
    factor = ELASTIC * weights[None, :]
    log_part = -0.5 * (3.0 - 4.0 * NU) * jnp.log(square_dist)
    g_xx = factor * (log_part + delta_x * delta_x / square_dist)
    g_xy = factor * (delta_x * delta_y / square_dist)
    g_yy = factor * (log_part + delta_y * delta_y / square_dist)
    return (
        g_xx.astype(jnp.bfloat16),
        g_xy.astype(jnp.bfloat16),
        g_yy.astype(jnp.bfloat16),
    )


ROWS = 8


def factor_kernel(gram_ref, remainder_ref, upper_ref, new_ref, work_ref, inverse_ref):
    order = gram_ref.shape[0]
    tile = (ROWS, order)
    lane = lax.broadcasted_iota(jnp.int32, tile, 1)
    row = lax.broadcasted_iota(jnp.int32, tile, 0)
    work_ref[...] = gram_ref[...]
    for block in range(order // ROWS):
        start = block * ROWS
        inverse_ref[start : start + ROWS, :] = jnp.where(lane == row + start, 1.0, 0.0)
    for block in range(order // ROWS):
        start = block * ROWS
        own = work_ref[start : start + ROWS, :]
        own_inverse = inverse_ref[start : start + ROWS, :]
        columns = [
            jnp.broadcast_to(own[:, start + m : start + m + 1], tile) for m in range(ROWS)
        ]
        entry = {
            (j, m): jnp.broadcast_to(columns[m][j : j + 1, :], tile)
            for m in range(ROWS)
            for j in range(m, ROWS)
        }
        scale = []
        for m in range(ROWS):
            scale.append(lax.rsqrt(entry[m, m]))
            for j in range(m + 1, ROWS):
                entry[j, m] = entry[j, m] * scale[m]
            for n in range(m + 1, ROWS):
                for j in range(n, ROWS):
                    entry[j, n] = entry[j, n] - entry[j, m] * entry[n, m]
        solved = []
        solved_inverse = []
        for m in range(ROWS):
            upper_row = jnp.broadcast_to(own[m : m + 1, :], tile)
            inverse_row = jnp.broadcast_to(own_inverse[m : m + 1, :], tile)
            for j in range(m):
                upper_row = upper_row - entry[m, j] * solved[j]
                inverse_row = inverse_row - entry[m, j] * solved_inverse[j]
            upper_row = upper_row * scale[m]
            inverse_row = inverse_row * scale[m]
            solved.append(upper_row)
            solved_inverse.append(inverse_row)
        upper_rows = solved[ROWS - 1]
        inverse_rows = solved_inverse[ROWS - 1]
        for m in range(ROWS - 1):
            upper_rows = jnp.where(row == m, solved[m], upper_rows)
            inverse_rows = jnp.where(row == m, solved_inverse[m], inverse_rows)
        upper_ref[start : start + ROWS, :] = jnp.where(lane >= row + start, upper_rows, 0.0)
        inverse_ref[start : start + ROWS, :] = inverse_rows
        for later in range(block + 1, order // ROWS):
            first = later * ROWS
            target = work_ref[first : first + ROWS, :]
            target_inverse = inverse_ref[first : first + ROWS, :]
            multiplier = []
            for m in range(ROWS):
                value = jnp.broadcast_to(target[:, start + m : start + m + 1], tile)
                for j in range(m):
                    value = value - multiplier[j] * entry[m, j]
                multiplier.append(value * scale[m])
            for m in range(ROWS):
                target = target - multiplier[m] * solved[m]
                target_inverse = target_inverse - multiplier[m] * solved_inverse[m]
            work_ref[first : first + ROWS, :] = target
            inverse_ref[first : first + ROWS, :] = target_inverse
    new_ref[...] = lax.dot_general(
        remainder_ref[...],
        inverse_ref[...],
        (((1,), (1,)), ((), ())),
        precision=HIGH,
        preferred_element_type=jnp.float32,
    )


def factor_and_solve(gram_matrix, remainder):
    order = gram_matrix.shape[0]
    return pl.pallas_call(
        factor_kernel,
        out_shape=(
            jax.ShapeDtypeStruct(gram_matrix.shape, jnp.float32),
            jax.ShapeDtypeStruct(remainder.shape, jnp.float32),
        ),
        scratch_shapes=[
            pltpu.VMEM((order, order), jnp.float32),
            pltpu.VMEM((order, order), jnp.float32),
        ],
    )(gram_matrix, remainder)


def dot32(left, right):
    return jnp.dot(left, right, preferred_element_type=jnp.float32)


def body(
    points,
    quad_weight,
    basis,
    jacobi,
    near_panel,
    near_count,
    near_block,
    agg_index,
    coarse_inverse,
):
    block_total = basis.shape[0]
    point_count = basis.shape[2]
    rhs_count = basis.shape[3]
    coarse_count = coarse_inverse.shape[1]
    narrow_count = lax.axis_size("narrow")
    wide_count = lax.axis_size("wide")
    newest = basis[block_total - 1]
    member = (
        agg_index[:, :, None] == jnp.arange(coarse_count, dtype=jnp.int32)[None, None, :]
    ).astype(jnp.float32)
    coarse_rhs = jnp.einsum("apc,apr->cr", member, newest, precision=HIGH)
    source_info = jnp.concatenate([points, quad_weight[None, :]], axis=0)
    from_wide = gather_all(jnp.concatenate([coarse_rhs, source_info], axis=0), "wide")
    coarse_part = jnp.einsum(
        "abc,cr->abr",
        coarse_inverse,
        from_wide[:, :coarse_count].reshape(wide_count * coarse_count, rhs_count),
        precision=HIGH,
    )
    to_narrow = jnp.concatenate(
        [coarse_part, jnp.broadcast_to(points[None], (narrow_count,) + points.shape)], axis=1
    )
    from_narrow = lax.all_to_all(to_narrow, "narrow", 0, 0, tiled=True)
    coarse_sol = jnp.sum(from_narrow[:, :coarse_count], axis=0)
    lifted = jnp.einsum("apc,cr->apr", member, coarse_sol, precision=HIGH)
    precond = (jacobi[:, :, None] * newest + lifted).astype(jnp.bfloat16)
    targets = jnp.transpose(from_narrow[:, coarse_count:], (1, 0, 2)).reshape(
        2, narrow_count * point_count
    )
    source_all = jnp.transpose(from_wide[:, coarse_count:], (1, 0, 2)).reshape(
        3, wide_count * point_count
    )
    g_xx, g_xy, g_yy = far_kernel(targets, source_all[0:2], source_all[2])
    fields = gather_all(precond, "wide")
    f_x = fields[:, 0].reshape(wide_count * point_count, rhs_count)
    f_y = fields[:, 1].reshape(wide_count * point_count, rhs_count)
    far_x = dot32(g_xx, f_x) + dot32(g_xy, f_y)
    far_y = dot32(g_xy, f_x) + dot32(g_yy, f_y)
    shape = (narrow_count, point_count, rhs_count)
    far_local = sum_scatter(
        jnp.stack([far_x.reshape(shape), far_y.reshape(shape)], axis=1), "narrow"
    )
    panels_dev = near_panel.shape[0]
    slot_total = near_panel.shape[1]
    nodes = near_block.shape[2] // 2
    padded = halo_fields(precond, fields, SPAN * nodes)
    panel_fields = padded.reshape(2, panels_dev + 2 * SPAN, nodes, rhs_count)
    local_index = near_panel - lax.axis_index(AXES) * panels_dev + SPAN
    gathered = panel_fields[:, local_index]
    slot_live = jnp.arange(slot_total, dtype=jnp.int32)[None, :] < near_count[:, None]
    gathered = jnp.where(slot_live[None, :, :, None, None], gathered, jnp.zeros((), gathered.dtype))
    gathered = jnp.transpose(gathered, (1, 2, 0, 3, 4)).reshape(
        panels_dev, slot_total, 2 * nodes, rhs_count
    )
    near_terms = jnp.einsum(
        "pkxy,pkyr->pxr", near_block, gathered, preferred_element_type=jnp.float32
    )
    near = jnp.transpose(near_terms.reshape(panels_dev, 2, nodes, rhs_count), (1, 0, 2, 3)).reshape(
        2, point_count, rhs_count
    )
    image = 0.5 * precond.astype(jnp.float32) + far_local + near
    weighted = basis * quad_weight[None, None, :, None]
    local_proj = jnp.einsum("jair,aiw->jrw", weighted, image, precision=HIGH)
    hessenberg = sum_all(
        local_proj.reshape(block_total * rhs_count, rhs_count), AXES
    ).reshape(block_total, rhs_count, rhs_count)
    remainder = image - jnp.einsum("jair,jrw->aiw", basis, hessenberg, precision=HIGH)
    gram_matrix = sum_all(
        jnp.einsum(
            "air,aiw->rw", remainder * quad_weight[None, :, None], remainder, precision=HIGH
        ),
        AXES,
    )
    upper_factor, new_block = factor_and_solve(
        gram_matrix, remainder.reshape(2 * point_count, rhs_count)
    )
    return (new_block.reshape(2, point_count, rhs_count), hessenberg, upper_factor)


def solution(mesh):
    in_specs = (
        P(None, ("narrow", "wide")),
        P(("narrow", "wide")),
        P(None, None, ("narrow", "wide"), None),
        P(None, ("narrow", "wide")),
        P(("narrow", "wide"), None),
        P(("narrow", "wide")),
        P(("narrow", "wide"), None, None, None),
        P(None, ("narrow", "wide")),
        P(None, "wide", "narrow"),
    )
    out_specs = (P(None, ("narrow", "wide"), None), P(), P())
    return jax.shard_map(body, mesh=mesh, in_specs=in_specs, out_specs=out_specs, check_vma=False)
```

```python
import jax
import jax.numpy as jnp
from jax import lax
from jax.experimental import pallas as pl
from jax.experimental.pallas import tpu as pltpu
from jax.sharding import PartitionSpec as P

SPAN = 4


NU = 0.3
DELTA2 = 1e-05
ELASTIC = 40.0
HIGH = lax.Precision.HIGHEST
AXES = ("narrow", "wide")
EXTRA = 8
ROWS = 8
SMEM = pl.BlockSpec(memory_space=pltpu.SMEM)
VMEM = pl.BlockSpec(memory_space=pltpu.VMEM)
PARAMS = pltpu.CompilerParams(vmem_limit_bytes=48 * 1024 * 1024)


def dot_rows(left, right, precision=HIGH):
    return lax.dot_general(
        left, right, (((1,), (0,)), ((), ())), precision=precision, preferred_element_type=jnp.float32
    )


def dot_first(left, right):
    return lax.dot_general(
        left, right, (((0,), (0,)), ((), ())), precision=HIGH, preferred_element_type=jnp.float32
    )


def as_column(row, width):
    return jnp.transpose(jnp.broadcast_to(row, (width, row.shape[1])))


def swap(block, axis, offset):
    count = lax.axis_size(axis)
    return lax.ppermute(block, axis, [(i, i ^ offset) for i in range(count)])


def gather_relative(block, axis):
    return [block] + [swap(block, axis, k) for k in range(1, lax.axis_size(axis))]


def gather_all(copies, axis):
    return lax.all_to_all(copies, axis, 0, 0, tiled=True)


def restrict_kernel(agg_ref, newest_ref, points_ref, weight_ref, pack_ref):
    coarse_count = pack_ref.shape[0] - EXTRA
    point_count = newest_ref.shape[1]
    ids = lax.broadcasted_iota(jnp.int32, (coarse_count, point_count), 0)
    total = None
    for a in range(2):
        member = jnp.where(ids == agg_ref[a : a + 1, :], 1.0, 0.0)
        term = dot_rows(member, newest_ref[a])
        total = term if total is None else total + term
    pack_ref[:coarse_count, :] = total
    pack_ref[coarse_count:, :] = jnp.concatenate(
        [points_ref[...], weight_ref[...], jnp.zeros((EXTRA - 3, point_count), jnp.float32)], axis=0
    )


def coarse_kernel(index_ref, inverse_ref, points_ref, *refs):
    wide_count = inverse_ref.shape[2] // inverse_ref.shape[1]
    narrow_count = inverse_ref.shape[0]
    coarse_count = inverse_ref.shape[1]
    packs = refs[:wide_count]
    outs = refs[wide_count : wide_count + narrow_count]
    rhs_ref = refs[wide_count + narrow_count]
    narrow_index = index_ref[0]
    wide_index = index_ref[1]
    for k in range(wide_count):
        first = pl.multiple_of((wide_index ^ k) * coarse_count, 8)
        rhs_ref[pl.ds(first, coarse_count), :] = packs[k][:coarse_count, :]
    tail = jnp.concatenate(
        [points_ref[...], jnp.zeros((EXTRA - 2, points_ref.shape[1]), jnp.float32)], axis=0
    )
    for k in range(narrow_count):
        outs[k][:coarse_count, :] = dot_rows(inverse_ref[narrow_index ^ k], rhs_ref[...])
        outs[k][coarse_count:, :] = tail


def precond_kernel(index_ref, agg_ref, jacobi_ref, newest_ref, *refs):
    parts = refs[:-2]
    precond_ref, edge_ref = refs[-2:]
    coarse_count = parts[0].shape[0] - EXTRA
    point_count = newest_ref.shape[1]
    rhs_count = newest_ref.shape[2]
    width = edge_ref.shape[1]
    coarse_sol = parts[0][:coarse_count, :]
    for part in parts[1:]:
        coarse_sol = coarse_sol + part[:coarse_count, :]
    ids = lax.broadcasted_iota(jnp.int32, (coarse_count, point_count), 0)
    for a in range(2):
        member = jnp.where(ids == agg_ref[a : a + 1, :], 1.0, 0.0)
        lifted = dot_first(member, coarse_sol)
        value = as_column(jacobi_ref[a : a + 1, :], rhs_count) * newest_ref[a] + lifted
        precond_ref[a] = value.astype(jnp.bfloat16)
    first = pl.multiple_of(jnp.where(index_ref[1] == 0, 0, point_count - width), 16)
    for a in range(2):
        edge_ref[a] = precond_ref[a, pl.ds(first, width), :]


def matrix_kernel(*refs):
    matrix_ref = refs[-1]
    point_count = refs[0].shape[1]
    source_count = matrix_ref.shape[3] // point_count
    sources = refs[:source_count]
    targets = refs[source_count:-1]
    coarse_count = sources[0].shape[0] - EXTRA
    for k in range(len(targets)):

        @pl.when(pl.program_id(0) == k)
        def _(k=k):
            target = targets[k][coarse_count:, :]
            target_x = as_column(target[0:1, :], point_count)
            target_y = as_column(target[1:2, :], point_count)
            for s in range(source_count):
                source = sources[s][coarse_count:, :]
                delta_x = target_x - source[0:1, :]
                delta_y = target_y - source[1:2, :]
                factor = ELASTIC * source[2:3, :]
                square_x = delta_x * delta_x
                square_y = delta_y * delta_y
                square_dist = square_x + square_y + DELTA2
                inverse = 1.0 / square_dist
                log_part = (-0.5 * (3.0 - 4.0 * NU)) * jnp.log(square_dist)
                lanes = slice(s * point_count, (s + 1) * point_count)
                matrix_ref[0, 0, :, lanes] = (factor * (log_part + square_x * inverse)).astype(
                    jnp.bfloat16
                )
                matrix_ref[0, 1, :, lanes] = (factor * (delta_x * delta_y * inverse)).astype(
                    jnp.bfloat16
                )
                matrix_ref[0, 2, :, lanes] = (factor * (log_part + square_y * inverse)).astype(
                    jnp.bfloat16
                )


def far_kernel(matrix_ref, *refs):
    keep_ref, send_ref, fields_ref = refs[-3:]
    fields = refs[:-3]
    point_count = fields[0].shape[1]
    step = pl.program_id(0)

    @pl.when(step == 0)
    def _():
        for s, field in enumerate(fields):
            for b in range(2):
                fields_ref[b, s * point_count : (s + 1) * point_count, :] = field[b]

    out_x = dot_rows(matrix_ref[0, 0], fields_ref[0], None) + dot_rows(
        matrix_ref[0, 1], fields_ref[1], None
    )
    out_y = dot_rows(matrix_ref[0, 1], fields_ref[0], None) + dot_rows(
        matrix_ref[0, 2], fields_ref[1], None
    )

    @pl.when(step % 2 == 0)
    def _():
        keep_ref[0, 0] = out_x
        keep_ref[0, 1] = out_y

    @pl.when(step % 2 == 1)
    def _():
        send_ref[0, 0] = out_x
        send_ref[0, 1] = out_y


def near_kernel(index_ref, panel_ref, count_ref, block_ref, crossed_ref, *refs):
    out_ref, line_ref, gathered_ref = refs[-3:]
    fields = refs[:-3]
    wide_count = len(fields)
    point_count = fields[0].shape[1]
    width = crossed_ref.shape[1]
    panels_dev, double_nodes, _ = block_ref.shape
    nodes = double_nodes // 2
    slot_total = panel_ref.shape[1]
    wide_index = index_ref[1]
    for b in range(2):
        line_ref[b, :width, :] = crossed_ref[b]
        line_ref[b, width + wide_count * point_count :, :] = crossed_ref[b]
        for k in range(wide_count):
            first = pl.multiple_of((wide_index ^ k) * point_count + width, 16)
            line_ref[b, pl.ds(first, point_count), :] = fields[k][b]
    group_start = index_ref[0] * (wide_count * panels_dev)
    lane = lax.broadcasted_iota(jnp.int32, block_ref.shape[1:], 1)
    for p in range(panels_dev):
        for k in range(slot_total):
            first = pl.multiple_of((panel_ref[p, k] - group_start) * nodes + width, 16)
            for b in range(2):
                row = (k * 2 + b) * nodes
                gathered_ref[p, row : row + nodes, :] = line_ref[b, pl.ds(first, nodes), :]
        blocks = jnp.where(
            lane < count_ref[p] * double_nodes, block_ref[p].astype(jnp.float32), 0.0
        ).astype(jnp.bfloat16)
        near = dot_rows(blocks, gathered_ref[p], None)
        for a in range(2):
            rows = slice(p * nodes, (p + 1) * nodes)
            own = fields[0][a, rows, :].astype(jnp.float32)
            out_ref[a, rows, :] = 0.5 * own + near[a * nodes : (a + 1) * nodes, :]


def project_kernel(weight_ref, basis_ref, base_ref, keep_ref, arrived_ref, image_ref, proj_ref):
    block_total, _, _, rhs_count = basis_ref.shape
    weight = as_column(weight_ref[...], rhs_count)
    weighted = []
    for a in range(2):
        image = base_ref[a] + keep_ref[0, a] + arrived_ref[0, a]
        image_ref[a] = image
        weighted.append(image * weight)
    for j in range(block_total):
        proj_ref[j] = dot_first(basis_ref[j, 0], weighted[0]) + dot_first(
            basis_ref[j, 1], weighted[1]
        )


def sum_kernel(parts_ref, out_ref):
    total = jnp.sum(parts_ref[...], axis=0)
    for k in range(out_ref.shape[0]):
        out_ref[k] = total


def remainder_kernel(weight_ref, basis_ref, image_ref, hess_ref, remainder_ref, gram_ref):
    block_total, _, _, rhs_count = basis_ref.shape
    weight = as_column(weight_ref[...], rhs_count)
    gram = None
    for a in range(2):
        value = image_ref[a]
        for j in range(block_total):
            value = value - dot_rows(basis_ref[j, a], hess_ref[j])
        remainder_ref[a] = value
        term = dot_first(value * weight, value)
        gram = term if gram is None else gram + term
    gram_ref[...] = gram


def factor_kernel(gram_ref, remainder_ref, upper_ref, new_ref, work_ref, inverse_ref):
    order = gram_ref.shape[0]
    tile = (ROWS, order)
    lane = lax.broadcasted_iota(jnp.int32, tile, 1)
    row = lax.broadcasted_iota(jnp.int32, tile, 0)
    work_ref[...] = gram_ref[...]
    for block in range(order // ROWS):
        start = block * ROWS
        inverse_ref[start : start + ROWS, :] = jnp.where(lane == row + start, 1.0, 0.0)
    for block in range(order // ROWS):
        start = block * ROWS
        own = work_ref[start : start + ROWS, :]
        own_inverse = inverse_ref[start : start + ROWS, :]
        columns = [
            jnp.broadcast_to(own[:, start + m : start + m + 1], tile) for m in range(ROWS)
        ]
        entry = {
            (j, m): jnp.broadcast_to(columns[m][j : j + 1, :], tile)
            for m in range(ROWS)
            for j in range(m, ROWS)
        }
        scale = []
        for m in range(ROWS):
            scale.append(lax.rsqrt(entry[m, m]))
            for j in range(m + 1, ROWS):
                entry[j, m] = entry[j, m] * scale[m]
            for n in range(m + 1, ROWS):
                for j in range(n, ROWS):
                    entry[j, n] = entry[j, n] - entry[j, m] * entry[n, m]
        solved = []
        solved_inverse = []
        for m in range(ROWS):
            upper_row = jnp.broadcast_to(own[m : m + 1, :], tile)
            inverse_row = jnp.broadcast_to(own_inverse[m : m + 1, :], tile)
            for j in range(m):
                upper_row = upper_row - entry[m, j] * solved[j]
                inverse_row = inverse_row - entry[m, j] * solved_inverse[j]
            upper_row = upper_row * scale[m]
            inverse_row = inverse_row * scale[m]
            solved.append(upper_row)
            solved_inverse.append(inverse_row)
        upper_rows = solved[ROWS - 1]
        inverse_rows = solved_inverse[ROWS - 1]
        for m in range(ROWS - 1):
            upper_rows = jnp.where(row == m, solved[m], upper_rows)
            inverse_rows = jnp.where(row == m, solved_inverse[m], inverse_rows)
        upper_ref[start : start + ROWS, :] = jnp.where(lane >= row + start, upper_rows, 0.0)
        inverse_ref[start : start + ROWS, :] = inverse_rows
        for later in range(block + 1, order // ROWS):
            first = later * ROWS
            target = work_ref[first : first + ROWS, :]
            target_inverse = inverse_ref[first : first + ROWS, :]
            multiplier = []
            for m in range(ROWS):
                value = jnp.broadcast_to(target[:, start + m : start + m + 1], tile)
                for j in range(m):
                    value = value - multiplier[j] * entry[m, j]
                multiplier.append(value * scale[m])
            for m in range(ROWS):
                target = target - multiplier[m] * solved[m]
                target_inverse = target_inverse - multiplier[m] * solved_inverse[m]
            work_ref[first : first + ROWS, :] = target
            inverse_ref[first : first + ROWS, :] = target_inverse
    new_ref[...] = lax.dot_general(
        remainder_ref[...],
        inverse_ref[...],
        (((1,), (1,)), ((), ())),
        precision=HIGH,
        preferred_element_type=jnp.float32,
    )


def factor_and_solve(gram_matrix, remainder):
    order = gram_matrix.shape[0]
    return pl.pallas_call(
        factor_kernel,
        out_shape=(
            jax.ShapeDtypeStruct(gram_matrix.shape, jnp.float32),
            jax.ShapeDtypeStruct(remainder.shape, jnp.float32),
        ),
        scratch_shapes=[
            pltpu.VMEM((order, order), jnp.float32),
            pltpu.VMEM((order, order), jnp.float32),
        ],
    )(gram_matrix, remainder)


def f32(*shape):
    return jax.ShapeDtypeStruct(shape, jnp.float32)


def b16(*shape):
    return jax.ShapeDtypeStruct(shape, jnp.bfloat16)


def call(kernel, out_shape, operands, scalars=0, scratch=()):
    many = isinstance(out_shape, (tuple, list))
    return pl.pallas_call(
        kernel,
        out_shape=out_shape,
        in_specs=[SMEM] * scalars + [VMEM] * (len(operands) - scalars),
        out_specs=[VMEM] * len(out_shape) if many else VMEM,
        scratch_shapes=list(scratch),
        compiler_params=PARAMS,
    )(*operands)


def sum_everywhere(block):
    count = lax.axis_size(AXES)
    if block.shape[0] % count:
        return lax.psum(block, AXES)
    parts = block.reshape((count, block.shape[0] // count) + block.shape[1:])
    parts = lax.all_to_all(parts, AXES, 0, 0, tiled=True)
    copies = call(sum_kernel, f32(*parts.shape), (parts,))
    return gather_all(copies, AXES).reshape(block.shape)


def body(
    points,
    quad_weight,
    basis,
    jacobi,
    near_panel,
    near_count,
    near_block,
    agg_index,
    coarse_inverse,
):
    block_total, _, point_count, rhs_count = basis.shape
    coarse_count = coarse_inverse.shape[1]
    narrow_count = lax.axis_size("narrow")
    wide_count = lax.axis_size("wide")
    panels_dev, slot_total = near_panel.shape
    nodes = near_block.shape[2] // 2
    width = SPAN * nodes
    pack_rows = coarse_count + EXTRA
    index = jnp.stack([lax.axis_index("narrow"), lax.axis_index("wide")]).astype(jnp.int32)
    newest = basis[block_total - 1]
    weight_row = quad_weight[None, :]

    pack = call(
        restrict_kernel, f32(pack_rows, point_count), (agg_index, newest, points, weight_row)
    )
    packs = gather_relative(pack, "wide")
    parts = call(
        coarse_kernel,
        [f32(pack_rows, rhs_count)] * narrow_count,
        (index, coarse_inverse, points, *packs),
        1,
        [pltpu.VMEM((wide_count * coarse_count, rhs_count), jnp.float32)],
    )
    arrived = [parts[0]] + [swap(parts[k], "narrow", k) for k in range(1, narrow_count)]
    precond, edge = call(
        precond_kernel,
        [b16(2, point_count, rhs_count), b16(2, width, rhs_count)],
        (index, agg_index, jacobi, newest, *arrived),
        1,
    )
    pairs = []
    for group in range(narrow_count - 1):
        left = group * wide_count + wide_count - 1
        pairs += [(left, left + 1), (left + 1, left)]
    fields = gather_relative(precond, "wide")
    crossed = lax.ppermute(edge, AXES, pairs)

    source_total = wide_count * point_count
    matrix = pl.pallas_call(
        matrix_kernel,
        out_shape=b16(narrow_count, 3, point_count, source_total),
        grid=(narrow_count,),
        in_specs=[VMEM] * (wide_count + narrow_count),
        out_specs=pl.BlockSpec((1, 3, point_count, source_total), lambda k: (k, 0, 0, 0)),
        compiler_params=PARAMS,
    )(*packs, *arrived)
    half = f32(narrow_count // 2, 2, point_count, rhs_count)
    half_spec = pl.BlockSpec((1, 2, point_count, rhs_count), lambda k: (k // 2, 0, 0, 0))
    keep, send = pl.pallas_call(
        far_kernel,
        out_shape=[half, half],
        grid=(narrow_count,),
        in_specs=[pl.BlockSpec((1, 3, point_count, source_total), lambda k: (k, 0, 0, 0))]
        + [VMEM] * wide_count,
        out_specs=[half_spec, half_spec],
        scratch_shapes=[pltpu.VMEM((2, source_total, rhs_count), jnp.bfloat16)],
        compiler_params=PARAMS,
    )(matrix, *fields)
    offset = 1
    got = swap(send, "narrow", offset)
    while keep.shape[0] > 1:
        offset *= 2
        send = keep[1::2] + got[1::2]
        keep = keep[0::2] + got[0::2]
        got = swap(send, "narrow", offset)
    near_rows = jnp.transpose(near_block, (0, 2, 1, 3)).reshape(
        panels_dev, 2 * nodes, slot_total * 2 * nodes
    )
    base = call(
        near_kernel,
        f32(2, point_count, rhs_count),
        (index, near_panel, near_count, near_rows, crossed, *fields),
        3,
        [
            pltpu.VMEM((2, 2 * width + source_total, rhs_count), jnp.bfloat16),
            pltpu.VMEM((panels_dev, slot_total * 2 * nodes, rhs_count), jnp.bfloat16),
        ],
    )
    image, local_proj = call(
        project_kernel,
        [f32(2, point_count, rhs_count), f32(block_total, rhs_count, rhs_count)],
        (weight_row, basis, base, keep, got),
    )
    hessenberg = sum_everywhere(local_proj.reshape(block_total * rhs_count, rhs_count)).reshape(
        block_total, rhs_count, rhs_count
    )
    remainder, local_gram = call(
        remainder_kernel,
        [f32(2, point_count, rhs_count), f32(rhs_count, rhs_count)],
        (weight_row, basis, image, hessenberg),
    )
    gram_matrix = sum_everywhere(local_gram)
    upper_factor, new_block = factor_and_solve(
        gram_matrix, remainder.reshape(2 * point_count, rhs_count)
    )
    return (new_block.reshape(2, point_count, rhs_count), hessenberg, upper_factor)


def solution(mesh):
    in_specs = (
        P(None, ("narrow", "wide")),
        P(("narrow", "wide")),
        P(None, None, ("narrow", "wide"), None),
        P(None, ("narrow", "wide")),
        P(("narrow", "wide"), None),
        P(("narrow", "wide")),
        P(("narrow", "wide"), None, None, None),
        P(None, ("narrow", "wide")),
        P(None, "wide", "narrow"),
    )
    out_specs = (P(None, ("narrow", "wide"), None), P(), P())
    return jax.shard_map(body, mesh=mesh, in_specs=in_specs, out_specs=out_specs, check_vma=False)
```

```python
import functools

import jax
import jax.numpy as jnp
from jax import lax
from jax.experimental import pallas as pl
from jax.experimental.pallas import tpu as pltpu
from jax.sharding import PartitionSpec as P

SPAN = 4


NU = 0.3
DELTA2 = 1e-05
ELASTIC = 40.0
HIGH = lax.Precision.HIGHEST
AXES = ("narrow", "wide")
EXTRA = 8
ROWS = 8
SMEM = pl.BlockSpec(memory_space=pltpu.SMEM)
VMEM = pl.BlockSpec(memory_space=pltpu.VMEM)
ANY = pl.BlockSpec(memory_space=pl.ANY)
PARAMS = pltpu.CompilerParams(vmem_limit_bytes=48 * 1024 * 1024)


def dot_rows(left, right, precision=HIGH):
    return lax.dot_general(
        left, right, (((1,), (0,)), ((), ())), precision=precision, preferred_element_type=jnp.float32
    )


def dot_first(left, right):
    return lax.dot_general(
        left, right, (((0,), (0,)), ((), ())), precision=HIGH, preferred_element_type=jnp.float32
    )


def as_column(row, width):
    return jnp.transpose(jnp.broadcast_to(row, (width, row.shape[1])))


def swap(block, axis, offset):
    count = lax.axis_size(axis)
    return lax.ppermute(block, axis, [(i, i ^ offset) for i in range(count)])


def offsets_of(count):
    return [1 << bit for bit in range(count.bit_length() - 1)]


def join_kernel(left_ref, right_ref, out_ref):
    half = left_ref.shape[0]
    out_ref[:half] = left_ref[...]
    out_ref[half:] = right_ref[...]


def join(left, right):
    shape = (2 * left.shape[0],) + left.shape[1:]
    return call(join_kernel, jax.ShapeDtypeStruct(shape, left.dtype), (left, right))


def add_kernel(left_ref, right_ref, out_ref):
    out_ref[...] = left_ref[...] + right_ref[...]


def add(left, right):
    return call(add_kernel, f32(*left.shape), (left, right))


def halve_kernel(kept_ref, got_ref, keep_ref, send_ref):
    for k in range(keep_ref.shape[0]):
        keep_ref[k] = kept_ref[2 * k] + got_ref[2 * k]
        send_ref[k] = kept_ref[2 * k + 1] + got_ref[2 * k + 1]


def halve(keep, got):
    half = f32(keep.shape[0] // 2, *keep.shape[1:])
    return call(halve_kernel, [half, half], (keep, got))


def gather_steps(held, steps):
    got = None
    for axis, offset in steps:
        if got is not None:
            held = join(held, got)
        got = swap(held, axis, offset)
    return held, got


def gather_order(offsets):
    order = [0]
    for offset in offsets:
        order = order + [k ^ offset for k in order]
    return order


def sum_steps(keep, send, halving, butterfly):
    for number, (axis, offset) in enumerate(halving):
        if number:
            keep, send = halve(keep, got)
        got = swap(send, axis, offset)
    total = add(keep, got)
    for axis, offset in butterfly:
        total = add(total, swap(total, axis, offset))
    return gather_steps(total, halving[::-1])


def members(agg_ref, a, coarse_count):
    ids = lax.broadcasted_iota(jnp.int32, (coarse_count, agg_ref.shape[1]), 0)
    return jnp.where(ids == agg_ref[a : a + 1, :], 1.0, 0.0)


def load_all(pairs, sems):
    copies = [
        pltpu.make_async_copy(source, target, sems.at[k])
        for k, (source, target) in enumerate(pairs)
    ]
    for copy in copies:
        copy.start()
    for copy in copies:
        copy.wait()


def restrict_kernel(
    agg_hbm, basis_hbm, points_hbm, weight_hbm, pack_ref, agg_ref, newest_ref, points_ref, weight_ref, sems
):
    coarse_count = pack_ref.shape[1] - EXTRA
    point_count = newest_ref.shape[1]
    load_all(
        [
            (basis_hbm.at[basis_hbm.shape[0] - 1], newest_ref),
            (agg_hbm, agg_ref),
            (points_hbm, points_ref),
            (weight_hbm, weight_ref),
        ],
        sems,
    )
    total = dot_rows(members(agg_ref, 0, coarse_count), newest_ref[0]) + dot_rows(
        members(agg_ref, 1, coarse_count), newest_ref[1]
    )
    pack_ref[0, :coarse_count, :] = total
    pack_ref[0, coarse_count:, :] = jnp.concatenate(
        [points_ref[...], weight_ref[...], jnp.zeros((EXTRA - 3, point_count), jnp.float32)], axis=0
    )


def prefetch_kernel(
    pack_hbm,
    agg_hbm,
    basis_hbm,
    jacobi_hbm,
    weight_hbm,
    inverse_hbm,
    inverse_ref,
    member_ref,
    smooth_ref,
    weight_out_ref,
    agg_ref,
    newest_ref,
    jacobi_ref,
    weight_ref,
    sems,
):
    coarse_count = member_ref.shape[1]
    rhs_count = newest_ref.shape[2]
    load_all(
        [
            (basis_hbm.at[basis_hbm.shape[0] - 1], newest_ref),
            (agg_hbm, agg_ref),
            (jacobi_hbm, jacobi_ref),
            (weight_hbm, weight_ref),
            (inverse_hbm, inverse_ref),
        ],
        sems,
    )
    for a in range(2):
        member_ref[a] = members(agg_ref, a, coarse_count)
        smooth_ref[a] = as_column(jacobi_ref[a : a + 1, :], rhs_count) * newest_ref[a]
    weight_out_ref[...] = as_column(weight_ref[...], rhs_count)


def coarse_kernel(order, index_ref, inverse_ref, held_ref, got_ref, keep_ref, send_ref, rhs_ref):
    narrow_count = inverse_ref.shape[0]
    coarse_count = inverse_ref.shape[1]
    half = held_ref.shape[0]
    narrow_index = index_ref[0]
    wide_index = index_ref[1]
    for k, offset in enumerate(order):
        first = pl.multiple_of((wide_index ^ offset) * coarse_count, 8)
        part = held_ref[k] if k < half else got_ref[k - half]
        rhs_ref[pl.ds(first, coarse_count), :] = part[:coarse_count, :]
    own = held_ref[0, coarse_count:, :]
    for k in range(narrow_count):
        out_ref = send_ref if k % 2 else keep_ref
        out_ref[k // 2, :coarse_count, :] = dot_rows(
            inverse_ref[narrow_index ^ k], rhs_ref[...]
        )
        out_ref[k // 2, coarse_count:, :] = own


def coarse_halve_kernel(pairs, kept_ref, got_ref, keep_ref, send_ref):
    coarse_count = kept_ref.shape[1] - EXTRA
    rows = 2 * pairs
    own = kept_ref[0, coarse_count : coarse_count + rows, :]
    other = got_ref[0, coarse_count : coarse_count + rows, :]
    tail = [own, other]
    if 2 * rows < EXTRA:
        tail.append(jnp.zeros((EXTRA - 2 * rows, own.shape[1]), jnp.float32))
    tail = jnp.concatenate(tail, axis=0)
    for k in range(keep_ref.shape[0]):
        for out_ref, source in ((keep_ref, 2 * k), (send_ref, 2 * k + 1)):
            out_ref[k, :coarse_count, :] = (
                kept_ref[source, :coarse_count, :] + got_ref[source, :coarse_count, :]
            )
            out_ref[k, coarse_count:, :] = tail


def precond_kernel(index_ref, member_ref, smooth_ref, keep_ref, got_ref, precond_ref, edge_ref):
    coarse_count = member_ref.shape[1]
    point_count = smooth_ref.shape[1]
    width = edge_ref.shape[1]
    coarse_sol = keep_ref[0, :coarse_count, :] + got_ref[0, :coarse_count, :]
    for a in range(2):
        value = smooth_ref[a] + dot_first(member_ref[a], coarse_sol)
        precond_ref[0, a] = value.astype(jnp.bfloat16)
    first = pl.multiple_of(jnp.where(index_ref[1] == 0, 0, point_count - width), 16)
    for a in range(2):
        edge_ref[a] = precond_ref[0, a, pl.ds(first, width), :]


def matrix_kernel(coarse_count, held_ref, got_ref, own_ref, other_ref, matrix_ref):
    half, _, point_count = held_ref.shape
    target_half = pl.num_programs(0) // 2
    step = pl.program_id(0)
    first = coarse_count + 2 * lax.rem(step, target_half)
    target = jnp.where(
        step < target_half,
        own_ref[0, pl.ds(first, 2), :],
        other_ref[0, pl.ds(first, 2), :],
    )
    target_x = as_column(target[0:1, :], point_count)
    target_y = as_column(target[1:2, :], point_count)
    for s in range(2 * half):
        part = held_ref[s] if s < half else got_ref[s - half]
        source = part[coarse_count:, :]
        delta_x = target_x - source[0:1, :]
        delta_y = target_y - source[1:2, :]
        factor = ELASTIC * source[2:3, :]
        square_x = delta_x * delta_x
        square_y = delta_y * delta_y
        square_dist = square_x + square_y + DELTA2
        inverse = 1.0 / square_dist
        log_part = (-0.5 * (3.0 - 4.0 * NU)) * jnp.log(square_dist)
        lanes = slice(s * point_count, (s + 1) * point_count)
        matrix_ref[0, 0, :, lanes] = (factor * (log_part + square_x * inverse)).astype(jnp.bfloat16)
        matrix_ref[0, 1, :, lanes] = (factor * (delta_x * delta_y * inverse)).astype(jnp.bfloat16)
        matrix_ref[0, 2, :, lanes] = (factor * (log_part + square_y * inverse)).astype(jnp.bfloat16)


def far_kernel(matrix_ref, held_ref, got_ref, keep_ref, send_ref, fields_ref):
    half, _, point_count, _ = held_ref.shape
    step = pl.program_id(0)

    @pl.when(step == 0)
    def _():
        for s in range(half):
            for b in range(2):
                fields_ref[b, s * point_count : (s + 1) * point_count, :] = held_ref[s, b]
                first = (half + s) * point_count
                fields_ref[b, first : first + point_count, :] = got_ref[s, b]

    out_x = dot_rows(matrix_ref[0, 0], fields_ref[0], None) + dot_rows(
        matrix_ref[0, 1], fields_ref[1], None
    )
    out_y = dot_rows(matrix_ref[0, 1], fields_ref[0], None) + dot_rows(
        matrix_ref[0, 2], fields_ref[1], None
    )

    @pl.when(step % 2 == 0)
    def _():
        keep_ref[0, 0] = out_x
        keep_ref[0, 1] = out_y

    @pl.when(step % 2 == 1)
    def _():
        send_ref[0, 0] = out_x
        send_ref[0, 1] = out_y


def near_kernel(
    order,
    index_ref,
    panel_ref,
    count_ref,
    block_ref,
    crossed_ref,
    held_ref,
    got_ref,
    out_ref,
    line_ref,
    gathered_ref,
):
    half, _, point_count, _ = held_ref.shape
    width = crossed_ref.shape[1]
    panels_dev, double_nodes, _ = block_ref.shape
    nodes = double_nodes // 2
    slot_total = panel_ref.shape[1]
    wide_index = index_ref[1]
    for b in range(2):
        line_ref[b, :width, :] = crossed_ref[b]
        line_ref[b, width + len(order) * point_count :, :] = crossed_ref[b]
        for k, offset in enumerate(order):
            first = pl.multiple_of((wide_index ^ offset) * point_count + width, 16)
            line_ref[b, pl.ds(first, point_count), :] = (
                held_ref[k, b] if k < half else got_ref[k - half, b]
            )
    group_start = index_ref[0] * (len(order) * panels_dev)
    lane = lax.broadcasted_iota(jnp.int32, block_ref.shape[1:], 1)
    for p in range(panels_dev):
        for k in range(slot_total):
            first = pl.multiple_of((panel_ref[p, k] - group_start) * nodes + width, 16)
            for b in range(2):
                row = (k * 2 + b) * nodes
                gathered_ref[p, row : row + nodes, :] = line_ref[b, pl.ds(first, nodes), :]
        blocks = jnp.where(
            lane < count_ref[p] * double_nodes, block_ref[p].astype(jnp.float32), 0.0
        ).astype(jnp.bfloat16)
        near = dot_rows(blocks, gathered_ref[p], None)
        for a in range(2):
            rows = slice(p * nodes, (p + 1) * nodes)
            own = held_ref[0, a, rows, :].astype(jnp.float32)
            out_ref[a, rows, :] = 0.5 * own + near[a * nodes : (a + 1) * nodes, :]


def spread(full_ref, keep_ref, send_ref, own):
    rows = keep_ref.shape[1]
    for k in range(2 * keep_ref.shape[0]):
        first = pl.multiple_of((own ^ k) * rows, 8)
        out_ref = send_ref if k % 2 else keep_ref
        out_ref[k // 2] = full_ref[pl.ds(first, rows), :]


def collect(order, held_ref, got_ref, full_ref, own):
    half, rows, _ = held_ref.shape
    for k, offset in enumerate(order):
        first = pl.multiple_of((own ^ offset) * rows, 8)
        full_ref[pl.ds(first, rows), :] = held_ref[k] if k < half else got_ref[k - half]


def own_part(index_ref, narrow_count, part_count):
    if part_count <= narrow_count:
        return index_ref[0] & (part_count - 1)
    return index_ref[0] + narrow_count * (index_ref[1] & (part_count // narrow_count - 1))


def project_kernel(
    narrow_count,
    index_ref,
    weight_ref,
    basis_ref,
    base_ref,
    kept_ref,
    arrived_ref,
    image_ref,
    keep_ref,
    send_ref,
    full_ref,
):
    block_total, _, _, rhs_count = basis_ref.shape
    weighted = []
    for a in range(2):
        image = base_ref[a] + kept_ref[0, a] + arrived_ref[0, a]
        image_ref[a] = image
        weighted.append(image * weight_ref[...])
    for j in range(block_total):
        full_ref[j * rhs_count : (j + 1) * rhs_count, :] = dot_first(
            basis_ref[j, 0], weighted[0]
        ) + dot_first(basis_ref[j, 1], weighted[1])
    spread(
        full_ref, keep_ref, send_ref, own_part(index_ref, narrow_count, 2 * keep_ref.shape[0])
    )


def remainder_kernel(
    order,
    narrow_count,
    index_ref,
    weight_ref,
    basis_ref,
    image_ref,
    held_ref,
    got_ref,
    hess_ref,
    remainder_ref,
    keep_ref,
    send_ref,
    gram_ref,
):
    block_total, _, point_count, rhs_count = basis_ref.shape
    collect(order, held_ref, got_ref, hess_ref, own_part(index_ref, narrow_count, len(order)))
    gram = None
    for a in range(2):
        value = image_ref[a]
        for j in range(block_total):
            value = value - dot_rows(
                basis_ref[j, a], hess_ref[j * rhs_count : (j + 1) * rhs_count, :]
            )
        remainder_ref[a * point_count : (a + 1) * point_count, :] = value
        term = dot_first(value * weight_ref[...], value)
        gram = term if gram is None else gram + term
    gram_ref[...] = gram
    spread(
        gram_ref, keep_ref, send_ref, own_part(index_ref, narrow_count, 2 * keep_ref.shape[0])
    )


def factor_kernel(
    gather,
    narrow_count,
    index_ref,
    held_ref,
    got_ref,
    remainder_ref,
    upper_ref,
    new_ref,
    work_ref,
    inverse_ref,
):
    order = remainder_ref.shape[1]
    tile = (ROWS, order)
    lane = lax.broadcasted_iota(jnp.int32, tile, 1)
    row = lax.broadcasted_iota(jnp.int32, tile, 0)
    collect(gather, held_ref, got_ref, work_ref, own_part(index_ref, narrow_count, len(gather)))
    for block in range(order // ROWS):
        start = block * ROWS
        inverse_ref[start : start + ROWS, :] = jnp.where(lane == row + start, 1.0, 0.0)
    for block in range(order // ROWS):
        start = block * ROWS
        own = work_ref[start : start + ROWS, :]
        own_inverse = inverse_ref[start : start + ROWS, :]
        columns = [
            jnp.broadcast_to(own[:, start + m : start + m + 1], tile) for m in range(ROWS)
        ]
        entry = {
            (j, m): jnp.broadcast_to(columns[m][j : j + 1, :], tile)
            for m in range(ROWS)
            for j in range(m, ROWS)
        }
        scale = []
        for m in range(ROWS):
            scale.append(lax.rsqrt(entry[m, m]))
            for j in range(m + 1, ROWS):
                entry[j, m] = entry[j, m] * scale[m]
            for n in range(m + 1, ROWS):
                for j in range(n, ROWS):
                    entry[j, n] = entry[j, n] - entry[j, m] * entry[n, m]
        solved = []
        solved_inverse = []
        for m in range(ROWS):
            upper_row = jnp.broadcast_to(own[m : m + 1, :], tile)
            inverse_row = jnp.broadcast_to(own_inverse[m : m + 1, :], tile)
            for j in range(m):
                upper_row = upper_row - entry[m, j] * solved[j]
                inverse_row = inverse_row - entry[m, j] * solved_inverse[j]
            upper_row = upper_row * scale[m]
            inverse_row = inverse_row * scale[m]
            solved.append(upper_row)
            solved_inverse.append(inverse_row)
        upper_rows = solved[ROWS - 1]
        inverse_rows = solved_inverse[ROWS - 1]
        for m in range(ROWS - 1):
            upper_rows = jnp.where(row == m, solved[m], upper_rows)
            inverse_rows = jnp.where(row == m, solved_inverse[m], inverse_rows)
        upper_ref[start : start + ROWS, :] = jnp.where(lane >= row + start, upper_rows, 0.0)
        inverse_ref[start : start + ROWS, :] = inverse_rows
        for later in range(block + 1, order // ROWS):
            first = later * ROWS
            target = work_ref[first : first + ROWS, :]
            target_inverse = inverse_ref[first : first + ROWS, :]
            multiplier = []
            for m in range(ROWS):
                value = jnp.broadcast_to(target[:, start + m : start + m + 1], tile)
                for j in range(m):
                    value = value - multiplier[j] * entry[m, j]
                multiplier.append(value * scale[m])
            for m in range(ROWS):
                target = target - multiplier[m] * solved[m]
                target_inverse = target_inverse - multiplier[m] * solved_inverse[m]
            work_ref[first : first + ROWS, :] = target
            inverse_ref[first : first + ROWS, :] = target_inverse
    new_ref[...] = lax.dot_general(
        remainder_ref[...],
        inverse_ref[...],
        (((1,), (1,)), ((), ())),
        precision=HIGH,
        preferred_element_type=jnp.float32,
    )


def f32(*shape):
    return jax.ShapeDtypeStruct(shape, jnp.float32)


def b16(*shape):
    return jax.ShapeDtypeStruct(shape, jnp.bfloat16)


def call(kernel, out_shape, operands, scalars=0, scratch=(), anywhere=False):
    many = isinstance(out_shape, (tuple, list))
    return pl.pallas_call(
        kernel,
        out_shape=out_shape,
        in_specs=[SMEM] * scalars + [ANY if anywhere else VMEM] * (len(operands) - scalars),
        out_specs=[VMEM] * len(out_shape) if many else VMEM,
        scratch_shapes=list(scratch),
        compiler_params=PARAMS,
    )(*operands)


def body(
    points,
    quad_weight,
    basis,
    jacobi,
    near_panel,
    near_count,
    near_block,
    agg_index,
    coarse_inverse,
):
    block_total, _, point_count, rhs_count = basis.shape
    coarse_count = coarse_inverse.shape[1]
    narrow_count = lax.axis_size("narrow")
    wide_count = lax.axis_size("wide")
    panels_dev, slot_total = near_panel.shape
    nodes = near_block.shape[2] // 2
    width = SPAN * nodes
    pack_rows = coarse_count + EXTRA
    source_total = wide_count * point_count
    index = jnp.stack([lax.axis_index("narrow"), lax.axis_index("wide")]).astype(jnp.int32)
    weight_row = quad_weight[None, :]
    narrow_steps = [("narrow", offset) for offset in offsets_of(narrow_count)]
    wide_steps = [("wide", offset) for offset in offsets_of(wide_count)]
    wide_order = gather_order([offset for _, offset in wide_steps[::-1]])
    pair_row = pltpu.VMEM((2, point_count), jnp.float32)
    one_row = pltpu.VMEM((1, point_count), jnp.float32)
    pair_index = pltpu.VMEM((2, point_count), jnp.int32)
    field = pltpu.VMEM((2, point_count, rhs_count), jnp.float32)

    pack = call(
        restrict_kernel,
        f32(1, pack_rows, point_count),
        (agg_index, basis, points, weight_row),
        0,
        [pair_index, field, pair_row, one_row, pltpu.SemaphoreType.DMA((4,))],
        True,
    )
    inverse, member, smooth, weight = call(
        prefetch_kernel,
        [
            f32(*coarse_inverse.shape),
            f32(2, coarse_count, point_count),
            f32(2, point_count, rhs_count),
            f32(point_count, rhs_count),
        ],
        (pack, agg_index, basis, jacobi, weight_row, coarse_inverse),
        0,
        [pair_index, field, pair_row, one_row, pltpu.SemaphoreType.DMA((5,))],
        True,
    )
    packs = gather_steps(pack, wide_steps[::-1])
    half = f32(narrow_count // 2, pack_rows, rhs_count)
    keep, send = call(
        functools.partial(coarse_kernel, wide_order),
        [half, half],
        (index, inverse, *packs),
        1,
        [pltpu.VMEM((wide_count * coarse_count, rhs_count), jnp.float32)],
    )
    got = swap(send, *narrow_steps[0])
    for number, (axis, offset) in enumerate(narrow_steps[1:]):
        half = f32(keep.shape[0] // 2, pack_rows, rhs_count)
        keep, send = call(
            functools.partial(coarse_halve_kernel, 1 << number), [half, half], (keep, got)
        )
        got = swap(send, axis, offset)
    precond, edge = call(
        precond_kernel,
        [b16(1, 2, point_count, rhs_count), b16(2, width, rhs_count)],
        (index, member, smooth, keep, got),
        1,
    )
    pairs = []
    for group in range(narrow_count - 1):
        left = group * wide_count + wide_count - 1
        pairs += [(left, left + 1), (left + 1, left)]
    fields = gather_steps(precond, wide_steps[::-1])
    crossed = lax.ppermute(edge, AXES, pairs)

    matrix_spec = pl.BlockSpec((1, 3, point_count, source_total), lambda k: (k, 0, 0, 0))
    matrix = pl.pallas_call(
        functools.partial(matrix_kernel, coarse_count),
        out_shape=b16(narrow_count, 3, point_count, source_total),
        grid=(narrow_count,),
        in_specs=[VMEM] * 4,
        out_specs=matrix_spec,
        compiler_params=PARAMS,
    )(*packs, keep, got)
    half = f32(narrow_count // 2, 2, point_count, rhs_count)
    half_spec = pl.BlockSpec((1, 2, point_count, rhs_count), lambda k: (k // 2, 0, 0, 0))
    keep, send = pl.pallas_call(
        far_kernel,
        out_shape=[half, half],
        grid=(narrow_count,),
        in_specs=[matrix_spec, VMEM, VMEM],
        out_specs=[half_spec, half_spec],
        scratch_shapes=[pltpu.VMEM((2, source_total, rhs_count), jnp.bfloat16)],
        compiler_params=PARAMS,
    )(matrix, *fields)
    got = swap(send, *narrow_steps[0])
    for axis, offset in narrow_steps[1:]:
        keep, send = halve(keep, got)
        got = swap(send, axis, offset)
    near_rows = jnp.transpose(near_block, (0, 2, 1, 3)).reshape(
        panels_dev, 2 * nodes, slot_total * 2 * nodes
    )
    base = call(
        functools.partial(near_kernel, wide_order),
        f32(2, point_count, rhs_count),
        (index, near_panel, near_count, near_rows, crossed, *fields),
        3,
        [
            pltpu.VMEM((2, 2 * width + source_total, rhs_count), jnp.bfloat16),
            pltpu.VMEM((panels_dev, slot_total * 2 * nodes, rhs_count), jnp.bfloat16),
        ],
    )

    hess_rows = block_total * rhs_count
    halving = narrow_steps + wide_steps[:1]
    butterfly = wide_steps[1:]
    hess_order = gather_order([1 << bit for bit in range(len(halving))][::-1])
    half = f32(len(hess_order) // 2, hess_rows // len(hess_order), rhs_count)
    image, keep, send = call(
        functools.partial(project_kernel, narrow_count),
        [f32(2, point_count, rhs_count), half, half],
        (index, weight, basis, base, keep, got),
        1,
        [pltpu.VMEM((hess_rows, rhs_count), jnp.float32)],
    )
    total = sum_steps(keep, send, halving, butterfly)
    gram_order = gather_order([1])
    half = f32(1, rhs_count // 2, rhs_count)
    hessenberg, remainder, keep, send = call(
        functools.partial(remainder_kernel, hess_order, narrow_count),
        [f32(hess_rows, rhs_count), f32(2 * point_count, rhs_count), half, half],
        (index, weight, basis, image, *total),
        1,
        [pltpu.VMEM((rhs_count, rhs_count), jnp.float32)],
    )
    total = sum_steps(keep, send, narrow_steps[:1], narrow_steps[1:] + wide_steps)
    upper_factor, new_block = call(
        functools.partial(factor_kernel, gram_order, narrow_count),
        [f32(rhs_count, rhs_count), f32(2 * point_count, rhs_count)],
        (index, *total, remainder),
        1,
        [pltpu.VMEM((rhs_count, rhs_count), jnp.float32)] * 2,
    )
    return (
        new_block.reshape(2, point_count, rhs_count),
        hessenberg.reshape(block_total, rhs_count, rhs_count),
        upper_factor,
    )


def solution(mesh):
    in_specs = (
        P(None, ("narrow", "wide")),
        P(("narrow", "wide")),
        P(None, None, ("narrow", "wide"), None),
        P(None, ("narrow", "wide")),
        P(("narrow", "wide"), None),
        P(("narrow", "wide")),
        P(("narrow", "wide"), None, None, None),
        P(None, ("narrow", "wide")),
        P(None, "wide", "narrow"),
    )
    out_specs = (P(None, ("narrow", "wide"), None), P(), P())
    return jax.shard_map(body, mesh=mesh, in_specs=in_specs, out_specs=out_specs, check_vma=False)
```

```python
import functools

import jax
import jax.numpy as jnp
from jax import lax
from jax.experimental import pallas as pl
from jax.experimental.pallas import tpu as pltpu
from jax.sharding import PartitionSpec as P

SPAN = 4


NU = 0.3
DELTA2 = 1e-05
ELASTIC = 40.0
HIGH = lax.Precision.HIGHEST
AXES = ("narrow", "wide")
EXTRA = 8
ROWS = 8
SMEM = pl.BlockSpec(memory_space=pltpu.SMEM)
VMEM = pl.BlockSpec(memory_space=pltpu.VMEM)
HBM = pl.BlockSpec(memory_space=pltpu.HBM)
PARAMS = pltpu.CompilerParams(vmem_limit_bytes=48 * 1024 * 1024)


def dot_rows(left, right, precision=HIGH):
    return lax.dot_general(
        left, right, (((1,), (0,)), ((), ())), precision=precision, preferred_element_type=jnp.float32
    )


def dot_first(left, right):
    return lax.dot_general(
        left, right, (((0,), (0,)), ((), ())), precision=HIGH, preferred_element_type=jnp.float32
    )


def as_column(row, width):
    return jnp.transpose(jnp.broadcast_to(row, (width, row.shape[1])))


def flip(block, mask):
    count = lax.axis_size(AXES)
    return lax.ppermute(block, AXES, [(i, i ^ mask) for i in range(count)])


def masks_of(count, scale=1):
    return [scale << bit for bit in range(count.bit_length() - 1)]


def in_pairs(masks):
    return [masks[k : k + 2] for k in range(0, len(masks), 2)]


def combined(group, number):
    mask = 0
    for bit, part in enumerate(group):
        if number >> bit & 1:
            mask ^= part
    return mask


def flip_each(parts, group):
    return [parts[0]] + [flip(parts[j], combined(group, j)) for j in range(1, 1 << len(group))]


def join_kernel(*refs):
    out_ref = refs[-1]
    size = refs[0].shape[0]
    for j, ref in enumerate(refs[:-1]):
        out_ref[j * size : (j + 1) * size] = ref[...]


def join(parts):
    shape = (len(parts) * parts[0].shape[0],) + parts[0].shape[1:]
    return call(join_kernel, jax.ShapeDtypeStruct(shape, parts[0].dtype), parts)


def gather_steps(held, groups):
    parts = [held]
    for group in groups:
        held = parts[0] if len(parts) == 1 else join(parts)
        parts = flip_each([held] * (1 << len(group)), group)
    return parts


def gather_order(groups):
    order = [0]
    for group in groups:
        order = [k ^ combined(group, j) for j in range(1 << len(group)) for k in order]
    return order


def total_of(values):
    while len(values) > 1:
        values = [values[k] + values[k + 1] for k in range(0, len(values), 2)]
    return values[0]


def sum_kernel(count, *refs):
    parts, outs = refs[:count], refs[count:]
    for k in range(outs[0].shape[0]):
        for j, out_ref in enumerate(outs):
            out_ref[k] = total_of([part[k * len(outs) + j] for part in parts])


def sum_parts(parts, ways):
    out = f32(parts[0].shape[0] // ways, *parts[0].shape[1:])
    return call(functools.partial(sum_kernel, len(parts)), [out] * ways, parts)


def scatter_steps(parts, groups):
    for number, group in enumerate(groups):
        if number:
            parts = sum_parts(parts, 1 << len(group))
        parts = flip_each(parts, group)
    return parts


def sum_steps(parts, halving, butterfly):
    (total,) = sum_parts(scatter_steps(parts, halving), 1)
    for group in butterfly:
        (total,) = sum_parts(flip_each([total] * (1 << len(group)), group), 1)
    return gather_steps(total, halving[::-1])


def part_groups(groups):
    bit, found = 0, []
    for group in groups:
        found.append([1 << (bit + k) for k in range(len(group))])
        bit += len(group)
    return found


def bits_of(index, masks):
    packed = 0
    for bit, mask in enumerate(masks):
        packed = packed + (lax.shift_right_logical(index, mask.bit_length() - 1) & 1) * (1 << bit)
    return packed


def members(agg_ref, a, coarse_count):
    ids = lax.broadcasted_iota(jnp.int32, (coarse_count, agg_ref.shape[1]), 0)
    return jnp.where(ids == agg_ref[a : a + 1, :], 1.0, 0.0)


def load_all(pairs, sems):
    copies = [
        pltpu.make_async_copy(source, target, sems.at[k])
        for k, (source, target) in enumerate(pairs)
    ]
    for copy in copies:
        copy.start()
    for copy in copies:
        copy.wait()


def restrict_kernel(
    agg_hbm, basis_hbm, points_hbm, weight_hbm, pack_ref, agg_ref, newest_ref, points_ref, weight_ref, sems
):
    coarse_count = pack_ref.shape[1] - EXTRA
    point_count = newest_ref.shape[1]
    load_all(
        [
            (basis_hbm.at[basis_hbm.shape[0] - 1], newest_ref),
            (agg_hbm, agg_ref),
            (points_hbm, points_ref),
            (weight_hbm, weight_ref),
        ],
        sems,
    )
    total = dot_rows(members(agg_ref, 0, coarse_count), newest_ref[0]) + dot_rows(
        members(agg_ref, 1, coarse_count), newest_ref[1]
    )
    pack_ref[0, :coarse_count, :] = total
    pack_ref[0, coarse_count:, :] = jnp.concatenate(
        [points_ref[...], weight_ref[...], jnp.zeros((EXTRA - 3, point_count), jnp.float32)], axis=0
    )


def prefetch_kernel(
    pack_hbm,
    agg_hbm,
    basis_hbm,
    jacobi_hbm,
    weight_hbm,
    inverse_hbm,
    inverse_ref,
    member_ref,
    smooth_ref,
    weight_out_ref,
    agg_ref,
    newest_ref,
    jacobi_ref,
    weight_ref,
    sems,
):
    coarse_count = member_ref.shape[1]
    rhs_count = newest_ref.shape[2]
    load_all(
        [
            (basis_hbm.at[basis_hbm.shape[0] - 1], newest_ref),
            (agg_hbm, agg_ref),
            (jacobi_hbm, jacobi_ref),
            (weight_hbm, weight_ref),
            (inverse_hbm, inverse_ref),
        ],
        sems,
    )
    for a in range(2):
        member_ref[a] = members(agg_ref, a, coarse_count)
        smooth_ref[a] = as_column(jacobi_ref[a : a + 1, :], rhs_count) * newest_ref[a]
    weight_out_ref[...] = as_column(weight_ref[...], rhs_count)


def part_at(parts, k):
    size = parts[0].shape[0]
    return parts[k // size], k % size


def coarse_kernel(order, ways, z_count, index_ref, inverse_ref, *refs):
    narrow_count, coarse_count, _ = inverse_ref.shape
    packs = refs[: len(refs) - ways - 3]
    outs = refs[len(packs) : len(packs) + ways]
    source_ref, target_ref, rhs_ref = refs[len(packs) + ways :]
    for k, offset in enumerate(order):
        first = pl.multiple_of((index_ref[1] ^ offset) * coarse_count, 8)
        ref, row = part_at(packs, k)
        rhs_ref[pl.ds(first, coarse_count), :] = ref[row, :coarse_count, :]
    for k in range(z_count):
        ref, row = part_at(packs, k)
        source_ref[k] = ref[row, coarse_count:, :]
    for k in range(target_ref.shape[0]):
        ref, row = part_at(packs, k * z_count)
        target_ref[k] = ref[row, coarse_count:, :]
    for k in range(narrow_count):
        outs[k % ways][k // ways] = dot_rows(inverse_ref[index_ref[0] ^ k], rhs_ref[...])


def precond_kernel(member_ref, smooth_ref, *refs):
    parts = refs[:-3]
    precond_ref, first_ref, last_ref = refs[-3:]
    point_count = smooth_ref.shape[1]
    width = first_ref.shape[1]
    coarse_sol = total_of([part[0] for part in parts])
    for a in range(2):
        value = (smooth_ref[a] + dot_first(member_ref[a], coarse_sol)).astype(jnp.bfloat16)
        precond_ref[0, a] = value
        first_ref[a] = value[:width]
        last_ref[a] = value[point_count - width :]


def matrix_kernel(source_parts, *refs):
    matrix_ref = refs[-1]
    sources = refs[:source_parts]
    targets = refs[source_parts:-1]
    point_count = sources[0].shape[2]
    size = targets[0].shape[0]
    step = pl.program_id(0)
    target = targets[0][lax.rem(step, size)]
    for j in range(1, len(targets)):
        target = jnp.where(step // size == j, targets[j][lax.rem(step, size)], target)
    target_x = as_column(target[0:1, :], point_count)
    target_y = as_column(target[1:2, :], point_count)
    for s in range(matrix_ref.shape[3] // point_count):
        ref, row = part_at(sources, s)
        source = ref[row]
        delta_x = target_x - source[0:1, :]
        delta_y = target_y - source[1:2, :]
        factor = ELASTIC * source[2:3, :]
        square_x = delta_x * delta_x
        square_y = delta_y * delta_y
        square_dist = square_x + square_y + DELTA2
        inverse = 1.0 / square_dist
        log_part = (-0.5 * (3.0 - 4.0 * NU)) * jnp.log(square_dist)
        lanes = slice(s * point_count, (s + 1) * point_count)
        matrix_ref[0, 0, :, lanes] = (factor * (log_part + square_x * inverse)).astype(jnp.bfloat16)
        matrix_ref[0, 1, :, lanes] = (factor * (delta_x * delta_y * inverse)).astype(jnp.bfloat16)
        matrix_ref[0, 2, :, lanes] = (factor * (log_part + square_y * inverse)).astype(jnp.bfloat16)


def far_kernel(ways, matrix_ref, *refs):
    fields = refs[: len(refs) - ways - 1]
    outs = refs[len(fields) : len(fields) + ways]
    fields_ref = refs[-1]
    point_count = fields[0].shape[2]
    step = pl.program_id(0)

    @pl.when(step == 0)
    def _():
        for s in range(fields_ref.shape[1] // point_count):
            ref, row = part_at(fields, s)
            for b in range(2):
                fields_ref[b, s * point_count : (s + 1) * point_count, :] = ref[row, b]

    out_x = dot_rows(matrix_ref[0, 0], fields_ref[0], None) + dot_rows(
        matrix_ref[0, 1], fields_ref[1], None
    )
    out_y = dot_rows(matrix_ref[0, 1], fields_ref[0], None) + dot_rows(
        matrix_ref[0, 2], fields_ref[1], None
    )
    for j, out_ref in enumerate(outs):

        @pl.when(lax.rem(step, ways) == j)
        def _(out_ref=out_ref):
            out_ref[step // ways, 0] = out_x
            out_ref[step // ways, 1] = out_y


def near_kernel(
    index_ref,
    panel_ref,
    count_ref,
    block_ref,
    low_ref,
    own_ref,
    high_ref,
    out_ref,
    line_ref,
    gathered_ref,
):
    point_count = own_ref.shape[2]
    width = low_ref.shape[1]
    panels_dev, double_nodes, _ = block_ref.shape
    nodes = double_nodes // 2
    slot_total = panel_ref.shape[1]
    for b in range(2):
        line_ref[b, :width, :] = low_ref[b]
        line_ref[b, width : width + point_count, :] = own_ref[0, b]
        line_ref[b, width + point_count :, :] = high_ref[b]
    first_panel = index_ref[2] * panels_dev
    lane = lax.broadcasted_iota(jnp.int32, block_ref.shape[1:], 1)
    for p in range(panels_dev):
        for k in range(slot_total):
            first = pl.multiple_of((panel_ref[p, k] - first_panel) * nodes + width, 16)
            for b in range(2):
                row = (k * 2 + b) * nodes
                gathered_ref[p, row : row + nodes, :] = line_ref[b, pl.ds(first, nodes), :]
        blocks = jnp.where(
            lane < count_ref[p] * double_nodes, block_ref[p].astype(jnp.float32), 0.0
        ).astype(jnp.bfloat16)
        near = dot_rows(blocks, gathered_ref[p], None)
        for a in range(2):
            rows = slice(p * nodes, (p + 1) * nodes)
            own = own_ref[0, a, rows, :].astype(jnp.float32)
            out_ref[a, rows, :] = 0.5 * own + near[a * nodes : (a + 1) * nodes, :]


def spread(full_ref, outs, own):
    rows = outs[0].shape[1]
    for k in range(len(outs) * outs[0].shape[0]):
        first = pl.multiple_of((own ^ k) * rows, 8)
        outs[k % len(outs)][k // len(outs)] = full_ref[pl.ds(first, rows), :]


def collect(order, parts, full_ref, own):
    rows = parts[0].shape[1]
    for k, offset in enumerate(order):
        first = pl.multiple_of((own ^ offset) * rows, 8)
        ref, row = part_at(parts, k)
        full_ref[pl.ds(first, rows), :] = ref[row]


def project_kernel(masks, ways, index_ref, weight_ref, basis_ref, base_ref, *refs):
    arrived = refs[: len(refs) - ways - 2]
    image_ref = refs[len(arrived)]
    outs = refs[len(arrived) + 1 : -1]
    full_ref = refs[-1]
    block_total, _, _, rhs_count = basis_ref.shape
    weighted = []
    for a in range(2):
        image = base_ref[a] + total_of([part[0, a] for part in arrived])
        image_ref[a] = image
        weighted.append(image * weight_ref[...])
    for j in range(block_total):
        full_ref[j * rhs_count : (j + 1) * rhs_count, :] = dot_first(
            basis_ref[j, 0], weighted[0]
        ) + dot_first(basis_ref[j, 1], weighted[1])
    spread(full_ref, outs, bits_of(index_ref[2], masks))


def remainder_kernel(
    order, masks, gram_masks, ways, index_ref, weight_ref, basis_ref, image_ref, *refs
):
    parts = refs[: len(refs) - ways - 3]
    hess_ref, remainder_ref = refs[len(parts) : len(parts) + 2]
    outs = refs[len(parts) + 2 : -1]
    gram_ref = refs[-1]
    block_total, _, point_count, rhs_count = basis_ref.shape
    collect(order, parts, hess_ref, bits_of(index_ref[2], masks))
    gram = None
    for a in range(2):
        value = image_ref[a]
        for j in range(block_total):
            value = value - dot_rows(
                basis_ref[j, a], hess_ref[j * rhs_count : (j + 1) * rhs_count, :]
            )
        remainder_ref[a * point_count : (a + 1) * point_count, :] = value
        term = dot_first(value * weight_ref[...], value)
        gram = term if gram is None else gram + term
    gram_ref[...] = gram
    spread(gram_ref, outs, bits_of(index_ref[2], gram_masks))


def factor_kernel(gather, masks, index_ref, remainder_ref, *refs):
    parts = refs[:-4]
    upper_ref, new_ref, work_ref, inverse_ref = refs[-4:]
    order = remainder_ref.shape[1]
    tile = (ROWS, order)
    lane = lax.broadcasted_iota(jnp.int32, tile, 1)
    row = lax.broadcasted_iota(jnp.int32, tile, 0)
    collect(gather, parts, work_ref, bits_of(index_ref[2], masks))
    for block in range(order // ROWS):
        start = block * ROWS
        inverse_ref[start : start + ROWS, :] = jnp.where(lane == row + start, 1.0, 0.0)
    for block in range(order // ROWS):
        start = block * ROWS
        own = work_ref[start : start + ROWS, :]
        own_inverse = inverse_ref[start : start + ROWS, :]
        columns = [
            jnp.broadcast_to(own[:, start + m : start + m + 1], tile) for m in range(ROWS)
        ]
        entry = {
            (j, m): jnp.broadcast_to(columns[m][j : j + 1, :], tile)
            for m in range(ROWS)
            for j in range(m, ROWS)
        }
        scale = []
        for m in range(ROWS):
            scale.append(lax.rsqrt(entry[m, m]))
            for j in range(m + 1, ROWS):
                entry[j, m] = entry[j, m] * scale[m]
            for n in range(m + 1, ROWS):
                for j in range(n, ROWS):
                    entry[j, n] = entry[j, n] - entry[j, m] * entry[n, m]
        solved = []
        solved_inverse = []
        for m in range(ROWS):
            upper_row = jnp.broadcast_to(own[m : m + 1, :], tile)
            inverse_row = jnp.broadcast_to(own_inverse[m : m + 1, :], tile)
            for j in range(m):
                upper_row = upper_row - entry[m, j] * solved[j]
                inverse_row = inverse_row - entry[m, j] * solved_inverse[j]
            upper_row = upper_row * scale[m]
            inverse_row = inverse_row * scale[m]
            solved.append(upper_row)
            solved_inverse.append(inverse_row)
        upper_rows = solved[ROWS - 1]
        inverse_rows = solved_inverse[ROWS - 1]
        for m in range(ROWS - 1):
            upper_rows = jnp.where(row == m, solved[m], upper_rows)
            inverse_rows = jnp.where(row == m, solved_inverse[m], inverse_rows)
        upper_ref[start : start + ROWS, :] = jnp.where(lane >= row + start, upper_rows, 0.0)
        inverse_ref[start : start + ROWS, :] = inverse_rows
        for later in range(block + 1, order // ROWS):
            first = later * ROWS
            target = work_ref[first : first + ROWS, :]
            target_inverse = inverse_ref[first : first + ROWS, :]
            multiplier = []
            for m in range(ROWS):
                value = jnp.broadcast_to(target[:, start + m : start + m + 1], tile)
                for j in range(m):
                    value = value - multiplier[j] * entry[m, j]
                multiplier.append(value * scale[m])
            for m in range(ROWS):
                target = target - multiplier[m] * solved[m]
                target_inverse = target_inverse - multiplier[m] * solved_inverse[m]
            work_ref[first : first + ROWS, :] = target
            inverse_ref[first : first + ROWS, :] = target_inverse
    new_ref[...] = lax.dot_general(
        remainder_ref[...],
        inverse_ref[...],
        (((1,), (1,)), ((), ())),
        precision=HIGH,
        preferred_element_type=jnp.float32,
    )


def f32(*shape):
    return jax.ShapeDtypeStruct(shape, jnp.float32)


def b16(*shape):
    return jax.ShapeDtypeStruct(shape, jnp.bfloat16)


def call(kernel, out_shape, operands, scalars=0, scratch=(), in_hbm=False):
    many = isinstance(out_shape, (tuple, list))
    return pl.pallas_call(
        kernel,
        out_shape=out_shape,
        in_specs=[SMEM] * scalars + [HBM if in_hbm else VMEM] * (len(operands) - scalars),
        out_specs=[VMEM] * len(out_shape) if many else VMEM,
        scratch_shapes=list(scratch),
        compiler_params=PARAMS,
    )(*operands)


def body(
    points,
    quad_weight,
    basis,
    jacobi,
    near_panel,
    near_count,
    near_block,
    agg_index,
    coarse_inverse,
):
    block_total, _, point_count, rhs_count = basis.shape
    coarse_count = coarse_inverse.shape[1]
    narrow_count = lax.axis_size("narrow")
    wide_count = lax.axis_size("wide")
    panels_dev, slot_total = near_panel.shape
    nodes = near_block.shape[2] // 2
    width = SPAN * nodes
    pack_rows = coarse_count + EXTRA
    index = jnp.stack(
        [lax.axis_index("narrow"), lax.axis_index("wide"), lax.axis_index(AXES)]
    ).astype(jnp.int32)
    weight_row = quad_weight[None, :]
    low, *high = masks_of(wide_count)
    core, *across = masks_of(narrow_count, wide_count)
    high_groups = in_pairs(high)
    plane_groups = in_pairs([low] + across)
    wide_groups = high_groups + [[low]]
    narrow_groups = [[core]] + in_pairs(across)
    source_groups = high_groups + [[core]]
    high_count = 1 << len(high)
    source_total = 2 * high_count * point_count
    target_count = narrow_count
    pair_row = pltpu.VMEM((2, point_count), jnp.float32)
    one_row = pltpu.VMEM((1, point_count), jnp.float32)
    pair_index = pltpu.VMEM((2, point_count), jnp.int32)
    field = pltpu.VMEM((2, point_count, rhs_count), jnp.float32)

    pack = call(
        restrict_kernel,
        f32(1, pack_rows, point_count),
        (agg_index, basis, points, weight_row),
        0,
        [pair_index, field, pair_row, one_row, pltpu.SemaphoreType.DMA((4,))],
        True,
    )
    inverse, member, smooth, weight = call(
        prefetch_kernel,
        [
            f32(*coarse_inverse.shape),
            f32(2, coarse_count, point_count),
            f32(2, point_count, rhs_count),
            f32(point_count, rhs_count),
        ],
        (pack, agg_index, basis, jacobi, weight_row, coarse_inverse),
        0,
        [pair_index, field, pair_row, one_row, pltpu.SemaphoreType.DMA((5,))],
        True,
    )
    packs = gather_steps(pack, wide_groups)
    coarse_outs = call(
        functools.partial(coarse_kernel, gather_order(wide_groups), 2, high_count),
        [f32(narrow_count // 2, coarse_count, rhs_count)] * 2
        + [f32(high_count, EXTRA, point_count), f32(2, EXTRA, point_count)],
        (index, inverse, *packs),
        1,
        [pltpu.VMEM((wide_count * coarse_count, rhs_count), jnp.float32)],
    )
    coarse_parts = scatter_steps(coarse_outs[:2], narrow_groups)
    sources = flip_each([coarse_outs[2]] * 2, [core])
    targets = gather_steps(coarse_outs[3], in_pairs(across))
    precond, first, last = call(
        precond_kernel,
        [b16(1, 2, point_count, rhs_count)] + [b16(2, width, rhs_count)] * 2,
        (member, smooth, *coarse_parts),
    )
    fields = gather_steps(precond, source_groups)
    forward = [(i, i + 1) for i in range(narrow_count * wide_count - 1)]
    before = lax.ppermute(last, AXES, forward)
    after = lax.ppermute(first, AXES, [(target, source) for source, target in forward])

    matrix_spec = pl.BlockSpec((1, 3, point_count, source_total), lambda k: (k, 0, 0, 0))
    matrix = pl.pallas_call(
        functools.partial(matrix_kernel, len(sources)),
        out_shape=b16(target_count, 3, point_count, source_total),
        grid=(target_count,),
        in_specs=[VMEM] * (len(sources) + len(targets)),
        out_specs=matrix_spec,
        compiler_params=PARAMS,
    )(*sources, *targets)
    ways = 1 << len(plane_groups[0])
    far_parts = pl.pallas_call(
        functools.partial(far_kernel, ways),
        out_shape=[f32(target_count // ways, 2, point_count, rhs_count)] * ways,
        grid=(target_count,),
        in_specs=[matrix_spec] + [VMEM] * len(fields),
        out_specs=[VMEM] * ways,
        scratch_shapes=[pltpu.VMEM((2, source_total, rhs_count), jnp.bfloat16)],
        compiler_params=PARAMS,
    )(matrix, *fields)
    far_parts = scatter_steps(far_parts, plane_groups)
    near_rows = jnp.transpose(near_block, (0, 2, 1, 3)).reshape(
        panels_dev, 2 * nodes, slot_total * 2 * nodes
    )
    base = call(
        near_kernel,
        f32(2, point_count, rhs_count),
        (index, near_panel, near_count, near_rows, before, precond, after),
        3,
        [
            pltpu.VMEM((2, 2 * width + point_count, rhs_count), jnp.bfloat16),
            pltpu.VMEM((panels_dev, slot_total * 2 * nodes, rhs_count), jnp.bfloat16),
        ],
    )

    hess_rows = block_total * rhs_count
    halving = [[core]] + plane_groups
    hess_masks = [core, low] + across
    image, *parts = call(
        functools.partial(project_kernel, hess_masks, 2),
        [f32(2, point_count, rhs_count)]
        + [f32(narrow_count, hess_rows // (2 * narrow_count), rhs_count)] * 2,
        (index, weight, basis, base, *far_parts),
        1,
        [pltpu.VMEM((hess_rows, rhs_count), jnp.float32)],
    )
    parts = sum_steps(parts, halving, high_groups)
    hessenberg, remainder, *gram_parts = call(
        functools.partial(
            remainder_kernel, gather_order(part_groups(halving)[::-1]), hess_masks, [core], 2
        ),
        [f32(hess_rows, rhs_count), f32(2 * point_count, rhs_count)]
        + [f32(1, rhs_count // 2, rhs_count)] * 2,
        (index, weight, basis, image, *parts),
        1,
        [pltpu.VMEM((rhs_count, rhs_count), jnp.float32)],
    )
    gram_parts = sum_steps(gram_parts, [[core]], plane_groups + high_groups)
    upper_factor, new_block = call(
        functools.partial(factor_kernel, gather_order([[1]]), [core]),
        [f32(rhs_count, rhs_count), f32(2 * point_count, rhs_count)],
        (index, remainder, *gram_parts),
        1,
        [pltpu.VMEM((rhs_count, rhs_count), jnp.float32)] * 2,
    )
    return (
        new_block.reshape(2, point_count, rhs_count),
        hessenberg.reshape(block_total, rhs_count, rhs_count),
        upper_factor,
    )


def solution(mesh):
    in_specs = (
        P(None, ("narrow", "wide")),
        P(("narrow", "wide")),
        P(None, None, ("narrow", "wide"), None),
        P(None, ("narrow", "wide")),
        P(("narrow", "wide"), None),
        P(("narrow", "wide")),
        P(("narrow", "wide"), None, None, None),
        P(None, ("narrow", "wide")),
        P(None, "wide", "narrow"),
    )
    out_specs = (P(None, ("narrow", "wide"), None), P(), P())
    return jax.shard_map(body, mesh=mesh, in_specs=in_specs, out_specs=out_specs, check_vma=False)
```

```python
import functools

import jax
import jax.numpy as jnp
from jax import lax
from jax.experimental import pallas as pl
from jax.experimental.pallas import tpu as pltpu
from jax.sharding import PartitionSpec as P

SPAN = 4


NU = 0.3
DELTA2 = 1e-05
ELASTIC = 40.0
AXES = ("narrow", "wide")
EXTRA = 8
ROWS = 8
SMEM = pl.BlockSpec(memory_space=pltpu.SMEM)
VMEM = pl.BlockSpec(memory_space=pltpu.VMEM)
ANY = pl.BlockSpec(memory_space=pl.ANY)
PARAMS = pltpu.CompilerParams(vmem_limit_bytes=48 * 1024 * 1024)


def split(value):
    high = value.astype(jnp.bfloat16)
    return high, (value - high.astype(jnp.float32)).astype(jnp.bfloat16)


def dot16(left, right, contract=((1,), (0,))):
    return lax.dot_general(left, right, (contract, ((), ())), preferred_element_type=jnp.float32)


def dot_rows(left, right, contract=((1,), (0,))):
    left_high, left_low = split(left)
    right_high, right_low = split(right)
    return dot16(left_high, right_high, contract) + (
        dot16(left_high, right_low, contract) + dot16(left_low, right_high, contract)
    )


def dot_first(left, right):
    return dot_rows(left, right, ((0,), (0,)))


def pick(member, value, contract=((1,), (0,))):
    member = member.astype(jnp.bfloat16)
    high, low = split(value)
    lowest = (value - high.astype(jnp.float32) - low.astype(jnp.float32)).astype(jnp.bfloat16)
    return dot16(member, high, contract) + (
        dot16(member, low, contract) + dot16(member, lowest, contract)
    )


def as_column(row, width):
    return jnp.transpose(jnp.broadcast_to(row, (width, row.shape[1])))


def flip(block, mask):
    count = lax.axis_size(AXES)
    return lax.ppermute(block, AXES, [(i, i ^ mask) for i in range(count)])


def masks_of(count, scale=1):
    return [scale << bit for bit in range(count.bit_length() - 1)]


def in_pairs(masks):
    return [masks[k : k + 2] for k in range(0, len(masks), 2)]


def combined(group, number):
    mask = 0
    for bit, part in enumerate(group):
        if number >> bit & 1:
            mask ^= part
    return mask


def flip_each(parts, group):
    return [parts[0]] + [flip(parts[j], combined(group, j)) for j in range(1, 1 << len(group))]


def join_kernel(*refs):
    out_ref = refs[-1]
    size = refs[0].shape[0]
    for j, ref in enumerate(refs[:-1]):
        out_ref[j * size : (j + 1) * size] = ref[...]


def join(parts):
    shape = (len(parts) * parts[0].shape[0],) + parts[0].shape[1:]
    return call(join_kernel, jax.ShapeDtypeStruct(shape, parts[0].dtype), parts)


def gather_steps(held, groups):
    parts = [held]
    for group in groups:
        held = parts[0] if len(parts) == 1 else join(parts)
        parts = flip_each([held] * (1 << len(group)), group)
    return parts


def gather_order(groups):
    order = [0]
    for group in groups:
        order = [k ^ combined(group, j) for j in range(1 << len(group)) for k in order]
    return order


def total_of(values):
    while len(values) > 1:
        values = [values[k] + values[k + 1] for k in range(0, len(values), 2)]
    return values[0]


def sum_kernel(count, *refs):
    parts, outs = refs[:count], refs[count:]
    for k in range(outs[0].shape[0]):
        for j, out_ref in enumerate(outs):
            out_ref[k] = total_of([part[k * len(outs) + j] for part in parts])


def sum_parts(parts, ways):
    out = f32(parts[0].shape[0] // ways, *parts[0].shape[1:])
    return call(functools.partial(sum_kernel, len(parts)), [out] * ways, parts)


def scatter_steps(parts, groups):
    for number, group in enumerate(groups):
        if number:
            parts = sum_parts(parts, 1 << len(group))
        parts = flip_each(parts, group)
    return parts


def sum_steps(parts, halving, butterfly):
    (total,) = sum_parts(scatter_steps(parts, halving), 1)
    for group in butterfly:
        (total,) = sum_parts(flip_each([total] * (1 << len(group)), group), 1)
    return gather_steps(total, halving[::-1])


def part_groups(groups):
    bit, found = 0, []
    for group in groups:
        found.append([1 << (bit + k) for k in range(len(group))])
        bit += len(group)
    return found


def bits_of(index, masks):
    packed = 0
    for bit, mask in enumerate(masks):
        packed = packed + (lax.shift_right_logical(index, mask.bit_length() - 1) & 1) * (1 << bit)
    return packed


def members(agg_ref, a, coarse_count):
    ids = lax.broadcasted_iota(jnp.int32, (coarse_count, agg_ref.shape[1]), 0)
    return jnp.where(ids == agg_ref[a : a + 1, :], 1.0, 0.0)


def load_all(pairs, sems):
    copies = [
        pltpu.make_async_copy(source, target, sems.at[k])
        for k, (source, target) in enumerate(pairs)
    ]
    for copy in copies:
        copy.start()
    for copy in copies:
        copy.wait()


def restrict_kernel(
    agg_hbm, basis_hbm, points_hbm, weight_hbm, pack_ref, agg_ref, newest_ref, points_ref, weight_ref, sems
):
    coarse_count = pack_ref.shape[1] - EXTRA
    point_count = newest_ref.shape[1]
    load_all(
        [
            (basis_hbm.at[basis_hbm.shape[0] - 1], newest_ref),
            (agg_hbm, agg_ref),
            (points_hbm, points_ref),
            (weight_hbm, weight_ref),
        ],
        sems,
    )
    total = pick(members(agg_ref, 0, coarse_count), newest_ref[0]) + pick(
        members(agg_ref, 1, coarse_count), newest_ref[1]
    )
    pack_ref[0, :coarse_count, :] = total
    pack_ref[0, coarse_count:, :] = jnp.concatenate(
        [points_ref[...], weight_ref[...], jnp.zeros((EXTRA - 3, point_count), jnp.float32)], axis=0
    )


def prefetch_kernel(
    pack_hbm,
    agg_hbm,
    basis_hbm,
    jacobi_hbm,
    weight_hbm,
    inverse_hbm,
    inverse_ref,
    member_ref,
    smooth_ref,
    weight_out_ref,
    agg_ref,
    newest_ref,
    jacobi_ref,
    weight_ref,
    sems,
):
    coarse_count = member_ref.shape[1]
    rhs_count = newest_ref.shape[2]
    load_all(
        [
            (basis_hbm.at[basis_hbm.shape[0] - 1], newest_ref),
            (agg_hbm, agg_ref),
            (jacobi_hbm, jacobi_ref),
            (weight_hbm, weight_ref),
            (inverse_hbm, inverse_ref),
        ],
        sems,
    )
    for a in range(2):
        member_ref[a] = members(agg_ref, a, coarse_count)
        smooth_ref[a] = as_column(jacobi_ref[a : a + 1, :], rhs_count) * newest_ref[a]
    weight_out_ref[...] = as_column(weight_ref[...], rhs_count)


def part_at(parts, k):
    size = parts[0].shape[0]
    return parts[k // size], k % size


def coarse_kernel(order, ways, z_count, rows, index_ref, inverse_ref, near_ref, *refs):
    narrow_count, coarse_count, _ = inverse_ref.shape
    packs = refs[: len(refs) - ways - 3]
    outs = refs[len(packs) : len(packs) + ways]
    source_ref, target_ref, rhs_ref = refs[len(packs) + ways :]
    for k, offset in enumerate(order):
        first = pl.multiple_of((index_ref[1] ^ offset) * coarse_count, 8)
        ref, row = part_at(packs, k)
        rhs_ref[pl.ds(first, coarse_count), :] = ref[row, :coarse_count, :]
    for k in range(z_count):
        ref, row = part_at(packs, k)
        source_ref[k] = ref[row, coarse_count:, :]
    for k in range(target_ref.shape[0]):
        ref, row = part_at(packs, k * z_count)
        target_ref[k] = ref[row, coarse_count:, :]
    left = jnp.concatenate(
        [inverse_ref[index_ref[0] ^ k] for k in range(narrow_count)], axis=0
    )
    product = dot_rows(left, rhs_ref[...])
    tail = jnp.concatenate([source_ref[k] for k in range(z_count)], axis=0)
    each = z_count * EXTRA // (narrow_count // ways)
    for k in range(narrow_count):
        part = product[k * coarse_count : (k + 1) * coarse_count, :]
        outs[k % ways][k // ways, :coarse_count, :] = part
        first = (k // ways) * each
        outs[k % ways][k // ways, coarse_count:, :] = tail[first : first + each, :]


def coarse_sum_kernel(ways, kept_ref, got_ref, target_ref, *refs):
    outs, source_ref = refs[:ways], refs[ways]
    rows = target_ref.shape[0] * EXTRA
    coarse_count = outs[0].shape[1] - rows
    each = (kept_ref.shape[1] - coarse_count) // EXTRA
    for k in range(kept_ref.shape[0]):
        for j in range(each):
            first = coarse_count + j * EXTRA
            source_ref[k * each + j] = got_ref[k, first : first + EXTRA, :]
    for k in range(outs[0].shape[0]):
        for j in range(ways):
            source = k * ways + j
            outs[j][k, :coarse_count, :] = (
                kept_ref[source, :coarse_count, :] + got_ref[source, :coarse_count, :]
            )
            for t in range(target_ref.shape[0]):
                first = coarse_count + t * EXTRA
                outs[j][k, first : first + EXTRA, :] = target_ref[t]


def precond_kernel(index_ref, member_ref, smooth_ref, *refs):
    parts = refs[:-3]
    precond_ref, pair_ref, next_ref = refs[-3:]
    coarse_count = member_ref.shape[1]
    point_count = smooth_ref.shape[1]
    width = pair_ref.shape[1]
    even = (index_ref[2] & 1) == 0
    coarse_sol = total_of([part[0, :coarse_count, :] for part in parts])
    for a in range(2):
        value = smooth_ref[a] + pick(member_ref[a], coarse_sol, ((0,), (0,)))
        precond_ref[0, a] = value.astype(jnp.bfloat16)
        first = value[:width]
        last = value[point_count - width :]
        pair_ref[a] = jnp.where(even, last, first).astype(jnp.bfloat16)
        next_ref[a] = jnp.where(even, first, last).astype(jnp.bfloat16)


def matrix_kernel(coarse_count, own_ref, other_ref, *refs):
    targets, matrix_ref = refs[:-1], refs[-1]
    point_count = own_ref.shape[2]
    size = (targets[0].shape[1] - coarse_count) // EXTRA
    step = pl.program_id(0)
    first = pl.multiple_of(coarse_count + lax.rem(step, size) * EXTRA, EXTRA)
    target = targets[0][0, pl.ds(first, EXTRA), :]
    for j in range(1, len(targets)):
        target = jnp.where(step // size == j, targets[j][0, pl.ds(first, EXTRA), :], target)
    target_x = as_column(target[0:1, :], point_count)
    target_y = as_column(target[1:2, :], point_count)
    for s in range(matrix_ref.shape[3] // point_count):
        ref, row = part_at((own_ref, other_ref), s)
        source = ref[row]
        delta_x = target_x - source[0:1, :]
        delta_y = target_y - source[1:2, :]
        factor = ELASTIC * source[2:3, :]
        square_x = delta_x * delta_x
        square_y = delta_y * delta_y
        square_dist = square_x + square_y + DELTA2
        inverse = 1.0 / square_dist
        log_part = (-0.5 * (3.0 - 4.0 * NU)) * jnp.log(square_dist)
        lanes = slice(s * point_count, (s + 1) * point_count)
        matrix_ref[0, 0, :, lanes] = (factor * (log_part + square_x * inverse)).astype(jnp.bfloat16)
        matrix_ref[0, 1, :, lanes] = (factor * (delta_x * delta_y * inverse)).astype(jnp.bfloat16)
        matrix_ref[0, 2, :, lanes] = (factor * (log_part + square_y * inverse)).astype(jnp.bfloat16)


def far_kernel(ways, pair_hbm, next_hbm, matrix_ref, *refs):
    fields = refs[: len(refs) - ways - 1]
    outs = refs[len(fields) : len(fields) + ways]
    fields_ref = refs[-1]
    point_count, rhs_count = fields[0].shape[2:]
    step = pl.program_id(0)

    @pl.when(step == 0)
    def _():
        for s in range(fields_ref.shape[0] // point_count):
            ref, row = part_at(fields, s)
            for b in range(2):
                rows = slice(s * point_count, (s + 1) * point_count)
                fields_ref[rows, b * rhs_count : (b + 1) * rhs_count] = ref[row, b]

    mixed = dot16(matrix_ref[0, 1], fields_ref[...])
    out_x = dot16(matrix_ref[0, 0], fields_ref[:, :rhs_count]) + mixed[:, rhs_count:]
    out_y = dot16(matrix_ref[0, 2], fields_ref[:, rhs_count:]) + mixed[:, :rhs_count]
    for j, out_ref in enumerate(outs):

        @pl.when(lax.rem(step, ways) == j)
        def _(out_ref=out_ref):
            out_ref[step // ways, 0] = out_x
            out_ref[step // ways, 1] = out_y


def near_kernel(
    index_ref,
    panel_ref,
    count_ref,
    block_ref,
    own_ref,
    pair_ref,
    next_ref,
    out_ref,
    line_ref,
    gathered_ref,
):
    point_count = own_ref.shape[2]
    width = pair_ref.shape[1]
    even = (index_ref[2] & 1) == 0
    panels_dev, double_nodes, _ = block_ref.shape
    nodes = double_nodes // 2
    slot_total = panel_ref.shape[1]
    for b in range(2):
        pair = pair_ref[b].astype(jnp.float32)
        following = next_ref[b].astype(jnp.float32)
        line_ref[b, :width, :] = jnp.where(even, following, pair).astype(jnp.bfloat16)
        line_ref[b, width : width + point_count, :] = own_ref[0, b]
        line_ref[b, width + point_count :, :] = jnp.where(even, pair, following).astype(
            jnp.bfloat16
        )
    first_panel = index_ref[2] * panels_dev
    lane = lax.broadcasted_iota(jnp.int32, block_ref.shape[1:], 1)
    for p in range(panels_dev):
        for k in range(slot_total):
            first = pl.multiple_of((panel_ref[p, k] - first_panel) * nodes + width, 16)
            for b in range(2):
                row = (k * 2 + b) * nodes
                gathered_ref[p, row : row + nodes, :] = line_ref[b, pl.ds(first, nodes), :]
        blocks = jnp.where(
            lane < count_ref[p] * double_nodes, block_ref[p].astype(jnp.float32), 0.0
        ).astype(jnp.bfloat16)
        near = dot16(blocks, gathered_ref[p])
        for a in range(2):
            rows = slice(p * nodes, (p + 1) * nodes)
            own = own_ref[0, a, rows, :].astype(jnp.float32)
            out_ref[a, rows, :] = 0.5 * own + near[a * nodes : (a + 1) * nodes, :]


def spread(full_ref, outs, own):
    rows = outs[0].shape[1]
    for k in range(len(outs) * outs[0].shape[0]):
        first = pl.multiple_of((own ^ k) * rows, 8)
        outs[k % len(outs)][k // len(outs)] = full_ref[pl.ds(first, rows), :]


def collect(order, parts, full_ref, own):
    rows = parts[0].shape[1]
    for k, offset in enumerate(order):
        first = pl.multiple_of((own ^ offset) * rows, 8)
        ref, row = part_at(parts, k)
        full_ref[pl.ds(first, rows), :] = ref[row]


def stacked(basis_ref):
    return jnp.concatenate(
        [
            jnp.concatenate([basis_ref[j, a] for j in range(basis_ref.shape[0])], axis=1)
            for a in range(2)
        ],
        axis=0,
    )


def project_kernel(masks, ways, index_ref, weight_ref, basis_ref, base_ref, *refs):
    arrived = refs[: len(refs) - ways - 2]
    image_ref = refs[len(arrived)]
    outs = refs[len(arrived) + 1 : -1]
    full_ref = refs[-1]
    weighted = []
    for a in range(2):
        image = base_ref[a] + total_of([part[0, a] for part in arrived])
        image_ref[a] = image
        weighted.append(image * weight_ref[...])
    full_ref[...] = dot_first(stacked(basis_ref), jnp.concatenate(weighted, axis=0))
    spread(full_ref, outs, bits_of(index_ref[2], masks))


def remainder_kernel(
    order, masks, gram_masks, ways, index_ref, weight_ref, basis_ref, image_ref, *refs
):
    parts = refs[: len(refs) - ways - 3]
    hess_ref, remainder_ref = refs[len(parts) : len(parts) + 2]
    outs = refs[len(parts) + 2 : -1]
    gram_ref = refs[-1]
    collect(order, parts, hess_ref, bits_of(index_ref[2], masks))
    image = jnp.concatenate([image_ref[0], image_ref[1]], axis=0)
    value = image - dot_rows(stacked(basis_ref), hess_ref[...])
    remainder_ref[...] = value
    weight = jnp.concatenate([weight_ref[...]] * 2, axis=0)
    gram_ref[...] = dot_first(value * weight, value)
    spread(gram_ref, outs, bits_of(index_ref[2], gram_masks))


def factor_kernel(gather, masks, index_ref, remainder_ref, *refs):
    parts = refs[:-4]
    upper_ref, new_ref, work_ref, inverse_ref = refs[-4:]
    order = remainder_ref.shape[1]
    tile = (ROWS, order)
    lane = lax.broadcasted_iota(jnp.int32, tile, 1)
    row = lax.broadcasted_iota(jnp.int32, tile, 0)
    collect(gather, parts, work_ref, bits_of(index_ref[2], masks))
    for block in range(order // ROWS):
        start = block * ROWS
        inverse_ref[start : start + ROWS, :] = jnp.where(lane == row + start, 1.0, 0.0)
    for block in range(order // ROWS):
        start = block * ROWS
        own = work_ref[start : start + ROWS, :]
        own_inverse = inverse_ref[start : start + ROWS, :]
        columns = [
            jnp.broadcast_to(own[:, start + m : start + m + 1], tile) for m in range(ROWS)
        ]
        entry = {
            (j, m): jnp.broadcast_to(columns[m][j : j + 1, :], tile)
            for m in range(ROWS)
            for j in range(m, ROWS)
        }
        scale = []
        for m in range(ROWS):
            scale.append(lax.rsqrt(entry[m, m]))
            for j in range(m + 1, ROWS):
                entry[j, m] = entry[j, m] * scale[m]
            for n in range(m + 1, ROWS):
                for j in range(n, ROWS):
                    entry[j, n] = entry[j, n] - entry[j, m] * entry[n, m]
        solved = []
        solved_inverse = []
        for m in range(ROWS):
            upper_row = jnp.broadcast_to(own[m : m + 1, :], tile)
            inverse_row = jnp.broadcast_to(own_inverse[m : m + 1, :], tile)
            for j in range(m):
                upper_row = upper_row - entry[m, j] * solved[j]
                inverse_row = inverse_row - entry[m, j] * solved_inverse[j]
            upper_row = upper_row * scale[m]
            inverse_row = inverse_row * scale[m]
            solved.append(upper_row)
            solved_inverse.append(inverse_row)
        upper_rows = solved[ROWS - 1]
        inverse_rows = solved_inverse[ROWS - 1]
        for m in range(ROWS - 1):
            upper_rows = jnp.where(row == m, solved[m], upper_rows)
            inverse_rows = jnp.where(row == m, solved_inverse[m], inverse_rows)
        upper_ref[start : start + ROWS, :] = jnp.where(lane >= row + start, upper_rows, 0.0)
        inverse_ref[start : start + ROWS, :] = inverse_rows
        for later in range(block + 1, order // ROWS):
            first = later * ROWS
            target = work_ref[first : first + ROWS, :]
            target_inverse = inverse_ref[first : first + ROWS, :]
            multiplier = []
            for m in range(ROWS):
                value = jnp.broadcast_to(target[:, start + m : start + m + 1], tile)
                for j in range(m):
                    value = value - multiplier[j] * entry[m, j]
                multiplier.append(value * scale[m])
            for m in range(ROWS):
                target = target - multiplier[m] * solved[m]
                target_inverse = target_inverse - multiplier[m] * solved_inverse[m]
            work_ref[first : first + ROWS, :] = target
            inverse_ref[first : first + ROWS, :] = target_inverse
    new_ref[...] = dot_rows(remainder_ref[...], inverse_ref[...], ((1,), (1,)))


def f32(*shape):
    return jax.ShapeDtypeStruct(shape, jnp.float32)


def b16(*shape):
    return jax.ShapeDtypeStruct(shape, jnp.bfloat16)


def call(kernel, out_shape, operands, scalars=0, scratch=(), in_hbm=False):
    many = isinstance(out_shape, (tuple, list))
    return pl.pallas_call(
        kernel,
        out_shape=out_shape,
        in_specs=[SMEM] * scalars + [ANY if in_hbm else VMEM] * (len(operands) - scalars),
        out_specs=[VMEM] * len(out_shape) if many else VMEM,
        scratch_shapes=list(scratch),
        compiler_params=None if in_hbm else PARAMS,
    )(*operands)


def body(
    points,
    quad_weight,
    basis,
    jacobi,
    near_panel,
    near_count,
    near_block,
    agg_index,
    coarse_inverse,
):
    block_total, _, point_count, rhs_count = basis.shape
    coarse_count = coarse_inverse.shape[1]
    narrow_count = lax.axis_size("narrow")
    wide_count = lax.axis_size("wide")
    panels_dev, slot_total = near_panel.shape
    nodes = near_block.shape[2] // 2
    width = SPAN * nodes
    pack_rows = coarse_count + EXTRA
    index = jnp.stack(
        [lax.axis_index("narrow"), lax.axis_index("wide"), lax.axis_index(AXES)]
    ).astype(jnp.int32)
    weight_row = quad_weight[None, :]
    low, *high = masks_of(wide_count)
    core, *across = masks_of(narrow_count, wide_count)
    high_groups = in_pairs(high)
    plane_groups = in_pairs([low] + across)
    wide_groups = high_groups + [[low]]
    narrow_groups = [[core]] + in_pairs(across)
    source_groups = high_groups + [[core]]
    high_count = 1 << len(high)
    source_total = 2 * high_count * point_count
    target_count = narrow_count
    pair_row = pltpu.VMEM((2, point_count), jnp.float32)
    one_row = pltpu.VMEM((1, point_count), jnp.float32)
    pair_index = pltpu.VMEM((2, point_count), jnp.int32)
    field = pltpu.VMEM((2, point_count, rhs_count), jnp.float32)

    pack = call(
        restrict_kernel,
        f32(1, pack_rows, point_count),
        (agg_index, basis, points, weight_row),
        0,
        [pair_index, field, pair_row, one_row, pltpu.SemaphoreType.DMA((4,))],
        True,
    )
    inverse, member, smooth, weight = call(
        prefetch_kernel,
        [
            f32(*coarse_inverse.shape),
            f32(2, coarse_count, point_count),
            f32(2, point_count, rhs_count),
            f32(point_count, rhs_count),
        ],
        (pack, agg_index, basis, jacobi, weight_row, coarse_inverse),
        0,
        [pair_index, field, pair_row, one_row, pltpu.SemaphoreType.DMA((5,))],
        True,
    )
    near_rows = jnp.transpose(near_block, (0, 2, 1, 3)).reshape(
        panels_dev, 2 * nodes, slot_total * 2 * nodes
    )
    packs = gather_steps(pack, wide_groups)
    source_rows = high_count * EXTRA // (narrow_count // 2)
    target_rows = 2 * EXTRA
    coarse_outs = pl.pallas_call(
        functools.partial(
            coarse_kernel, gather_order(wide_groups), 2, high_count, source_rows
        ),
        out_shape=[f32(narrow_count // 2, coarse_count + source_rows, rhs_count)] * 2
        + [f32(high_count, EXTRA, point_count), f32(2, EXTRA, point_count)],
        in_specs=[SMEM, VMEM, ANY] + [VMEM] * len(packs),
        out_specs=[VMEM] * 4,
        scratch_shapes=[pltpu.VMEM((wide_count * coarse_count, rhs_count), jnp.float32)],
        compiler_params=PARAMS,
    )(index, inverse, near_rows, *packs)
    own_sources = coarse_outs[2]
    kept, got = flip_each(coarse_outs[:2], [core])
    groups = in_pairs(across)
    ways = 1 << len(groups[0])
    *coarse_parts, other_sources = call(
        functools.partial(coarse_sum_kernel, ways),
        [f32(narrow_count // 2 // ways, coarse_count + target_rows, rhs_count)] * ways
        + [f32(high_count, EXTRA, point_count)],
        (kept, got, coarse_outs[3]),
    )
    coarse_parts = scatter_steps(coarse_parts, groups)
    precond, pair_edge, next_edge = call(
        precond_kernel,
        [b16(1, 2, point_count, rhs_count)] + [b16(2, width, rhs_count)] * 2,
        (index, member, smooth, *coarse_parts),
        1,
    )
    fields = gather_steps(precond, source_groups)
    device_count = narrow_count * wide_count
    pair_edge = flip(pair_edge, 1)
    pairs = [(i, i + 1) for i in range(1, device_count - 1, 2)]
    next_edge = lax.ppermute(next_edge, AXES, pairs + [(j, i) for i, j in pairs])

    matrix_spec = pl.BlockSpec((1, 3, point_count, source_total), lambda k: (k, 0, 0, 0))
    matrix = pl.pallas_call(
        functools.partial(matrix_kernel, coarse_count),
        out_shape=b16(target_count, 3, point_count, source_total),
        grid=(target_count,),
        in_specs=[VMEM] * (2 + len(coarse_parts)),
        out_specs=matrix_spec,
        compiler_params=PARAMS,
    )(own_sources, other_sources, *coarse_parts)
    ways = 1 << len(plane_groups[0])
    far_parts = pl.pallas_call(
        functools.partial(far_kernel, ways),
        out_shape=[f32(target_count // ways, 2, point_count, rhs_count)] * ways,
        grid=(target_count,),
        in_specs=[ANY, ANY, matrix_spec] + [VMEM] * len(fields),
        out_specs=[VMEM] * ways,
        scratch_shapes=[pltpu.VMEM((source_total, 2 * rhs_count), jnp.bfloat16)],
        compiler_params=PARAMS,
    )(pair_edge, next_edge, matrix, *fields)
    far_parts = scatter_steps(far_parts, plane_groups)
    base = call(
        near_kernel,
        f32(2, point_count, rhs_count),
        (index, near_panel, near_count, near_rows, precond, pair_edge, next_edge),
        3,
        [
            pltpu.VMEM((2, 2 * width + point_count, rhs_count), jnp.bfloat16),
            pltpu.VMEM((panels_dev, slot_total * 2 * nodes, rhs_count), jnp.bfloat16),
        ],
    )

    hess_rows = block_total * rhs_count
    halving = [[core]] + plane_groups
    hess_masks = [core, low] + across
    image, *parts = call(
        functools.partial(project_kernel, hess_masks, 2),
        [f32(2, point_count, rhs_count)]
        + [f32(narrow_count, hess_rows // (2 * narrow_count), rhs_count)] * 2,
        (index, weight, basis, base, *far_parts),
        1,
        [pltpu.VMEM((hess_rows, rhs_count), jnp.float32)],
    )
    parts = sum_steps(parts, halving, high_groups)
    hessenberg, remainder, *gram_parts = call(
        functools.partial(
            remainder_kernel, gather_order(part_groups(halving)[::-1]), hess_masks, [core], 2
        ),
        [f32(hess_rows, rhs_count), f32(2 * point_count, rhs_count)]
        + [f32(1, rhs_count // 2, rhs_count)] * 2,
        (index, weight, basis, image, *parts),
        1,
        [pltpu.VMEM((rhs_count, rhs_count), jnp.float32)],
    )
    gram_parts = sum_steps(gram_parts, [[core]], plane_groups + high_groups)
    upper_factor, new_block = call(
        functools.partial(factor_kernel, gather_order([[1]]), [core]),
        [f32(rhs_count, rhs_count), f32(2 * point_count, rhs_count)],
        (index, remainder, *gram_parts),
        1,
        [pltpu.VMEM((rhs_count, rhs_count), jnp.float32)] * 2,
    )
    return (
        new_block.reshape(2, point_count, rhs_count),
        hessenberg.reshape(block_total, rhs_count, rhs_count),
        upper_factor,
    )


def solution(mesh):
    in_specs = (
        P(None, ("narrow", "wide")),
        P(("narrow", "wide")),
        P(None, None, ("narrow", "wide"), None),
        P(None, ("narrow", "wide")),
        P(("narrow", "wide"), None),
        P(("narrow", "wide")),
        P(("narrow", "wide"), None, None, None),
        P(None, ("narrow", "wide")),
        P(None, "wide", "narrow"),
    )
    out_specs = (P(None, ("narrow", "wide"), None), P(), P())
    return jax.shard_map(body, mesh=mesh, in_specs=in_specs, out_specs=out_specs, check_vma=False)
```

```python
import functools

import jax
import jax.numpy as jnp
from jax import lax
from jax.experimental import pallas as pl
from jax.experimental.pallas import tpu as pltpu
from jax.sharding import PartitionSpec as P

SPAN = 4


NU = 0.3
DELTA2 = 1e-05
ELASTIC = 40.0
AXES = ("narrow", "wide")
EXTRA = 8
ROWS = 8
SMEM = pl.BlockSpec(memory_space=pltpu.SMEM)
VMEM = pl.BlockSpec(memory_space=pltpu.VMEM)
ANY = pl.BlockSpec(memory_space=pl.ANY)
PARAMS = pltpu.CompilerParams(vmem_limit_bytes=48 * 1024 * 1024)


def split(value):
    high = value.astype(jnp.bfloat16)
    return high, (value - high.astype(jnp.float32)).astype(jnp.bfloat16)


def dot16(left, right, contract=((1,), (0,))):
    return lax.dot_general(left, right, (contract, ((), ())), preferred_element_type=jnp.float32)


def dot_rows(left, right, contract=((1,), (0,))):
    left_high, left_low = split(left)
    right_high, right_low = split(right)
    return dot16(left_high, right_high, contract) + (
        dot16(left_high, right_low, contract) + dot16(left_low, right_high, contract)
    )


def dot_first(left, right):
    return dot_rows(left, right, ((0,), (0,)))


def pick(member, value, contract=((1,), (0,))):
    member = member.astype(jnp.bfloat16)
    high, low = split(value)
    lowest = (value - high.astype(jnp.float32) - low.astype(jnp.float32)).astype(jnp.bfloat16)
    return dot16(member, high, contract) + (
        dot16(member, low, contract) + dot16(member, lowest, contract)
    )


def as_column(row, width):
    return jnp.transpose(jnp.broadcast_to(row, (width, row.shape[1])))


def flip(block, mask):
    count = lax.axis_size(AXES)
    return lax.ppermute(block, AXES, [(i, i ^ mask) for i in range(count)])


def masks_of(count, scale=1):
    return [scale << bit for bit in range(count.bit_length() - 1)]


def in_pairs(masks):
    return [masks[k : k + 2] for k in range(0, len(masks), 2)]


def combined(group, number):
    mask = 0
    for bit, part in enumerate(group):
        if number >> bit & 1:
            mask ^= part
    return mask


def flip_each(parts, group):
    return [parts[0]] + [flip(parts[j], combined(group, j)) for j in range(1, 1 << len(group))]


def join_kernel(count, *refs):
    parts, out_ref = refs[-1 - count : -1], refs[-1]
    size = parts[0].shape[0]
    for j, ref in enumerate(parts):
        out_ref[j * size : (j + 1) * size] = ref[...]


def join(parts, after=()):
    shape = (len(parts) * parts[0].shape[0],) + parts[0].shape[1:]
    return pl.pallas_call(
        functools.partial(join_kernel, len(parts)),
        out_shape=jax.ShapeDtypeStruct(shape, parts[0].dtype),
        in_specs=[ANY] * len(after) + [VMEM] * len(parts),
        out_specs=VMEM,
        compiler_params=PARAMS,
    )(*after, *parts)


def gather_steps(held, groups, after=()):
    parts = [held]
    for group in groups:
        if len(parts) > 1:
            held = join(parts, after)
            after = ()
        parts = flip_each([held] * (1 << len(group)), group)
    return parts


def gather_order(groups):
    order = [0]
    for group in groups:
        order = [k ^ combined(group, j) for j in range(1 << len(group)) for k in order]
    return order


def total_of(values):
    while len(values) > 1:
        values = [values[k] + values[k + 1] for k in range(0, len(values), 2)]
    return values[0]


def sum_kernel(count, *refs):
    parts, outs = refs[:count], refs[count:]
    for k in range(outs[0].shape[0]):
        for j, out_ref in enumerate(outs):
            out_ref[k] = total_of([part[k * len(outs) + j] for part in parts])


def sum_parts(parts, ways):
    out = f32(parts[0].shape[0] // ways, *parts[0].shape[1:])
    return call(functools.partial(sum_kernel, len(parts)), [out] * ways, parts)


def scatter_steps(parts, groups):
    for number, group in enumerate(groups):
        if number:
            parts = sum_parts(parts, 1 << len(group))
        parts = flip_each(parts, group)
    return parts


def sum_steps(parts, halving, butterfly):
    (total,) = sum_parts(scatter_steps(parts, halving), 1)
    for group in butterfly:
        (total,) = sum_parts(flip_each([total] * (1 << len(group)), group), 1)
    return gather_steps(total, halving[::-1])


def part_groups(groups):
    bit, found = 0, []
    for group in groups:
        found.append([1 << (bit + k) for k in range(len(group))])
        bit += len(group)
    return found


def bits_of(index, masks):
    packed = 0
    for bit, mask in enumerate(masks):
        packed = packed + (lax.shift_right_logical(index, mask.bit_length() - 1) & 1) * (1 << bit)
    return packed


def members(agg_ref, a, coarse_count):
    ids = lax.broadcasted_iota(jnp.int32, (coarse_count, agg_ref.shape[1]), 0)
    return jnp.where(ids == agg_ref[a : a + 1, :], 1.0, 0.0)


def load_all(pairs, sems):
    copies = [
        pltpu.make_async_copy(source, target, sems.at[k])
        for k, (source, target) in enumerate(pairs)
    ]
    for copy in copies:
        copy.start()
    for copy in copies:
        copy.wait()


def restrict_kernel(
    agg_hbm, basis_hbm, points_hbm, weight_hbm, pack_ref, agg_ref, newest_ref, points_ref, weight_ref, sems
):
    coarse_count = pack_ref.shape[1] - EXTRA
    point_count = newest_ref.shape[1]
    load_all(
        [
            (basis_hbm.at[basis_hbm.shape[0] - 1], newest_ref),
            (agg_hbm, agg_ref),
            (points_hbm, points_ref),
            (weight_hbm, weight_ref),
        ],
        sems,
    )
    total = pick(members(agg_ref, 0, coarse_count), newest_ref[0]) + pick(
        members(agg_ref, 1, coarse_count), newest_ref[1]
    )
    pack_ref[0, :coarse_count, :] = total
    pack_ref[0, coarse_count:, :] = jnp.concatenate(
        [points_ref[...], weight_ref[...], jnp.zeros((EXTRA - 3, point_count), jnp.float32)], axis=0
    )


def prefetch_kernel(
    pack_hbm,
    agg_hbm,
    basis_hbm,
    jacobi_hbm,
    weight_hbm,
    inverse_hbm,
    inverse_ref,
    member_ref,
    smooth_ref,
    weight_out_ref,
    half_ref,
    agg_ref,
    basis_ref,
    jacobi_ref,
    weight_ref,
    sems,
):
    coarse_count = member_ref.shape[1]
    block_total, _, _, rhs_count = basis_ref.shape
    load_all(
        [
            (basis_hbm, basis_ref),
            (agg_hbm, agg_ref),
            (jacobi_hbm, jacobi_ref),
            (weight_hbm, weight_ref),
            (inverse_hbm, inverse_ref),
        ],
        sems,
    )
    for a in range(2):
        member_ref[a] = members(agg_ref, a, coarse_count)
        smooth_ref[a] = (
            as_column(jacobi_ref[a : a + 1, :], rhs_count) * basis_ref[block_total - 1, a]
        )
    weight = as_column(weight_ref[...], rhs_count)
    weight_out_ref[...] = weight
    right = stacked(basis_ref)
    number = 0
    for i in range(block_total):
        left = jnp.concatenate([basis_ref[i, a] * weight for a in range(2)], axis=0)
        row = dot_first(left, right[:, i * rhs_count :])
        for j in range(i, block_total):
            block = row[:, (j - i) * rhs_count : (j - i + 1) * rhs_count]
            half_ref[number] = block * 0.5 if i == j else block
            number += 1


def part_at(parts, k):
    size = parts[0].shape[0]
    return parts[k // size], k % size


def coarse_kernel(order, ways, z_count, index_ref, inverse_ref, *refs):
    narrow_count, coarse_count, _ = inverse_ref.shape
    packs = refs[: len(refs) - ways - 3]
    outs = refs[len(packs) : len(packs) + ways]
    source_ref, target_ref, rhs_ref = refs[len(packs) + ways :]
    for k, offset in enumerate(order):
        first = pl.multiple_of((index_ref[1] ^ offset) * coarse_count, 8)
        ref, row = part_at(packs, k)
        rhs_ref[pl.ds(first, coarse_count), :] = ref[row, :coarse_count, :]
    for k in range(z_count):
        ref, row = part_at(packs, k)
        source_ref[k] = ref[row, coarse_count:, :]
    for k in range(target_ref.shape[0]):
        ref, row = part_at(packs, k * z_count)
        target_ref[k] = ref[row, coarse_count:, :]
    left = jnp.concatenate(
        [inverse_ref[index_ref[0] ^ k] for k in range(narrow_count)], axis=0
    )
    product = dot_rows(left, rhs_ref[...])
    tail = jnp.concatenate([source_ref[k] for k in range(z_count)], axis=0)
    each = z_count * EXTRA // (narrow_count // ways)
    for k in range(narrow_count):
        part = product[k * coarse_count : (k + 1) * coarse_count, :]
        outs[k % ways][k // ways, :coarse_count, :] = part
        first = (k // ways) * each
        outs[k % ways][k // ways, coarse_count:, :] = tail[first : first + each, :]


def coarse_sum_kernel(ways, kept_ref, got_ref, target_ref, *refs):
    outs, source_ref = refs[:ways], refs[ways]
    rows = target_ref.shape[0] * EXTRA
    coarse_count = outs[0].shape[1] - rows
    each = (kept_ref.shape[1] - coarse_count) // EXTRA
    for k in range(kept_ref.shape[0]):
        for j in range(each):
            first = coarse_count + j * EXTRA
            source_ref[k * each + j] = got_ref[k, first : first + EXTRA, :]
    for k in range(outs[0].shape[0]):
        for j in range(ways):
            source = k * ways + j
            outs[j][k, :coarse_count, :] = (
                kept_ref[source, :coarse_count, :] + got_ref[source, :coarse_count, :]
            )
            for t in range(target_ref.shape[0]):
                first = coarse_count + t * EXTRA
                outs[j][k, first : first + EXTRA, :] = target_ref[t]


def precond_kernel(index_ref, member_ref, smooth_ref, near_ref, *refs):
    parts = refs[:-3]
    precond_ref, pair_ref, next_ref = refs[-3:]
    coarse_count = member_ref.shape[1]
    point_count = smooth_ref.shape[1]
    width = pair_ref.shape[1]
    even = (index_ref[2] & 1) == 0
    coarse_sol = total_of([part[0, :coarse_count, :] for part in parts])
    for a in range(2):
        value = smooth_ref[a] + pick(member_ref[a], coarse_sol, ((0,), (0,)))
        precond_ref[0, a] = value.astype(jnp.bfloat16)
        first = value[:width]
        last = value[point_count - width :]
        pair_ref[a] = jnp.where(even, last, first).astype(jnp.bfloat16)
        next_ref[a] = jnp.where(even, first, last).astype(jnp.bfloat16)


def matrix_kernel(coarse_count, own_ref, other_ref, *refs):
    targets, matrix_ref = refs[:-1], refs[-1]
    point_count = own_ref.shape[2]
    size = (targets[0].shape[1] - coarse_count) // EXTRA
    step = pl.program_id(0)
    first = pl.multiple_of(coarse_count + lax.rem(step, size) * EXTRA, EXTRA)
    target = targets[0][0, pl.ds(first, EXTRA), :]
    for j in range(1, len(targets)):
        target = jnp.where(step // size == j, targets[j][0, pl.ds(first, EXTRA), :], target)
    target_x = as_column(target[0:1, :], point_count)
    target_y = as_column(target[1:2, :], point_count)
    for s in range(matrix_ref.shape[3] // point_count):
        ref, row = part_at((own_ref, other_ref), s)
        source = ref[row]
        delta_x = target_x - source[0:1, :]
        delta_y = target_y - source[1:2, :]
        factor = ELASTIC * source[2:3, :]
        square_x = delta_x * delta_x
        square_y = delta_y * delta_y
        square_dist = square_x + square_y + DELTA2
        inverse = 1.0 / square_dist
        log_part = (-0.5 * (3.0 - 4.0 * NU)) * jnp.log(square_dist)
        lanes = slice(s * point_count, (s + 1) * point_count)
        matrix_ref[0, 0, :, lanes] = (factor * (log_part + square_x * inverse)).astype(jnp.bfloat16)
        matrix_ref[0, 1, :, lanes] = (factor * (delta_x * delta_y * inverse)).astype(jnp.bfloat16)
        matrix_ref[0, 2, :, lanes] = (factor * (log_part + square_y * inverse)).astype(jnp.bfloat16)


def far_kernel(ways, pair_hbm, next_hbm, matrix_ref, *refs):
    fields = refs[: len(refs) - ways - 1]
    outs = refs[len(fields) : len(fields) + ways]
    fields_ref = refs[-1]
    point_count, rhs_count = fields[0].shape[2:]
    step = pl.program_id(0)

    @pl.when(step == 0)
    def _():
        for s in range(fields_ref.shape[0] // point_count):
            ref, row = part_at(fields, s)
            for b in range(2):
                rows = slice(s * point_count, (s + 1) * point_count)
                fields_ref[rows, b * rhs_count : (b + 1) * rhs_count] = ref[row, b]

    mixed = dot16(matrix_ref[0, 1], fields_ref[...])
    out_x = dot16(matrix_ref[0, 0], fields_ref[:, :rhs_count]) + mixed[:, rhs_count:]
    out_y = dot16(matrix_ref[0, 2], fields_ref[:, rhs_count:]) + mixed[:, :rhs_count]
    for j, out_ref in enumerate(outs):

        @pl.when(lax.rem(step, ways) == j)
        def _(out_ref=out_ref):
            out_ref[step // ways, 0] = out_x
            out_ref[step // ways, 1] = out_y


def near_kernel(
    index_ref,
    panel_ref,
    count_ref,
    block_ref,
    own_ref,
    pair_ref,
    next_ref,
    out_ref,
    line_ref,
    gathered_ref,
):
    point_count = own_ref.shape[2]
    width = pair_ref.shape[1]
    even = (index_ref[2] & 1) == 0
    panels_dev, double_nodes, _ = block_ref.shape
    nodes = double_nodes // 2
    slot_total = panel_ref.shape[1]
    for b in range(2):
        pair = pair_ref[b].astype(jnp.float32)
        following = next_ref[b].astype(jnp.float32)
        line_ref[b, :width, :] = jnp.where(even, following, pair).astype(jnp.bfloat16)
        line_ref[b, width : width + point_count, :] = own_ref[0, b]
        line_ref[b, width + point_count :, :] = jnp.where(even, pair, following).astype(
            jnp.bfloat16
        )
    first_panel = index_ref[2] * panels_dev
    lane = lax.broadcasted_iota(jnp.int32, block_ref.shape[1:], 1)
    for p in range(panels_dev):
        for k in range(slot_total):
            first = pl.multiple_of((panel_ref[p, k] - first_panel) * nodes + width, 16)
            for b in range(2):
                row = (k * 2 + b) * nodes
                gathered_ref[p, row : row + nodes, :] = line_ref[b, pl.ds(first, nodes), :]
        blocks = jnp.where(
            lane < count_ref[p] * double_nodes, block_ref[p].astype(jnp.float32), 0.0
        ).astype(jnp.bfloat16)
        near = dot16(blocks, gathered_ref[p])
        for a in range(2):
            rows = slice(p * nodes, (p + 1) * nodes)
            own = own_ref[0, a, rows, :].astype(jnp.float32)
            out_ref[a, rows, :] = 0.5 * own + near[a * nodes : (a + 1) * nodes, :]


def spread(full_ref, outs, own):
    rows = outs[0].shape[1]
    for k in range(len(outs) * outs[0].shape[0]):
        first = pl.multiple_of((own ^ k) * rows, 8)
        outs[k % len(outs)][k // len(outs)] = full_ref[pl.ds(first, rows), :]


def collect(order, parts, full_ref, own):
    rows = parts[0].shape[1]
    for k, offset in enumerate(order):
        first = pl.multiple_of((own ^ offset) * rows, 8)
        ref, row = part_at(parts, k)
        full_ref[pl.ds(first, rows), :] = ref[row]


def stacked(basis_ref):
    return jnp.concatenate(
        [
            jnp.concatenate([basis_ref[j, a] for j in range(basis_ref.shape[0])], axis=1)
            for a in range(2)
        ],
        axis=0,
    )


def project_kernel(masks, ways, index_ref, weight_ref, basis_ref, base_ref, *refs):
    arrived = refs[: len(refs) - ways - 2]
    image_ref = refs[len(arrived)]
    outs = refs[len(arrived) + 1 : -1]
    full_ref = refs[-1]
    weighted = []
    for a in range(2):
        image = base_ref[a] + total_of([part[0, a] for part in arrived])
        image_ref[a] = image
        weighted.append(image * weight_ref[...])
    image = jnp.concatenate([image_ref[0], image_ref[1]], axis=0)
    left = jnp.concatenate([stacked(basis_ref), image], axis=1)
    full_ref[...] = dot_first(left, jnp.concatenate(weighted, axis=0))
    spread(full_ref, outs, bits_of(index_ref[2], masks))


def factor_kernel(gather, masks, index_ref, basis_ref, image_ref, half_ref, *refs):
    parts = refs[:-6]
    hess_ref, upper_ref, new_ref, full_ref, work_ref, inverse_ref = refs[-6:]
    block_total, _, _, order = basis_ref.shape
    hess_rows = block_total * order
    tile = (ROWS, order)
    lane = lax.broadcasted_iota(jnp.int32, tile, 1)
    row = lax.broadcasted_iota(jnp.int32, tile, 0)
    collect(gather, parts, full_ref, bits_of(index_ref[2], masks))
    hessenberg = full_ref[:hess_rows, :]
    hess_ref[...] = hessenberg
    rows = []
    number = 0
    for i in range(block_total):
        count = block_total - i
        left = jnp.concatenate([half_ref[number + j] for j in range(count)], axis=1)
        rows.append(dot_rows(left, full_ref[i * order : hess_rows, :]))
        number += count
    product = dot_first(hessenberg, jnp.concatenate(rows, axis=0) - hessenberg)
    work_ref[...] = full_ref[hess_rows:, :] + (product + jnp.transpose(product))
    for block in range(order // ROWS):
        start = block * ROWS
        inverse_ref[start : start + ROWS, :] = jnp.where(lane == row + start, 1.0, 0.0)
    for block in range(order // ROWS):
        start = block * ROWS
        own = work_ref[start : start + ROWS, :]
        own_inverse = inverse_ref[start : start + ROWS, :]
        columns = [
            jnp.broadcast_to(own[:, start + m : start + m + 1], tile) for m in range(ROWS)
        ]
        entry = {
            (j, m): jnp.broadcast_to(columns[m][j : j + 1, :], tile)
            for m in range(ROWS)
            for j in range(m, ROWS)
        }
        scale = []
        for m in range(ROWS):
            scale.append(lax.rsqrt(entry[m, m]))
            for j in range(m + 1, ROWS):
                entry[j, m] = entry[j, m] * scale[m]
            for n in range(m + 1, ROWS):
                for j in range(n, ROWS):
                    entry[j, n] = entry[j, n] - entry[j, m] * entry[n, m]
        solved = []
        solved_inverse = []
        for m in range(ROWS):
            upper_row = jnp.broadcast_to(own[m : m + 1, :], tile)
            inverse_row = jnp.broadcast_to(own_inverse[m : m + 1, :], tile)
            for j in range(m):
                upper_row = upper_row - entry[m, j] * solved[j]
                inverse_row = inverse_row - entry[m, j] * solved_inverse[j]
            upper_row = upper_row * scale[m]
            inverse_row = inverse_row * scale[m]
            solved.append(upper_row)
            solved_inverse.append(inverse_row)
        upper_rows = solved[ROWS - 1]
        inverse_rows = solved_inverse[ROWS - 1]
        for m in range(ROWS - 1):
            upper_rows = jnp.where(row == m, solved[m], upper_rows)
            inverse_rows = jnp.where(row == m, solved_inverse[m], inverse_rows)
        upper_ref[start : start + ROWS, :] = jnp.where(lane >= row + start, upper_rows, 0.0)
        inverse_ref[start : start + ROWS, :] = inverse_rows
        for later in range(block + 1, order // ROWS):
            first = later * ROWS
            target = work_ref[first : first + ROWS, :]
            target_inverse = inverse_ref[first : first + ROWS, :]
            multiplier = []
            for m in range(ROWS):
                value = jnp.broadcast_to(target[:, start + m : start + m + 1], tile)
                for j in range(m):
                    value = value - multiplier[j] * entry[m, j]
                multiplier.append(value * scale[m])
            for m in range(ROWS):
                target = target - multiplier[m] * solved[m]
                target_inverse = target_inverse - multiplier[m] * solved_inverse[m]
            work_ref[first : first + ROWS, :] = target
            inverse_ref[first : first + ROWS, :] = target_inverse
    image = jnp.concatenate([image_ref[0], image_ref[1]], axis=0)
    remainder = image - dot_rows(stacked(basis_ref), hessenberg)
    new_ref[...] = dot_rows(remainder, inverse_ref[...], ((1,), (1,)))


def f32(*shape):
    return jax.ShapeDtypeStruct(shape, jnp.float32)


def b16(*shape):
    return jax.ShapeDtypeStruct(shape, jnp.bfloat16)


def call(kernel, out_shape, operands, scalars=0, scratch=(), in_hbm=0):
    many = isinstance(out_shape, (tuple, list))
    free = len(operands) - in_hbm
    operands = list(operands[:free]) + [
        pltpu.with_memory_space_constraint(x, pltpu.HBM) for x in operands[free:]
    ]
    return pl.pallas_call(
        kernel,
        out_shape=out_shape,
        in_specs=[SMEM] * scalars + [ANY if in_hbm else VMEM] * (len(operands) - scalars),
        out_specs=[VMEM] * len(out_shape) if many else VMEM,
        scratch_shapes=list(scratch),
        compiler_params=PARAMS,
    )(*operands)


def body(
    points,
    quad_weight,
    basis,
    jacobi,
    near_panel,
    near_count,
    near_block,
    agg_index,
    coarse_inverse,
):
    block_total, _, point_count, rhs_count = basis.shape
    coarse_count = coarse_inverse.shape[1]
    narrow_count = lax.axis_size("narrow")
    wide_count = lax.axis_size("wide")
    panels_dev, slot_total = near_panel.shape
    nodes = near_block.shape[2] // 2
    width = SPAN * nodes
    pack_rows = coarse_count + EXTRA
    index = jnp.stack(
        [lax.axis_index("narrow"), lax.axis_index("wide"), lax.axis_index(AXES)]
    ).astype(jnp.int32)
    weight_row = quad_weight[None, :]
    low, *high = masks_of(wide_count)
    core, *across = masks_of(narrow_count, wide_count)
    high_groups = in_pairs(high)
    plane_groups = in_pairs([low] + across)
    wide_groups = high_groups + [[low]]
    narrow_groups = [[core]] + in_pairs(across)
    source_groups = high_groups + [[core]]
    high_count = 1 << len(high)
    source_total = 2 * high_count * point_count
    target_count = narrow_count
    pair_row = pltpu.VMEM((2, point_count), jnp.float32)
    one_row = pltpu.VMEM((1, point_count), jnp.float32)
    pair_index = pltpu.VMEM((2, point_count), jnp.int32)
    field = pltpu.VMEM((2, point_count, rhs_count), jnp.float32)

    pack = call(
        restrict_kernel,
        f32(1, pack_rows, point_count),
        (agg_index, basis, points, weight_row),
        0,
        [pair_index, field, pair_row, one_row, pltpu.SemaphoreType.DMA((4,))],
        4,
    )
    half_blocks = block_total * (block_total + 1) // 2
    inverse, member, smooth, weight, half_gram = call(
        prefetch_kernel,
        [
            f32(*coarse_inverse.shape),
            f32(2, coarse_count, point_count),
            f32(2, point_count, rhs_count),
            f32(point_count, rhs_count),
            f32(half_blocks, rhs_count, rhs_count),
        ],
        (pack, agg_index, basis, jacobi, weight_row, coarse_inverse),
        0,
        [
            pair_index,
            pltpu.VMEM(basis.shape, jnp.float32),
            pair_row,
            one_row,
            pltpu.SemaphoreType.DMA((5,)),
        ],
        5,
    )
    half_gram = lax.psum(half_gram, AXES)
    near_rows = jnp.transpose(near_block, (0, 2, 1, 3)).reshape(
        panels_dev, 2 * nodes, slot_total * 2 * nodes
    )
    packs = gather_steps(pack, wide_groups, (weight,))
    source_rows = high_count * EXTRA // (narrow_count // 2)
    target_rows = 2 * EXTRA
    coarse_outs = pl.pallas_call(
        functools.partial(
            coarse_kernel, gather_order(wide_groups), 2, high_count
        ),
        out_shape=[f32(narrow_count // 2, coarse_count + source_rows, rhs_count)] * 2
        + [f32(high_count, EXTRA, point_count), f32(2, EXTRA, point_count)],
        in_specs=[SMEM, VMEM] + [VMEM] * len(packs),
        out_specs=[VMEM] * 4,
        scratch_shapes=[pltpu.VMEM((wide_count * coarse_count, rhs_count), jnp.float32)],
        compiler_params=PARAMS,
    )(index, inverse, *packs)
    own_sources = coarse_outs[2]
    kept, got = flip_each(coarse_outs[:2], [core])
    groups = in_pairs(across)
    ways = 1 << len(groups[0])
    *coarse_parts, other_sources = call(
        functools.partial(coarse_sum_kernel, ways),
        [f32(narrow_count // 2 // ways, coarse_count + target_rows, rhs_count)] * ways
        + [f32(high_count, EXTRA, point_count)],
        (kept, got, coarse_outs[3]),
    )
    coarse_parts = scatter_steps(coarse_parts, groups)
    precond, pair_edge, next_edge = call(
        precond_kernel,
        [b16(1, 2, point_count, rhs_count)] + [b16(2, width, rhs_count)] * 2,
        (index, member, smooth, near_rows, *coarse_parts),
        1,
    )
    matrix_spec = pl.BlockSpec((1, 3, point_count, source_total), lambda k: (k, 0, 0, 0))
    matrix = pl.pallas_call(
        functools.partial(matrix_kernel, coarse_count),
        out_shape=b16(target_count, 3, point_count, source_total),
        grid=(target_count,),
        in_specs=[VMEM] * (2 + len(coarse_parts)),
        out_specs=matrix_spec,
        compiler_params=PARAMS,
    )(own_sources, other_sources, *coarse_parts)
    fields = gather_steps(precond, source_groups, (matrix,))
    device_count = narrow_count * wide_count
    pair_edge = flip(pair_edge, 1)
    pairs = [(i, i + 1) for i in range(1, device_count - 1, 2)]
    next_edge = lax.ppermute(next_edge, AXES, pairs + [(j, i) for i, j in pairs])

    ways = 1 << len(plane_groups[0])
    far_parts = pl.pallas_call(
        functools.partial(far_kernel, ways),
        out_shape=[f32(target_count // ways, 2, point_count, rhs_count)] * ways,
        grid=(target_count,),
        in_specs=[ANY, ANY, matrix_spec] + [VMEM] * len(fields),
        out_specs=[VMEM] * ways,
        scratch_shapes=[pltpu.VMEM((source_total, 2 * rhs_count), jnp.bfloat16)],
        compiler_params=PARAMS,
    )(pair_edge, next_edge, matrix, *fields)
    far_parts = scatter_steps(far_parts, plane_groups)
    base = call(
        near_kernel,
        f32(2, point_count, rhs_count),
        (index, near_panel, near_count, near_rows, precond, pair_edge, next_edge),
        3,
        [
            pltpu.VMEM((2, 2 * width + point_count, rhs_count), jnp.bfloat16),
            pltpu.VMEM((panels_dev, slot_total * 2 * nodes, rhs_count), jnp.bfloat16),
        ],
    )

    hess_rows = block_total * rhs_count
    sum_rows = hess_rows + rhs_count
    halving = [[core]] + plane_groups
    masks = [core, low] + across
    image, *parts = call(
        functools.partial(project_kernel, masks, 2),
        [f32(2, point_count, rhs_count)]
        + [f32(narrow_count, sum_rows // (2 * narrow_count), rhs_count)] * 2,
        (index, weight, basis, base, *far_parts),
        1,
        [pltpu.VMEM((sum_rows, rhs_count), jnp.float32)],
    )
    parts = sum_steps(parts, halving, high_groups)
    hessenberg, upper_factor, new_block = call(
        functools.partial(factor_kernel, gather_order(part_groups(halving)[::-1]), masks),
        [
            f32(hess_rows, rhs_count),
            f32(rhs_count, rhs_count),
            f32(2 * point_count, rhs_count),
        ],
        (index, basis, image, half_gram, *parts),
        1,
        [pltpu.VMEM((sum_rows, rhs_count), jnp.float32)]
        + [pltpu.VMEM((rhs_count, rhs_count), jnp.float32)] * 2,
    )
    return (
        new_block.reshape(2, point_count, rhs_count),
        hessenberg.reshape(block_total, rhs_count, rhs_count),
        upper_factor,
    )


def solution(mesh):
    in_specs = (
        P(None, ("narrow", "wide")),
        P(("narrow", "wide")),
        P(None, None, ("narrow", "wide"), None),
        P(None, ("narrow", "wide")),
        P(("narrow", "wide"), None),
        P(("narrow", "wide")),
        P(("narrow", "wide"), None, None, None),
        P(None, ("narrow", "wide")),
        P(None, "wide", "narrow"),
    )
    out_specs = (P(None, ("narrow", "wide"), None), P(), P())
    return jax.shard_map(body, mesh=mesh, in_specs=in_specs, out_specs=out_specs, check_vma=False)
```

```python
import functools

import jax
import jax.numpy as jnp
from jax import lax
from jax.experimental import pallas as pl
from jax.experimental.pallas import tpu as pltpu
from jax.sharding import PartitionSpec as P

SPAN = 4


NU = 0.3
DELTA2 = 1e-05
ELASTIC = 40.0
AXES = ("narrow", "wide")
EXTRA = 8
ROWS = 8
SMEM = pl.BlockSpec(memory_space=pltpu.SMEM)
VMEM = pl.BlockSpec(memory_space=pltpu.VMEM)
ANY = pl.BlockSpec(memory_space=pl.ANY)
PARAMS = pltpu.CompilerParams(vmem_limit_bytes=48 * 1024 * 1024)


def split(value):
    high = value.astype(jnp.bfloat16)
    return high, (value - high.astype(jnp.float32)).astype(jnp.bfloat16)


def dot16(left, right, contract=((1,), (0,))):
    return lax.dot_general(left, right, (contract, ((), ())), preferred_element_type=jnp.float32)


def dot_rows(left, right, contract=((1,), (0,))):
    left_high, left_low = split(left)
    right_high, right_low = split(right)
    return dot16(left_high, right_high, contract) + (
        dot16(left_high, right_low, contract) + dot16(left_low, right_high, contract)
    )


def dot_first(left, right):
    return dot_rows(left, right, ((0,), (0,)))


def pick(member, value, contract=((1,), (0,))):
    member = member.astype(jnp.bfloat16)
    high, low = split(value)
    lowest = (value - high.astype(jnp.float32) - low.astype(jnp.float32)).astype(jnp.bfloat16)
    return dot16(member, high, contract) + (
        dot16(member, low, contract) + dot16(member, lowest, contract)
    )


def as_column(row, width):
    return jnp.transpose(jnp.broadcast_to(row, (width, row.shape[1])))


def flip(block, mask):
    count = lax.axis_size(AXES)
    return lax.ppermute(block, AXES, [(i, i ^ mask) for i in range(count)])


def masks_of(count, scale=1):
    return [scale << bit for bit in range(count.bit_length() - 1)]


def in_pairs(masks):
    return [masks[k : k + 2] for k in range(0, len(masks), 2)]


def combined(group, number):
    mask = 0
    for bit, part in enumerate(group):
        if number >> bit & 1:
            mask ^= part
    return mask


def flip_each(parts, group):
    return [parts[0]] + [flip(parts[j], combined(group, j)) for j in range(1, 1 << len(group))]


def join_kernel(count, *refs):
    parts, out_ref = refs[-1 - count : -1], refs[-1]
    size = parts[0].shape[0]
    for j, ref in enumerate(parts):
        out_ref[j * size : (j + 1) * size] = ref[...]


def join(parts, after=()):
    shape = (len(parts) * parts[0].shape[0],) + parts[0].shape[1:]
    return pl.pallas_call(
        functools.partial(join_kernel, len(parts)),
        out_shape=jax.ShapeDtypeStruct(shape, parts[0].dtype),
        in_specs=[ANY] * len(after) + [VMEM] * len(parts),
        out_specs=VMEM,
        compiler_params=PARAMS,
    )(*after, *parts)


def gather_steps(held, groups, after=()):
    parts = [held]
    for group in groups:
        if len(parts) > 1:
            held = join(parts, after)
            after = ()
        parts = flip_each([held] * (1 << len(group)), group)
    return parts


def gather_order(groups):
    order = [0]
    for group in groups:
        order = [k ^ combined(group, j) for j in range(1 << len(group)) for k in order]
    return order


def total_of(values):
    while len(values) > 1:
        values = [values[k] + values[k + 1] for k in range(0, len(values), 2)]
    return values[0]


def sum_kernel(count, skip, *refs):
    parts, outs = refs[skip : skip + count], refs[skip + count :]
    for k in range(outs[0].shape[0]):
        for j, out_ref in enumerate(outs):
            out_ref[k] = total_of([part[k * len(outs) + j] for part in parts])


def sum_parts(parts, ways, after=()):
    out = f32(parts[0].shape[0] // ways, *parts[0].shape[1:])
    return pl.pallas_call(
        functools.partial(sum_kernel, len(parts), len(after)),
        out_shape=[out] * ways,
        in_specs=[ANY] * len(after) + [VMEM] * len(parts),
        out_specs=[VMEM] * ways,
        compiler_params=PARAMS,
    )(*after, *parts)


def scatter_steps(parts, groups):
    for number, group in enumerate(groups):
        if number:
            parts = sum_parts(parts, 1 << len(group))
        parts = flip_each(parts, group)
    return parts


def sum_butterfly(total, groups):
    for group in groups:
        (total,) = sum_parts(flip_each([total] * (1 << len(group)), group), 1)
    return total


def append_kernel(left_ref, right_ref, out_ref):
    rows = left_ref.shape[1]
    out_ref[:, :rows, :] = left_ref[...]
    out_ref[:, rows:, :] = right_ref[...]


def append(left, right):
    count, rows, width = left.shape
    shape = f32(count, rows + right.shape[1], width)
    return call(append_kernel, shape, (left, right))


def part_groups(groups):
    bit, found = 0, []
    for group in groups:
        found.append([1 << (bit + k) for k in range(len(group))])
        bit += len(group)
    return found


def bits_of(index, masks):
    packed = 0
    for bit, mask in enumerate(masks):
        packed = packed + (lax.shift_right_logical(index, mask.bit_length() - 1) & 1) * (1 << bit)
    return packed


def members(agg_ref, a, coarse_count):
    ids = lax.broadcasted_iota(jnp.int32, (coarse_count, agg_ref.shape[1]), 0)
    return jnp.where(ids == agg_ref[a : a + 1, :], 1.0, 0.0)


def load_all(pairs, sems):
    copies = [
        pltpu.make_async_copy(source, target, sems.at[k])
        for k, (source, target) in enumerate(pairs)
    ]
    for copy in copies:
        copy.start()
    for copy in copies:
        copy.wait()


def restrict_kernel(
    agg_hbm, basis_hbm, points_hbm, weight_hbm, pack_ref, agg_ref, newest_ref, points_ref, weight_ref, sems
):
    coarse_count = pack_ref.shape[1] - EXTRA
    point_count = newest_ref.shape[1]
    load_all(
        [
            (basis_hbm.at[basis_hbm.shape[0] - 1], newest_ref),
            (agg_hbm, agg_ref),
            (points_hbm, points_ref),
            (weight_hbm, weight_ref),
        ],
        sems,
    )
    total = pick(members(agg_ref, 0, coarse_count), newest_ref[0]) + pick(
        members(agg_ref, 1, coarse_count), newest_ref[1]
    )
    pack_ref[0, :coarse_count, :] = total
    pack_ref[0, coarse_count:, :] = jnp.concatenate(
        [points_ref[...], weight_ref[...], jnp.zeros((EXTRA - 3, point_count), jnp.float32)], axis=0
    )


def prefetch_kernel(
    masks,
    index_ref,
    pack_hbm,
    agg_hbm,
    basis_hbm,
    jacobi_hbm,
    weight_hbm,
    inverse_hbm,
    inverse_ref,
    member_ref,
    smooth_ref,
    weight_out_ref,
    keep_ref,
    send_ref,
    half_ref,
    agg_ref,
    basis_ref,
    jacobi_ref,
    weight_ref,
    sems,
):
    coarse_count = member_ref.shape[1]
    block_total, _, _, rhs_count = basis_ref.shape
    load_all(
        [
            (basis_hbm, basis_ref),
            (agg_hbm, agg_ref),
            (jacobi_hbm, jacobi_ref),
            (weight_hbm, weight_ref),
            (inverse_hbm, inverse_ref),
        ],
        sems,
    )
    for a in range(2):
        member_ref[a] = members(agg_ref, a, coarse_count)
        smooth_ref[a] = (
            as_column(jacobi_ref[a : a + 1, :], rhs_count) * basis_ref[block_total - 1, a]
        )
    weight = as_column(weight_ref[...], rhs_count)
    weight_out_ref[...] = weight
    right = stacked(basis_ref)
    number = 0
    for i in range(block_total):
        left = jnp.concatenate([basis_ref[i, a] * weight for a in range(2)], axis=0)
        row = dot_first(left, right[:, i * rhs_count :])
        for j in range(i, block_total):
            block = row[:, (j - i) * rhs_count : (j - i + 1) * rhs_count]
            rows = slice(number * rhs_count, (number + 1) * rhs_count)
            half_ref[rows, :] = block * 0.5 if i == j else block
            number += 1
    spread(half_ref, (keep_ref, send_ref), bits_of(index_ref[2], masks))


def part_at(parts, k):
    size = parts[0].shape[0]
    return parts[k // size], k % size


def coarse_kernel(order, ways, z_count, index_ref, inverse_ref, *refs):
    narrow_count, coarse_count, _ = inverse_ref.shape
    packs = refs[: len(refs) - ways - 3]
    outs = refs[len(packs) : len(packs) + ways]
    source_ref, target_ref, rhs_ref = refs[len(packs) + ways :]
    for k, offset in enumerate(order):
        first = pl.multiple_of((index_ref[1] ^ offset) * coarse_count, 8)
        ref, row = part_at(packs, k)
        rhs_ref[pl.ds(first, coarse_count), :] = ref[row, :coarse_count, :]
    for k in range(z_count):
        ref, row = part_at(packs, k)
        source_ref[k] = ref[row, coarse_count:, :]
    for k in range(target_ref.shape[0]):
        ref, row = part_at(packs, k * z_count)
        target_ref[k] = ref[row, coarse_count:, :]
    left = jnp.concatenate(
        [inverse_ref[index_ref[0] ^ k] for k in range(narrow_count)], axis=0
    )
    product = dot_rows(left, rhs_ref[...])
    tail = jnp.concatenate([source_ref[k] for k in range(z_count)], axis=0)
    each = z_count * EXTRA // (narrow_count // ways)
    for k in range(narrow_count):
        part = product[k * coarse_count : (k + 1) * coarse_count, :]
        outs[k % ways][k // ways, :coarse_count, :] = part
        first = (k // ways) * each
        outs[k % ways][k // ways, coarse_count:, :] = tail[first : first + each, :]


def coarse_sum_kernel(ways, kept_ref, got_ref, target_ref, *refs):
    outs, source_ref = refs[:ways], refs[ways]
    rows = target_ref.shape[0] * EXTRA
    coarse_count = outs[0].shape[1] - rows
    each = (kept_ref.shape[1] - coarse_count) // EXTRA
    for k in range(kept_ref.shape[0]):
        for j in range(each):
            first = coarse_count + j * EXTRA
            source_ref[k * each + j] = got_ref[k, first : first + EXTRA, :]
    for k in range(outs[0].shape[0]):
        for j in range(ways):
            source = k * ways + j
            outs[j][k, :coarse_count, :] = (
                kept_ref[source, :coarse_count, :] + got_ref[source, :coarse_count, :]
            )
            for t in range(target_ref.shape[0]):
                first = coarse_count + t * EXTRA
                outs[j][k, first : first + EXTRA, :] = target_ref[t]


def precond_kernel(index_ref, member_ref, smooth_ref, near_ref, *refs):
    parts = refs[:-3]
    precond_ref, pair_ref, next_ref = refs[-3:]
    coarse_count = member_ref.shape[1]
    point_count = smooth_ref.shape[1]
    width = pair_ref.shape[1]
    even = (index_ref[2] & 1) == 0
    coarse_sol = total_of([part[0, :coarse_count, :] for part in parts])
    for a in range(2):
        value = smooth_ref[a] + pick(member_ref[a], coarse_sol, ((0,), (0,)))
        precond_ref[0, a] = value.astype(jnp.bfloat16)
        first = value[:width]
        last = value[point_count - width :]
        pair_ref[a] = jnp.where(even, last, first).astype(jnp.bfloat16)
        next_ref[a] = jnp.where(even, first, last).astype(jnp.bfloat16)


def matrix_kernel(coarse_count, own_ref, other_ref, *refs):
    targets, matrix_ref = refs[:-1], refs[-1]
    point_count = own_ref.shape[2]
    size = (targets[0].shape[1] - coarse_count) // EXTRA
    step = pl.program_id(0)
    first = pl.multiple_of(coarse_count + lax.rem(step, size) * EXTRA, EXTRA)
    target = targets[0][0, pl.ds(first, EXTRA), :]
    for j in range(1, len(targets)):
        target = jnp.where(step // size == j, targets[j][0, pl.ds(first, EXTRA), :], target)
    target_x = as_column(target[0:1, :], point_count)
    target_y = as_column(target[1:2, :], point_count)
    for s in range(matrix_ref.shape[3] // point_count):
        ref, row = part_at((own_ref, other_ref), s)
        source = ref[row]
        delta_x = target_x - source[0:1, :]
        delta_y = target_y - source[1:2, :]
        factor = ELASTIC * source[2:3, :]
        square_x = delta_x * delta_x
        square_y = delta_y * delta_y
        square_dist = square_x + square_y + DELTA2
        inverse = 1.0 / square_dist
        log_part = (-0.5 * (3.0 - 4.0 * NU)) * jnp.log(square_dist)
        lanes = slice(s * point_count, (s + 1) * point_count)
        matrix_ref[0, 0, :, lanes] = (factor * (log_part + square_x * inverse)).astype(jnp.bfloat16)
        matrix_ref[0, 1, :, lanes] = (factor * (delta_x * delta_y * inverse)).astype(jnp.bfloat16)
        matrix_ref[0, 2, :, lanes] = (factor * (log_part + square_y * inverse)).astype(jnp.bfloat16)


def far_kernel(ways, pair_hbm, next_hbm, matrix_ref, *refs):
    fields = refs[: len(refs) - ways - 1]
    outs = refs[len(fields) : len(fields) + ways]
    fields_ref = refs[-1]
    point_count, rhs_count = fields[0].shape[2:]
    step = pl.program_id(0)

    @pl.when(step == 0)
    def _():
        for s in range(fields_ref.shape[0] // point_count):
            ref, row = part_at(fields, s)
            for b in range(2):
                rows = slice(s * point_count, (s + 1) * point_count)
                fields_ref[rows, b * rhs_count : (b + 1) * rhs_count] = ref[row, b]

    mixed = dot16(matrix_ref[0, 1], fields_ref[...])
    out_x = dot16(matrix_ref[0, 0], fields_ref[:, :rhs_count]) + mixed[:, rhs_count:]
    out_y = dot16(matrix_ref[0, 2], fields_ref[:, rhs_count:]) + mixed[:, :rhs_count]
    for j, out_ref in enumerate(outs):

        @pl.when(lax.rem(step, ways) == j)
        def _(out_ref=out_ref):
            out_ref[step // ways, 0] = out_x
            out_ref[step // ways, 1] = out_y


def near_kernel(
    index_ref,
    panel_ref,
    count_ref,
    block_ref,
    own_ref,
    pair_ref,
    next_ref,
    out_ref,
    line_ref,
    gathered_ref,
):
    point_count = own_ref.shape[2]
    width = pair_ref.shape[1]
    even = (index_ref[2] & 1) == 0
    panels_dev, double_nodes, _ = block_ref.shape
    nodes = double_nodes // 2
    slot_total = panel_ref.shape[1]
    for b in range(2):
        pair = pair_ref[b].astype(jnp.float32)
        following = next_ref[b].astype(jnp.float32)
        line_ref[b, :width, :] = jnp.where(even, following, pair).astype(jnp.bfloat16)
        line_ref[b, width : width + point_count, :] = own_ref[0, b]
        line_ref[b, width + point_count :, :] = jnp.where(even, pair, following).astype(
            jnp.bfloat16
        )
    first_panel = index_ref[2] * panels_dev
    lane = lax.broadcasted_iota(jnp.int32, block_ref.shape[1:], 1)
    for p in range(panels_dev):
        for k in range(slot_total):
            first = pl.multiple_of((panel_ref[p, k] - first_panel) * nodes + width, 16)
            for b in range(2):
                row = (k * 2 + b) * nodes
                gathered_ref[p, row : row + nodes, :] = line_ref[b, pl.ds(first, nodes), :]
        blocks = jnp.where(
            lane < count_ref[p] * double_nodes, block_ref[p].astype(jnp.float32), 0.0
        ).astype(jnp.bfloat16)
        near = dot16(blocks, gathered_ref[p])
        for a in range(2):
            rows = slice(p * nodes, (p + 1) * nodes)
            own = own_ref[0, a, rows, :].astype(jnp.float32)
            out_ref[a, rows, :] = 0.5 * own + near[a * nodes : (a + 1) * nodes, :]


def spread(full_ref, outs, own):
    rows = outs[0].shape[1]
    for k in range(len(outs) * outs[0].shape[0]):
        first = pl.multiple_of((own ^ k) * rows, 8)
        outs[k % len(outs)][k // len(outs)] = full_ref[pl.ds(first, rows), :]


def collect(order, parts, full_ref, own, start):
    rows = full_ref.shape[0] // len(order)
    for k, offset in enumerate(order):
        first = pl.multiple_of((own ^ offset) * rows, 8)
        ref, row = part_at(parts, k)
        full_ref[pl.ds(first, rows), :] = ref[row, start : start + rows, :]


def stacked(basis_ref):
    return jnp.concatenate(
        [
            jnp.concatenate([basis_ref[j, a] for j in range(basis_ref.shape[0])], axis=1)
            for a in range(2)
        ],
        axis=0,
    )


def project_kernel(masks, ways, index_ref, half_hbm, weight_ref, basis_ref, base_ref, *refs):
    arrived = refs[: len(refs) - ways - 2]
    image_ref = refs[len(arrived)]
    outs = refs[len(arrived) + 1 : -1]
    full_ref = refs[-1]
    weighted = []
    for a in range(2):
        image = base_ref[a] + total_of([part[0, a] for part in arrived])
        image_ref[a] = image
        weighted.append(image * weight_ref[...])
    image = jnp.concatenate([image_ref[0], image_ref[1]], axis=0)
    left = jnp.concatenate([stacked(basis_ref), image], axis=1)
    full_ref[...] = dot_first(left, jnp.concatenate(weighted, axis=0))
    spread(full_ref, outs, bits_of(index_ref[2], masks))


def factor_kernel(gather, masks, index_ref, basis_ref, image_ref, *refs):
    parts = refs[:-7]
    hess_ref, upper_ref, new_ref, full_ref, half_ref, work_ref, inverse_ref = refs[-7:]
    block_total, _, _, order = basis_ref.shape
    hess_rows = block_total * order
    tile = (ROWS, order)
    lane = lax.broadcasted_iota(jnp.int32, tile, 1)
    row = lax.broadcasted_iota(jnp.int32, tile, 0)
    own = bits_of(index_ref[2], masks)
    collect(gather, parts, full_ref, own, 0)
    collect(gather, parts, half_ref, own, full_ref.shape[0] // len(gather))
    hessenberg = full_ref[:hess_rows, :]
    hess_ref[...] = hessenberg
    rows = []
    number = 0
    for i in range(block_total):
        count = block_total - i
        left = jnp.concatenate(
            [
                half_ref[(number + j) * order : (number + j + 1) * order, :]
                for j in range(count)
            ],
            axis=1,
        )
        rows.append(dot_rows(left, full_ref[i * order : hess_rows, :]))
        number += count
    product = dot_first(hessenberg, jnp.concatenate(rows, axis=0) - hessenberg)
    work_ref[...] = full_ref[hess_rows:, :] + (product + jnp.transpose(product))
    for block in range(order // ROWS):
        start = block * ROWS
        inverse_ref[start : start + ROWS, :] = jnp.where(lane == row + start, 1.0, 0.0)
    for block in range(order // ROWS):
        start = block * ROWS
        own = work_ref[start : start + ROWS, :]
        own_inverse = inverse_ref[start : start + ROWS, :]
        columns = [
            jnp.broadcast_to(own[:, start + m : start + m + 1], tile) for m in range(ROWS)
        ]
        entry = {
            (j, m): jnp.broadcast_to(columns[m][j : j + 1, :], tile)
            for m in range(ROWS)
            for j in range(m, ROWS)
        }
        scale = []
        for m in range(ROWS):
            scale.append(lax.rsqrt(entry[m, m]))
            for j in range(m + 1, ROWS):
                entry[j, m] = entry[j, m] * scale[m]
            for n in range(m + 1, ROWS):
                for j in range(n, ROWS):
                    entry[j, n] = entry[j, n] - entry[j, m] * entry[n, m]
        solved = []
        solved_inverse = []
        for m in range(ROWS):
            upper_row = jnp.broadcast_to(own[m : m + 1, :], tile)
            inverse_row = jnp.broadcast_to(own_inverse[m : m + 1, :], tile)
            for j in range(m):
                upper_row = upper_row - entry[m, j] * solved[j]
                inverse_row = inverse_row - entry[m, j] * solved_inverse[j]
            upper_row = upper_row * scale[m]
            inverse_row = inverse_row * scale[m]
            solved.append(upper_row)
            solved_inverse.append(inverse_row)
        upper_rows = solved[ROWS - 1]
        inverse_rows = solved_inverse[ROWS - 1]
        for m in range(ROWS - 1):
            upper_rows = jnp.where(row == m, solved[m], upper_rows)
            inverse_rows = jnp.where(row == m, solved_inverse[m], inverse_rows)
        upper_ref[start : start + ROWS, :] = jnp.where(lane >= row + start, upper_rows, 0.0)
        inverse_ref[start : start + ROWS, :] = inverse_rows
        for later in range(block + 1, order // ROWS):
            first = later * ROWS
            target = work_ref[first : first + ROWS, :]
            target_inverse = inverse_ref[first : first + ROWS, :]
            multiplier = []
            for m in range(ROWS):
                value = jnp.broadcast_to(target[:, start + m : start + m + 1], tile)
                for j in range(m):
                    value = value - multiplier[j] * entry[m, j]
                multiplier.append(value * scale[m])
            for m in range(ROWS):
                target = target - multiplier[m] * solved[m]
                target_inverse = target_inverse - multiplier[m] * solved_inverse[m]
            work_ref[first : first + ROWS, :] = target
            inverse_ref[first : first + ROWS, :] = target_inverse
    image = jnp.concatenate([image_ref[0], image_ref[1]], axis=0)
    remainder = image - dot_rows(stacked(basis_ref), hessenberg)
    new_ref[...] = dot_rows(remainder, inverse_ref[...], ((1,), (1,)))


def f32(*shape):
    return jax.ShapeDtypeStruct(shape, jnp.float32)


def b16(*shape):
    return jax.ShapeDtypeStruct(shape, jnp.bfloat16)


def call(kernel, out_shape, operands, scalars=0, scratch=(), in_hbm=0):
    many = isinstance(out_shape, (tuple, list))
    free = len(operands) - in_hbm
    operands = list(operands[:free]) + [
        pltpu.with_memory_space_constraint(x, pltpu.HBM) for x in operands[free:]
    ]
    return pl.pallas_call(
        kernel,
        out_shape=out_shape,
        in_specs=[SMEM] * scalars + [ANY if in_hbm else VMEM] * (len(operands) - scalars),
        out_specs=[VMEM] * len(out_shape) if many else VMEM,
        scratch_shapes=list(scratch),
        compiler_params=PARAMS,
    )(*operands)


def body(
    points,
    quad_weight,
    basis,
    jacobi,
    near_panel,
    near_count,
    near_block,
    agg_index,
    coarse_inverse,
):
    block_total, _, point_count, rhs_count = basis.shape
    coarse_count = coarse_inverse.shape[1]
    narrow_count = lax.axis_size("narrow")
    wide_count = lax.axis_size("wide")
    panels_dev, slot_total = near_panel.shape
    nodes = near_block.shape[2] // 2
    width = SPAN * nodes
    pack_rows = coarse_count + EXTRA
    index = jnp.stack(
        [lax.axis_index("narrow"), lax.axis_index("wide"), lax.axis_index(AXES)]
    ).astype(jnp.int32)
    weight_row = quad_weight[None, :]
    low, *high = masks_of(wide_count)
    core, *across = masks_of(narrow_count, wide_count)
    high_groups = in_pairs(high)
    plane_groups = in_pairs([low] + across)
    wide_groups = high_groups + [[low]]
    narrow_groups = [[core]] + in_pairs(across)
    source_groups = high_groups + [[core]]
    high_count = 1 << len(high)
    source_total = 2 * high_count * point_count
    target_count = narrow_count
    pair_row = pltpu.VMEM((2, point_count), jnp.float32)
    one_row = pltpu.VMEM((1, point_count), jnp.float32)
    pair_index = pltpu.VMEM((2, point_count), jnp.int32)
    field = pltpu.VMEM((2, point_count, rhs_count), jnp.float32)

    pack = call(
        restrict_kernel,
        f32(1, pack_rows, point_count),
        (agg_index, basis, points, weight_row),
        0,
        [pair_index, field, pair_row, one_row, pltpu.SemaphoreType.DMA((4,))],
        4,
    )
    half_rows = block_total * (block_total + 1) // 2 * rhs_count
    halving = [[core]] + plane_groups
    masks = [core, low] + across
    inverse, member, smooth, weight, *half_parts = call(
        functools.partial(prefetch_kernel, masks),
        [
            f32(*coarse_inverse.shape),
            f32(2, coarse_count, point_count),
            f32(2, point_count, rhs_count),
            f32(point_count, rhs_count),
        ]
        + [f32(narrow_count, half_rows // (2 * narrow_count), rhs_count)] * 2,
        (index, pack, agg_index, basis, jacobi, weight_row, coarse_inverse),
        1,
        [
            pltpu.VMEM((half_rows, rhs_count), jnp.float32),
            pair_index,
            pltpu.VMEM(basis.shape, jnp.float32),
            pair_row,
            one_row,
            pltpu.SemaphoreType.DMA((5,)),
        ],
        5,
    )
    half_parts = flip_each(half_parts, [core])
    near_rows = jnp.transpose(near_block, (0, 2, 1, 3)).reshape(
        panels_dev, 2 * nodes, slot_total * 2 * nodes
    )
    packs = gather_steps(pack, wide_groups, (weight,))
    source_rows = high_count * EXTRA // (narrow_count // 2)
    target_rows = 2 * EXTRA
    coarse_outs = pl.pallas_call(
        functools.partial(
            coarse_kernel, gather_order(wide_groups), 2, high_count
        ),
        out_shape=[f32(narrow_count // 2, coarse_count + source_rows, rhs_count)] * 2
        + [f32(high_count, EXTRA, point_count), f32(2, EXTRA, point_count)],
        in_specs=[SMEM, VMEM] + [VMEM] * len(packs),
        out_specs=[VMEM] * 4,
        scratch_shapes=[pltpu.VMEM((wide_count * coarse_count, rhs_count), jnp.float32)],
        compiler_params=PARAMS,
    )(index, inverse, *packs)
    own_sources = coarse_outs[2]
    kept, got = flip_each(coarse_outs[:2], [core])
    groups = in_pairs(across)
    ways = 1 << len(groups[0])
    *coarse_parts, other_sources = call(
        functools.partial(coarse_sum_kernel, ways),
        [f32(narrow_count // 2 // ways, coarse_count + target_rows, rhs_count)] * ways
        + [f32(high_count, EXTRA, point_count)],
        (kept, got, coarse_outs[3]),
    )
    coarse_parts = scatter_steps(coarse_parts, groups)
    precond, pair_edge, next_edge = call(
        precond_kernel,
        [b16(1, 2, point_count, rhs_count)] + [b16(2, width, rhs_count)] * 2,
        (index, member, smooth, near_rows, *coarse_parts),
        1,
    )
    matrix_spec = pl.BlockSpec((1, 3, point_count, source_total), lambda k: (k, 0, 0, 0))
    matrix = pl.pallas_call(
        functools.partial(matrix_kernel, coarse_count),
        out_shape=b16(target_count, 3, point_count, source_total),
        grid=(target_count,),
        in_specs=[VMEM] * (2 + len(coarse_parts)),
        out_specs=matrix_spec,
        compiler_params=PARAMS,
    )(own_sources, other_sources, *coarse_parts)
    fields = flip_each([precond] * (1 << len(source_groups[0])), source_groups[0])
    half_parts = sum_parts(half_parts, 1 << len(plane_groups[0]), fields[1:])
    (half_total,) = sum_parts(scatter_steps(half_parts, plane_groups), 1)
    fields = gather_steps(join(fields, (matrix,)), source_groups[1:])
    device_count = narrow_count * wide_count
    pair_edge = flip(pair_edge, 1)
    pairs = [(i, i + 1) for i in range(1, device_count - 1, 2)]
    next_edge = lax.ppermute(next_edge, AXES, pairs + [(j, i) for i, j in pairs])

    ways = 1 << len(plane_groups[0])
    far_parts = pl.pallas_call(
        functools.partial(far_kernel, ways),
        out_shape=[f32(target_count // ways, 2, point_count, rhs_count)] * ways,
        grid=(target_count,),
        in_specs=[ANY, ANY, matrix_spec] + [VMEM] * len(fields),
        out_specs=[VMEM] * ways,
        scratch_shapes=[pltpu.VMEM((source_total, 2 * rhs_count), jnp.bfloat16)],
        compiler_params=PARAMS,
    )(pair_edge, next_edge, matrix, *fields)
    far_parts = scatter_steps(far_parts, plane_groups)
    base = call(
        near_kernel,
        f32(2, point_count, rhs_count),
        (index, near_panel, near_count, near_rows, precond, pair_edge, next_edge),
        3,
        [
            pltpu.VMEM((2, 2 * width + point_count, rhs_count), jnp.bfloat16),
            pltpu.VMEM((panels_dev, slot_total * 2 * nodes, rhs_count), jnp.bfloat16),
        ],
    )

    hess_rows = block_total * rhs_count
    sum_rows = hess_rows + rhs_count
    half_total = sum_butterfly(half_total, high_groups)
    image, *parts = pl.pallas_call(
        functools.partial(project_kernel, masks, 2),
        out_shape=[f32(2, point_count, rhs_count)]
        + [f32(narrow_count, sum_rows // (2 * narrow_count), rhs_count)] * 2,
        in_specs=[SMEM, ANY] + [VMEM] * (3 + len(far_parts)),
        out_specs=[VMEM] * 3,
        scratch_shapes=[pltpu.VMEM((sum_rows, rhs_count), jnp.float32)],
        compiler_params=PARAMS,
    )(index, half_total, weight, basis, base, *far_parts)
    (total,) = sum_parts(scatter_steps(parts, halving), 1)
    total = sum_butterfly(total, high_groups)
    parts = gather_steps(append(total, half_total), halving[::-1])
    hessenberg, upper_factor, new_block = call(
        functools.partial(factor_kernel, gather_order(part_groups(halving)[::-1]), masks),
        [
            f32(hess_rows, rhs_count),
            f32(rhs_count, rhs_count),
            f32(2 * point_count, rhs_count),
        ],
        (index, basis, image, *parts),
        1,
        [
            pltpu.VMEM((sum_rows, rhs_count), jnp.float32),
            pltpu.VMEM((half_rows, rhs_count), jnp.float32),
        ]
        + [pltpu.VMEM((rhs_count, rhs_count), jnp.float32)] * 2,
    )
    return (
        new_block.reshape(2, point_count, rhs_count),
        hessenberg.reshape(block_total, rhs_count, rhs_count),
        upper_factor,
    )


def solution(mesh):
    in_specs = (
        P(None, ("narrow", "wide")),
        P(("narrow", "wide")),
        P(None, None, ("narrow", "wide"), None),
        P(None, ("narrow", "wide")),
        P(("narrow", "wide"), None),
        P(("narrow", "wide")),
        P(("narrow", "wide"), None, None, None),
        P(None, ("narrow", "wide")),
        P(None, "wide", "narrow"),
    )
    out_specs = (P(None, ("narrow", "wide"), None), P(), P())
    return jax.shard_map(body, mesh=mesh, in_specs=in_specs, out_specs=out_specs, check_vma=False)
```

```python
import functools

import jax
import jax.numpy as jnp
from jax import lax
from jax.experimental import pallas as pl
from jax.experimental.pallas import tpu as pltpu
from jax.sharding import PartitionSpec as P

SPAN = 4


NU = 0.3
DELTA2 = 1e-05
ELASTIC = 40.0
AXES = ("narrow", "wide")
EXTRA = 8
ROWS = 8
SMEM = pl.BlockSpec(memory_space=pltpu.SMEM)
VMEM = pl.BlockSpec(memory_space=pltpu.VMEM)
ANY = pl.BlockSpec(memory_space=pl.ANY)
PARAMS = pltpu.CompilerParams(vmem_limit_bytes=48 * 1024 * 1024)


def split(value):
    high = value.astype(jnp.bfloat16)
    return high, (value - high.astype(jnp.float32)).astype(jnp.bfloat16)


def dot16(left, right, contract=((1,), (0,))):
    return lax.dot_general(left, right, (contract, ((), ())), preferred_element_type=jnp.float32)


def dot_rows(left, right, contract=((1,), (0,))):
    left_high, left_low = split(left)
    right_high, right_low = split(right)
    return dot16(left_high, right_high, contract) + (
        dot16(left_high, right_low, contract) + dot16(left_low, right_high, contract)
    )


def dot_first(left, right):
    return dot_rows(left, right, ((0,), (0,)))


def pick(member, value, contract=((1,), (0,))):
    member = member.astype(jnp.bfloat16)
    high, low = split(value)
    lowest = (value - high.astype(jnp.float32) - low.astype(jnp.float32)).astype(jnp.bfloat16)
    return dot16(member, high, contract) + (
        dot16(member, low, contract) + dot16(member, lowest, contract)
    )


def as_column(row, width):
    return jnp.transpose(jnp.broadcast_to(row, (width, row.shape[1])))


def flip(block, mask):
    count = lax.axis_size(AXES)
    return lax.ppermute(block, AXES, [(i, i ^ mask) for i in range(count)])


def masks_of(count, scale=1):
    return [scale << bit for bit in range(count.bit_length() - 1)]


def in_pairs(masks):
    return [masks[k : k + 2] for k in range(0, len(masks), 2)]


def combined(group, number):
    mask = 0
    for bit, part in enumerate(group):
        if number >> bit & 1:
            mask ^= part
    return mask


def flip_each(parts, group):
    return [parts[0]] + [flip(parts[j], combined(group, j)) for j in range(1, 1 << len(group))]


def join_kernel(count, *refs):
    parts, out_ref = refs[-1 - count : -1], refs[-1]
    size = parts[0].shape[0]
    for j, ref in enumerate(parts):
        out_ref[j * size : (j + 1) * size] = ref[...]


def join(parts, after=()):
    shape = (len(parts) * parts[0].shape[0],) + parts[0].shape[1:]
    return pl.pallas_call(
        functools.partial(join_kernel, len(parts)),
        out_shape=jax.ShapeDtypeStruct(shape, parts[0].dtype),
        in_specs=[ANY] * len(after) + [VMEM] * len(parts),
        out_specs=VMEM,
        compiler_params=PARAMS,
    )(*after, *parts)


def gather_steps(held, groups, after=()):
    parts = [held]
    for group in groups:
        if len(parts) > 1:
            held = join(parts, after)
            after = ()
        parts = flip_each([held] * (1 << len(group)), group)
    return parts


def gather_order(groups):
    order = [0]
    for group in groups:
        order = [k ^ combined(group, j) for j in range(1 << len(group)) for k in order]
    return order


def total_of(values):
    while len(values) > 1:
        values = [values[k] + values[k + 1] for k in range(0, len(values), 2)]
    return values[0]


def sum_kernel(count, skip, *refs):
    parts, outs = refs[skip : skip + count], refs[skip + count :]
    for k in range(outs[0].shape[0]):
        for j, out_ref in enumerate(outs):
            out_ref[k] = total_of([part[k * len(outs) + j] for part in parts])


def sum_parts(parts, ways, after=()):
    out = f32(parts[0].shape[0] // ways, *parts[0].shape[1:])
    return pl.pallas_call(
        functools.partial(sum_kernel, len(parts), len(after)),
        out_shape=[out] * ways,
        in_specs=[ANY] * len(after) + [VMEM] * len(parts),
        out_specs=[VMEM] * ways,
        compiler_params=PARAMS,
    )(*after, *parts)


def scatter_steps(parts, groups):
    for number, group in enumerate(groups):
        if number:
            parts = sum_parts(parts, 1 << len(group))
        parts = flip_each(parts, group)
    return parts


def sum_butterfly(total, groups):
    for group in groups:
        (total,) = sum_parts(flip_each([total] * (1 << len(group)), group), 1)
    return total


def append_kernel(left_ref, right_ref, out_ref):
    rows = left_ref.shape[1]
    out_ref[:, :rows, :] = left_ref[...]
    out_ref[:, rows:, :] = right_ref[...]


def append(left, right):
    count, rows, width = left.shape
    shape = f32(count, rows + right.shape[1], width)
    return call(append_kernel, shape, (left, right))


def part_groups(groups):
    bit, found = 0, []
    for group in groups:
        found.append([1 << (bit + k) for k in range(len(group))])
        bit += len(group)
    return found


def bits_of(index, masks):
    packed = 0
    for bit, mask in enumerate(masks):
        packed = packed + (lax.shift_right_logical(index, mask.bit_length() - 1) & 1) * (1 << bit)
    return packed


def members(agg_ref, a, coarse_count):
    ids = lax.broadcasted_iota(jnp.int32, (coarse_count, agg_ref.shape[1]), 0)
    return jnp.where(ids == agg_ref[a : a + 1, :], 1.0, 0.0)


def load_all(pairs, sems):
    copies = [
        pltpu.make_async_copy(source, target, sems.at[k])
        for k, (source, target) in enumerate(pairs)
    ]
    for copy in copies:
        copy.start()
    for copy in copies:
        copy.wait()


def restrict_kernel(
    agg_hbm, basis_hbm, points_hbm, weight_hbm, pack_ref, agg_ref, newest_ref, points_ref, weight_ref, sems
):
    coarse_count = pack_ref.shape[1] - EXTRA
    point_count = newest_ref.shape[1]
    load_all(
        [
            (basis_hbm.at[basis_hbm.shape[0] - 1], newest_ref),
            (agg_hbm, agg_ref),
            (points_hbm, points_ref),
            (weight_hbm, weight_ref),
        ],
        sems,
    )
    total = pick(members(agg_ref, 0, coarse_count), newest_ref[0]) + pick(
        members(agg_ref, 1, coarse_count), newest_ref[1]
    )
    pack_ref[0, :coarse_count, :] = total
    pack_ref[0, coarse_count:, :] = jnp.concatenate(
        [points_ref[...], weight_ref[...], jnp.zeros((EXTRA - 3, point_count), jnp.float32)], axis=0
    )


def prefetch_kernel(
    masks,
    index_ref,
    pack_hbm,
    agg_hbm,
    basis_hbm,
    jacobi_hbm,
    weight_hbm,
    inverse_hbm,
    inverse_ref,
    member_ref,
    smooth_ref,
    weight_out_ref,
    keep_ref,
    send_ref,
    half_ref,
    agg_ref,
    basis_ref,
    jacobi_ref,
    weight_ref,
    sems,
):
    coarse_count = member_ref.shape[1]
    block_total, _, _, rhs_count = basis_ref.shape
    load_all(
        [
            (basis_hbm, basis_ref),
            (agg_hbm, agg_ref),
            (jacobi_hbm, jacobi_ref),
            (weight_hbm, weight_ref),
            (inverse_hbm, inverse_ref),
        ],
        sems,
    )
    for a in range(2):
        member_ref[a] = members(agg_ref, a, coarse_count)
        smooth_ref[a] = (
            as_column(jacobi_ref[a : a + 1, :], rhs_count) * basis_ref[block_total - 1, a]
        )
    weight = as_column(weight_ref[...], rhs_count)
    weight_out_ref[...] = weight
    right = stacked(basis_ref)
    number = 0
    for i in range(block_total):
        left = jnp.concatenate([basis_ref[i, a] * weight for a in range(2)], axis=0)
        row = dot_first(left, right[:, i * rhs_count :])
        for j in range(i, block_total):
            block = row[:, (j - i) * rhs_count : (j - i + 1) * rhs_count]
            rows = slice(number * rhs_count, (number + 1) * rhs_count)
            half_ref[rows, :] = block * 0.5 if i == j else block
            number += 1
    spread(half_ref, (keep_ref, send_ref), bits_of(index_ref[2], masks))


def part_at(parts, k):
    size = parts[0].shape[0]
    return parts[k // size], k % size


def coarse_kernel(order, ways, z_count, index_ref, near_ref, inverse_ref, *refs):
    narrow_count, coarse_count, _ = inverse_ref.shape
    packs = refs[: len(refs) - ways - 3]
    outs = refs[len(packs) : len(packs) + ways]
    source_ref, target_ref, rhs_ref = refs[len(packs) + ways :]
    for k, offset in enumerate(order):
        first = pl.multiple_of((index_ref[1] ^ offset) * coarse_count, 8)
        ref, row = part_at(packs, k)
        rhs_ref[pl.ds(first, coarse_count), :] = ref[row, :coarse_count, :]
    for k in range(z_count):
        ref, row = part_at(packs, k)
        source_ref[k] = ref[row, coarse_count:, :]
    for k in range(target_ref.shape[0]):
        ref, row = part_at(packs, k * z_count)
        target_ref[k] = ref[row, coarse_count:, :]
    left = jnp.concatenate(
        [inverse_ref[index_ref[0] ^ k] for k in range(narrow_count)], axis=0
    )
    product = dot_rows(left, rhs_ref[...])
    tail = jnp.concatenate([source_ref[k] for k in range(z_count)], axis=0)
    each = z_count * EXTRA // (narrow_count // ways)
    for k in range(narrow_count):
        part = product[k * coarse_count : (k + 1) * coarse_count, :]
        outs[k % ways][k // ways, :coarse_count, :] = part
        first = (k // ways) * each
        outs[k % ways][k // ways, coarse_count:, :] = tail[first : first + each, :]


def coarse_sum_kernel(ways, kept_ref, got_ref, target_ref, *refs):
    outs, source_ref = refs[:ways], refs[ways]
    rows = target_ref.shape[0] * EXTRA
    coarse_count = outs[0].shape[1] - rows
    each = (kept_ref.shape[1] - coarse_count) // EXTRA
    for k in range(kept_ref.shape[0]):
        for j in range(each):
            first = coarse_count + j * EXTRA
            source_ref[k * each + j] = got_ref[k, first : first + EXTRA, :]
    for k in range(outs[0].shape[0]):
        for j in range(ways):
            source = k * ways + j
            outs[j][k, :coarse_count, :] = (
                kept_ref[source, :coarse_count, :] + got_ref[source, :coarse_count, :]
            )
            for t in range(target_ref.shape[0]):
                first = coarse_count + t * EXTRA
                outs[j][k, first : first + EXTRA, :] = target_ref[t]


def precond_kernel(index_ref, member_ref, smooth_ref, *refs):
    parts = refs[:-3]
    precond_ref, pair_ref, next_ref = refs[-3:]
    coarse_count = member_ref.shape[1]
    point_count = smooth_ref.shape[1]
    width = pair_ref.shape[1]
    even = (index_ref[2] & 1) == 0
    coarse_sol = total_of([part[0, :coarse_count, :] for part in parts])
    for a in range(2):
        value = smooth_ref[a] + pick(member_ref[a], coarse_sol, ((0,), (0,)))
        precond_ref[0, a] = value.astype(jnp.bfloat16)
        first = value[:width]
        last = value[point_count - width :]
        pair_ref[a] = jnp.where(even, last, first).astype(jnp.bfloat16)
        next_ref[a] = jnp.where(even, first, last).astype(jnp.bfloat16)


def matrix_kernel(coarse_count, own_ref, other_ref, *refs):
    targets, matrix_ref = refs[:-1], refs[-1]
    point_count = own_ref.shape[2]
    size = (targets[0].shape[1] - coarse_count) // EXTRA
    step = pl.program_id(0)
    first = pl.multiple_of(coarse_count + lax.rem(step, size) * EXTRA, EXTRA)
    target = targets[0][0, pl.ds(first, EXTRA), :]
    for j in range(1, len(targets)):
        target = jnp.where(step // size == j, targets[j][0, pl.ds(first, EXTRA), :], target)
    target_x = as_column(target[0:1, :], point_count)
    target_y = as_column(target[1:2, :], point_count)
    for s in range(matrix_ref.shape[3] // point_count):
        ref, row = part_at((own_ref, other_ref), s)
        source = ref[row]
        delta_x = target_x - source[0:1, :]
        delta_y = target_y - source[1:2, :]
        factor = ELASTIC * source[2:3, :]
        square_x = delta_x * delta_x
        square_y = delta_y * delta_y
        square_dist = square_x + square_y + DELTA2
        inverse = 1.0 / square_dist
        log_part = (-0.5 * (3.0 - 4.0 * NU)) * jnp.log(square_dist)
        lanes = slice(s * point_count, (s + 1) * point_count)
        matrix_ref[0, 0, :, lanes] = (factor * (log_part + square_x * inverse)).astype(jnp.bfloat16)
        matrix_ref[0, 1, :, lanes] = (factor * (delta_x * delta_y * inverse)).astype(jnp.bfloat16)
        matrix_ref[0, 2, :, lanes] = (factor * (log_part + square_y * inverse)).astype(jnp.bfloat16)


def far_kernel(ways, skip, *refs):
    matrix_ref, *refs = refs[skip:]
    fields = refs[: len(refs) - ways - 1]
    outs = refs[len(fields) : len(fields) + ways]
    fields_ref = refs[-1]
    point_count, rhs_count = fields[0].shape[2:]
    step = pl.program_id(0)

    @pl.when(step == 0)
    def _():
        for s in range(fields_ref.shape[0] // point_count):
            ref, row = part_at(fields, s)
            for b in range(2):
                rows = slice(s * point_count, (s + 1) * point_count)
                fields_ref[rows, b * rhs_count : (b + 1) * rhs_count] = ref[row, b]

    mixed = dot16(matrix_ref[0, 1], fields_ref[...])
    out_x = dot16(matrix_ref[0, 0], fields_ref[:, :rhs_count]) + mixed[:, rhs_count:]
    out_y = dot16(matrix_ref[0, 2], fields_ref[:, rhs_count:]) + mixed[:, :rhs_count]
    for j, out_ref in enumerate(outs):

        @pl.when(lax.rem(step, ways) == j)
        def _(out_ref=out_ref):
            out_ref[step // ways, 0] = out_x
            out_ref[step // ways, 1] = out_y


def near_kernel(
    index_ref,
    panel_ref,
    count_ref,
    block_ref,
    own_ref,
    pair_ref,
    next_ref,
    out_ref,
    line_ref,
    gathered_ref,
):
    point_count = own_ref.shape[2]
    width = pair_ref.shape[1]
    even = (index_ref[2] & 1) == 0
    panels_dev, double_nodes, _ = block_ref.shape
    nodes = double_nodes // 2
    slot_total = panel_ref.shape[1]
    for b in range(2):
        pair = pair_ref[b].astype(jnp.float32)
        following = next_ref[b].astype(jnp.float32)
        line_ref[b, :width, :] = jnp.where(even, following, pair).astype(jnp.bfloat16)
        line_ref[b, width : width + point_count, :] = own_ref[0, b]
        line_ref[b, width + point_count :, :] = jnp.where(even, pair, following).astype(
            jnp.bfloat16
        )
    first_panel = index_ref[2] * panels_dev
    lane = lax.broadcasted_iota(jnp.int32, block_ref.shape[1:], 1)
    for p in range(panels_dev):
        for k in range(slot_total):
            first = pl.multiple_of((panel_ref[p, k] - first_panel) * nodes + width, 16)
            for b in range(2):
                row = (k * 2 + b) * nodes
                gathered_ref[p, row : row + nodes, :] = line_ref[b, pl.ds(first, nodes), :]
        blocks = jnp.where(
            lane < count_ref[p] * double_nodes, block_ref[p].astype(jnp.float32), 0.0
        ).astype(jnp.bfloat16)
        near = dot16(blocks, gathered_ref[p])
        for a in range(2):
            rows = slice(p * nodes, (p + 1) * nodes)
            own = own_ref[0, a, rows, :].astype(jnp.float32)
            out_ref[a, rows, :] = 0.5 * own + near[a * nodes : (a + 1) * nodes, :]


def spread(full_ref, outs, own):
    rows = outs[0].shape[1]
    for k in range(len(outs) * outs[0].shape[0]):
        first = pl.multiple_of((own ^ k) * rows, 8)
        outs[k % len(outs)][k // len(outs)] = full_ref[pl.ds(first, rows), :]


def collect(order, parts, full_ref, own, start):
    rows = full_ref.shape[0] // len(order)
    for k, offset in enumerate(order):
        first = pl.multiple_of((own ^ offset) * rows, 8)
        ref, row = part_at(parts, k)
        full_ref[pl.ds(first, rows), :] = ref[row, start : start + rows, :]


def stacked(basis_ref):
    return jnp.concatenate(
        [
            jnp.concatenate([basis_ref[j, a] for j in range(basis_ref.shape[0])], axis=1)
            for a in range(2)
        ],
        axis=0,
    )


def project_kernel(masks, ways, index_ref, half_hbm, weight_ref, basis_ref, base_ref, *refs):
    arrived = refs[: len(refs) - ways - 2]
    image_ref = refs[len(arrived)]
    outs = refs[len(arrived) + 1 : -1]
    full_ref = refs[-1]
    weighted = []
    for a in range(2):
        image = base_ref[a] + total_of([part[0, a] for part in arrived])
        image_ref[a] = image
        weighted.append(image * weight_ref[...])
    image = jnp.concatenate([image_ref[0], image_ref[1]], axis=0)
    left = jnp.concatenate([stacked(basis_ref), image], axis=1)
    full_ref[...] = dot_first(left, jnp.concatenate(weighted, axis=0))
    spread(full_ref, outs, bits_of(index_ref[2], masks))


def factor_kernel(gather, masks, index_ref, basis_ref, image_ref, *refs):
    parts = refs[:-7]
    hess_ref, upper_ref, new_ref, full_ref, half_ref, work_ref, inverse_ref = refs[-7:]
    block_total, _, _, order = basis_ref.shape
    hess_rows = block_total * order
    tile = (ROWS, order)
    lane = lax.broadcasted_iota(jnp.int32, tile, 1)
    row = lax.broadcasted_iota(jnp.int32, tile, 0)
    own = bits_of(index_ref[2], masks)
    collect(gather, parts, full_ref, own, 0)
    collect(gather, parts, half_ref, own, full_ref.shape[0] // len(gather))
    hessenberg = full_ref[:hess_rows, :]
    hess_ref[...] = hessenberg
    rows = []
    number = 0
    for i in range(block_total):
        count = block_total - i
        left = jnp.concatenate(
            [
                half_ref[(number + j) * order : (number + j + 1) * order, :]
                for j in range(count)
            ],
            axis=1,
        )
        rows.append(dot_rows(left, full_ref[i * order : hess_rows, :]))
        number += count
    product = dot_first(hessenberg, jnp.concatenate(rows, axis=0) - hessenberg)
    work_ref[...] = full_ref[hess_rows:, :] + (product + jnp.transpose(product))
    for block in range(order // ROWS):
        start = block * ROWS
        inverse_ref[start : start + ROWS, :] = jnp.where(lane == row + start, 1.0, 0.0)
    for block in range(order // ROWS):
        start = block * ROWS
        own = work_ref[start : start + ROWS, :]
        own_inverse = inverse_ref[start : start + ROWS, :]
        columns = [
            jnp.broadcast_to(own[:, start + m : start + m + 1], tile) for m in range(ROWS)
        ]
        entry = {
            (j, m): jnp.broadcast_to(columns[m][j : j + 1, :], tile)
            for m in range(ROWS)
            for j in range(m, ROWS)
        }
        scale = []
        for m in range(ROWS):
            scale.append(lax.rsqrt(entry[m, m]))
            for j in range(m + 1, ROWS):
                entry[j, m] = entry[j, m] * scale[m]
            for n in range(m + 1, ROWS):
                for j in range(n, ROWS):
                    entry[j, n] = entry[j, n] - entry[j, m] * entry[n, m]
        solved = []
        solved_inverse = []
        for m in range(ROWS):
            upper_row = jnp.broadcast_to(own[m : m + 1, :], tile)
            inverse_row = jnp.broadcast_to(own_inverse[m : m + 1, :], tile)
            for j in range(m):
                upper_row = upper_row - entry[m, j] * solved[j]
                inverse_row = inverse_row - entry[m, j] * solved_inverse[j]
            upper_row = upper_row * scale[m]
            inverse_row = inverse_row * scale[m]
            solved.append(upper_row)
            solved_inverse.append(inverse_row)
        upper_rows = solved[ROWS - 1]
        inverse_rows = solved_inverse[ROWS - 1]
        for m in range(ROWS - 1):
            upper_rows = jnp.where(row == m, solved[m], upper_rows)
            inverse_rows = jnp.where(row == m, solved_inverse[m], inverse_rows)
        upper_ref[start : start + ROWS, :] = jnp.where(lane >= row + start, upper_rows, 0.0)
        inverse_ref[start : start + ROWS, :] = inverse_rows
        if block + 1 < order // ROWS:
            first = start + ROWS
            target = work_ref[first : first + ROWS, :]
            target_inverse = inverse_ref[first : first + ROWS, :]
            multiplier = []
            for m in range(ROWS):
                value = jnp.broadcast_to(target[:, start + m : start + m + 1], tile)
                for j in range(m):
                    value = value - multiplier[j] * entry[m, j]
                multiplier.append(value * scale[m])
            for m in range(ROWS):
                target = target - multiplier[m] * solved[m]
                target_inverse = target_inverse - multiplier[m] * solved_inverse[m]
            work_ref[first : first + ROWS, :] = target
            inverse_ref[first : first + ROWS, :] = target_inverse
        if block + 2 < order // ROWS:
            twice = [None] * ROWS
            twice_inverse = [None] * ROWS
            for m in reversed(range(ROWS)):
                upper_row = solved[m]
                inverse_row = solved_inverse[m]
                for j in range(m + 1, ROWS):
                    upper_row = upper_row - entry[j, m] * twice[j]
                    inverse_row = inverse_row - entry[j, m] * twice_inverse[j]
                twice[m] = upper_row * scale[m]
                twice_inverse[m] = inverse_row * scale[m]
        for later in range(block + 2, order // ROWS):
            first = later * ROWS
            target = work_ref[first : first + ROWS, :]
            target_inverse = inverse_ref[first : first + ROWS, :]
            values = [
                jnp.broadcast_to(target[:, start + m : start + m + 1], tile) for m in range(ROWS)
            ]
            target = target - total_of([values[m] * twice[m] for m in range(ROWS)])
            target_inverse = target_inverse - total_of(
                [values[m] * twice_inverse[m] for m in range(ROWS)]
            )
            work_ref[first : first + ROWS, :] = target
            inverse_ref[first : first + ROWS, :] = target_inverse
    image = jnp.concatenate([image_ref[0], image_ref[1]], axis=0)
    remainder = image - dot_rows(stacked(basis_ref), hessenberg)
    new_ref[...] = dot_rows(remainder, inverse_ref[...], ((1,), (1,)))


def f32(*shape):
    return jax.ShapeDtypeStruct(shape, jnp.float32)


def b16(*shape):
    return jax.ShapeDtypeStruct(shape, jnp.bfloat16)


def call(kernel, out_shape, operands, scalars=0, scratch=(), in_hbm=0):
    many = isinstance(out_shape, (tuple, list))
    free = len(operands) - in_hbm
    operands = list(operands[:free]) + [
        pltpu.with_memory_space_constraint(x, pltpu.HBM) for x in operands[free:]
    ]
    return pl.pallas_call(
        kernel,
        out_shape=out_shape,
        in_specs=[SMEM] * scalars + [ANY if in_hbm else VMEM] * (len(operands) - scalars),
        out_specs=[VMEM] * len(out_shape) if many else VMEM,
        scratch_shapes=list(scratch),
        compiler_params=PARAMS,
    )(*operands)


def body(
    points,
    quad_weight,
    basis,
    jacobi,
    near_panel,
    near_count,
    near_block,
    agg_index,
    coarse_inverse,
):
    block_total, _, point_count, rhs_count = basis.shape
    coarse_count = coarse_inverse.shape[1]
    narrow_count = lax.axis_size("narrow")
    wide_count = lax.axis_size("wide")
    panels_dev, slot_total = near_panel.shape
    nodes = near_block.shape[2] // 2
    width = SPAN * nodes
    pack_rows = coarse_count + EXTRA
    index = jnp.stack(
        [lax.axis_index("narrow"), lax.axis_index("wide"), lax.axis_index(AXES)]
    ).astype(jnp.int32)
    weight_row = quad_weight[None, :]
    low, *high = masks_of(wide_count)
    core, *across = masks_of(narrow_count, wide_count)
    high_groups = in_pairs(high)
    plane_groups = in_pairs([low] + across)
    wide_groups = high_groups + [[low]]
    narrow_groups = [[core]] + in_pairs(across)
    source_groups = high_groups + [[core]]
    high_count = 1 << len(high)
    source_total = 2 * high_count * point_count
    target_count = narrow_count
    pair_row = pltpu.VMEM((2, point_count), jnp.float32)
    one_row = pltpu.VMEM((1, point_count), jnp.float32)
    pair_index = pltpu.VMEM((2, point_count), jnp.int32)
    field = pltpu.VMEM((2, point_count, rhs_count), jnp.float32)

    pack = call(
        restrict_kernel,
        f32(1, pack_rows, point_count),
        (agg_index, basis, points, weight_row),
        0,
        [pair_index, field, pair_row, one_row, pltpu.SemaphoreType.DMA((4,))],
        4,
    )
    half_rows = block_total * (block_total + 1) // 2 * rhs_count
    halving = [[core]] + plane_groups
    masks = [core, low] + across
    inverse, member, smooth, weight, *half_parts = call(
        functools.partial(prefetch_kernel, masks),
        [
            f32(*coarse_inverse.shape),
            f32(2, coarse_count, point_count),
            f32(2, point_count, rhs_count),
            f32(point_count, rhs_count),
        ]
        + [f32(narrow_count, half_rows // (2 * narrow_count), rhs_count)] * 2,
        (index, pack, agg_index, basis, jacobi, weight_row, coarse_inverse),
        1,
        [
            pltpu.VMEM((half_rows, rhs_count), jnp.float32),
            pair_index,
            pltpu.VMEM(basis.shape, jnp.float32),
            pair_row,
            one_row,
            pltpu.SemaphoreType.DMA((5,)),
        ],
        5,
    )
    half_parts = sum_parts(flip_each(half_parts, [core]), 2)
    half_steps = []
    for number, mask in enumerate([low] + across + high):
        got = flip_each(half_parts, [mask])
        half_steps.append(got[1])
        half_parts = sum_parts(got, 2 if number < len(across) else 1)
        if len(half_parts) == 1:
            half_parts = half_parts * 2
    half_total = half_parts[0]
    near_rows = jnp.transpose(near_block, (0, 2, 1, 3)).reshape(
        panels_dev, 2 * nodes, slot_total * 2 * nodes
    )
    packs = gather_steps(pack, wide_groups, (weight,))
    source_rows = high_count * EXTRA // (narrow_count // 2)
    target_rows = 2 * EXTRA
    coarse_outs = pl.pallas_call(
        functools.partial(
            coarse_kernel, gather_order(wide_groups), 2, high_count
        ),
        out_shape=[f32(narrow_count // 2, coarse_count + source_rows, rhs_count)] * 2
        + [f32(high_count, EXTRA, point_count), f32(2, EXTRA, point_count)],
        in_specs=[SMEM, ANY, VMEM] + [VMEM] * len(packs),
        out_specs=[VMEM] * 4,
        scratch_shapes=[pltpu.VMEM((wide_count * coarse_count, rhs_count), jnp.float32)],
        compiler_params=PARAMS,
    )(index, near_rows, inverse, *packs)
    own_sources = coarse_outs[2]
    kept, got = flip_each(coarse_outs[:2], [core])
    groups = in_pairs(across)
    ways = 1 << len(groups[0])
    *coarse_parts, other_sources = call(
        functools.partial(coarse_sum_kernel, ways),
        [f32(narrow_count // 2 // ways, coarse_count + target_rows, rhs_count)] * ways
        + [f32(high_count, EXTRA, point_count)],
        (kept, got, coarse_outs[3]),
    )
    coarse_parts = scatter_steps(coarse_parts, groups)
    precond, pair_edge, next_edge = call(
        precond_kernel,
        [b16(1, 2, point_count, rhs_count)] + [b16(2, width, rhs_count)] * 2,
        (index, member, smooth, *coarse_parts),
        1,
    )
    matrix_spec = pl.BlockSpec((1, 3, point_count, source_total), lambda k: (k, 0, 0, 0))
    matrix = pl.pallas_call(
        functools.partial(matrix_kernel, coarse_count),
        out_shape=b16(target_count, 3, point_count, source_total),
        grid=(target_count,),
        in_specs=[VMEM] * (2 + len(coarse_parts)),
        out_specs=matrix_spec,
        compiler_params=PARAMS,
    )(own_sources, other_sources, *coarse_parts)
    fields = flip_each([precond] * (1 << len(source_groups[0])), source_groups[0])
    fields = gather_steps(join(fields, (matrix, half_steps[0])), source_groups[1:])
    device_count = narrow_count * wide_count
    pair_edge = flip(pair_edge, 1)
    pairs = [(i, i + 1) for i in range(1, device_count - 1, 2)]
    next_edge = lax.ppermute(next_edge, AXES, pairs + [(j, i) for i, j in pairs])

    after = (pair_edge, next_edge, half_steps[1])
    ways = 1 << len(plane_groups[0])
    far_parts = pl.pallas_call(
        functools.partial(far_kernel, ways, len(after)),
        out_shape=[f32(target_count // ways, 2, point_count, rhs_count)] * ways,
        grid=(target_count,),
        in_specs=[ANY] * len(after) + [matrix_spec] + [VMEM] * len(fields),
        out_specs=[VMEM] * ways,
        scratch_shapes=[pltpu.VMEM((source_total, 2 * rhs_count), jnp.bfloat16)],
        compiler_params=PARAMS,
    )(*after, matrix, *fields)
    far_parts = scatter_steps(far_parts, plane_groups)
    base = call(
        near_kernel,
        f32(2, point_count, rhs_count),
        (index, near_panel, near_count, near_rows, precond, pair_edge, next_edge),
        3,
        [
            pltpu.VMEM((2, 2 * width + point_count, rhs_count), jnp.bfloat16),
            pltpu.VMEM((panels_dev, slot_total * 2 * nodes, rhs_count), jnp.bfloat16),
        ],
    )

    hess_rows = block_total * rhs_count
    sum_rows = hess_rows + rhs_count
    image, *parts = pl.pallas_call(
        functools.partial(project_kernel, masks, 2),
        out_shape=[f32(2, point_count, rhs_count)]
        + [f32(narrow_count, sum_rows // (2 * narrow_count), rhs_count)] * 2,
        in_specs=[SMEM] + [ANY] + [VMEM] * (3 + len(far_parts)),
        out_specs=[VMEM] * 3,
        scratch_shapes=[pltpu.VMEM((sum_rows, rhs_count), jnp.float32)],
        compiler_params=PARAMS,
    )(index, half_steps[2], weight, basis, base, *far_parts)
    (total,) = sum_parts(scatter_steps(parts, halving), 1, half_steps[3:4])
    total = sum_butterfly(total, high_groups)
    parts = gather_steps(append(total, half_total), halving[::-1])
    hessenberg, upper_factor, new_block = call(
        functools.partial(factor_kernel, gather_order(part_groups(halving)[::-1]), masks),
        [
            f32(hess_rows, rhs_count),
            f32(rhs_count, rhs_count),
            f32(2 * point_count, rhs_count),
        ],
        (index, basis, image, *parts),
        1,
        [
            pltpu.VMEM((sum_rows, rhs_count), jnp.float32),
            pltpu.VMEM((half_rows, rhs_count), jnp.float32),
        ]
        + [pltpu.VMEM((rhs_count, rhs_count), jnp.float32)] * 2,
    )
    return (
        new_block.reshape(2, point_count, rhs_count),
        hessenberg.reshape(block_total, rhs_count, rhs_count),
        upper_factor,
    )


def solution(mesh):
    in_specs = (
        P(None, ("narrow", "wide")),
        P(("narrow", "wide")),
        P(None, None, ("narrow", "wide"), None),
        P(None, ("narrow", "wide")),
        P(("narrow", "wide"), None),
        P(("narrow", "wide")),
        P(("narrow", "wide"), None, None, None),
        P(None, ("narrow", "wide")),
        P(None, "wide", "narrow"),
    )
    out_specs = (P(None, ("narrow", "wide"), None), P(), P())
    return jax.shard_map(body, mesh=mesh, in_specs=in_specs, out_specs=out_specs, check_vma=False)
```

```python
import functools

import jax
import jax.numpy as jnp
from jax import lax
from jax.experimental import pallas as pl
from jax.experimental.pallas import tpu as pltpu
from jax.sharding import PartitionSpec as P

SPAN = 4


NU = 0.3
DELTA2 = 1e-05
ELASTIC = 40.0
AXES = ("narrow", "wide")
EXTRA = 8
ROWS = 8
SMEM = pl.BlockSpec(memory_space=pltpu.SMEM)
VMEM = pl.BlockSpec(memory_space=pltpu.VMEM)
ANY = pl.BlockSpec(memory_space=pl.ANY)
PARAMS = pltpu.CompilerParams(vmem_limit_bytes=48 * 1024 * 1024)


def split(value):
    high = value.astype(jnp.bfloat16)
    return high, (value - high.astype(jnp.float32)).astype(jnp.bfloat16)


def dot16(left, right, contract=((1,), (0,))):
    return lax.dot_general(left, right, (contract, ((), ())), preferred_element_type=jnp.float32)


def dot_rows(left, right, contract=((1,), (0,))):
    left_high, left_low = split(left)
    right_high, right_low = split(right)
    return dot16(left_high, right_high, contract) + (
        dot16(left_high, right_low, contract) + dot16(left_low, right_high, contract)
    )


def dot_first(left, right):
    return dot_rows(left, right, ((0,), (0,)))


def pick(member, value, contract=((1,), (0,))):
    member = member.astype(jnp.bfloat16)
    high, low = split(value)
    lowest = (value - high.astype(jnp.float32) - low.astype(jnp.float32)).astype(jnp.bfloat16)
    return dot16(member, high, contract) + (
        dot16(member, low, contract) + dot16(member, lowest, contract)
    )


def as_column(row, width):
    return jnp.transpose(jnp.broadcast_to(row, (width, row.shape[1])))


def flip(block, mask):
    count = lax.axis_size(AXES)
    return lax.ppermute(block, AXES, [(i, i ^ mask) for i in range(count)])


def masks_of(count, scale=1):
    return [scale << bit for bit in range(count.bit_length() - 1)]


def in_pairs(masks):
    return [masks[k : k + 2] for k in range(0, len(masks), 2)]


def combined(group, number):
    mask = 0
    for bit, part in enumerate(group):
        if number >> bit & 1:
            mask ^= part
    return mask


def flip_each(parts, group):
    return [parts[0]] + [flip(parts[j], combined(group, j)) for j in range(1, 1 << len(group))]


def join_kernel(count, *refs):
    parts, out_ref = refs[-1 - count : -1], refs[-1]
    size = parts[0].shape[0]
    for j, ref in enumerate(parts):
        out_ref[j * size : (j + 1) * size] = ref[...]


def join(parts, after=()):
    shape = (len(parts) * parts[0].shape[0],) + parts[0].shape[1:]
    return pl.pallas_call(
        functools.partial(join_kernel, len(parts)),
        out_shape=jax.ShapeDtypeStruct(shape, parts[0].dtype),
        in_specs=[ANY] * len(after) + [VMEM] * len(parts),
        out_specs=VMEM,
        compiler_params=PARAMS,
    )(*after, *parts)


def gather_steps(held, groups, after=()):
    parts = [held]
    for group in groups:
        if len(parts) > 1:
            held = join(parts, after)
            after = ()
        parts = flip_each([held] * (1 << len(group)), group)
    return parts


def gather_order(groups):
    order = [0]
    for group in groups:
        order = [k ^ combined(group, j) for j in range(1 << len(group)) for k in order]
    return order


def total_of(values):
    while len(values) > 1:
        values = [values[k] + values[k + 1] for k in range(0, len(values), 2)]
    return values[0]


def sum_kernel(count, skip, *refs):
    parts, outs = refs[skip : skip + count], refs[skip + count :]
    for k in range(outs[0].shape[0]):
        for j, out_ref in enumerate(outs):
            out_ref[k] = total_of([part[k * len(outs) + j] for part in parts])


def sum_parts(parts, ways, after=()):
    out = f32(parts[0].shape[0] // ways, *parts[0].shape[1:])
    return pl.pallas_call(
        functools.partial(sum_kernel, len(parts), len(after)),
        out_shape=[out] * ways,
        in_specs=[ANY] * len(after) + [VMEM] * len(parts),
        out_specs=[VMEM] * ways,
        compiler_params=PARAMS,
    )(*after, *parts)


def scatter_steps(parts, groups):
    for number, group in enumerate(groups):
        if number:
            parts = sum_parts(parts, 1 << len(group))
        parts = flip_each(parts, group)
    return parts


def sum_butterfly(total, groups):
    for group in groups:
        (total,) = sum_parts(flip_each([total] * (1 << len(group)), group), 1)
    return total


def append_kernel(left_ref, right_ref, out_ref):
    rows = left_ref.shape[1]
    out_ref[:, :rows, :] = left_ref[...]
    out_ref[:, rows:, :] = right_ref[...]


def append(left, right):
    count, rows, width = left.shape
    shape = f32(count, rows + right.shape[1], width)
    return call(append_kernel, shape, (left, right))


def part_groups(groups):
    bit, found = 0, []
    for group in groups:
        found.append([1 << (bit + k) for k in range(len(group))])
        bit += len(group)
    return found


def bits_of(index, masks):
    packed = 0
    for bit, mask in enumerate(masks):
        packed = packed + (lax.shift_right_logical(index, mask.bit_length() - 1) & 1) * (1 << bit)
    return packed


def members(agg_ref, a, coarse_count):
    ids = lax.broadcasted_iota(jnp.int32, (coarse_count, agg_ref.shape[1]), 0)
    return jnp.where(ids == agg_ref[a : a + 1, :], 1.0, 0.0)


def load_all(pairs, sems):
    copies = [
        pltpu.make_async_copy(source, target, sems.at[k])
        for k, (source, target) in enumerate(pairs)
    ]
    for copy in copies:
        copy.start()
    for copy in copies:
        copy.wait()


def restrict_kernel(
    agg_hbm, basis_hbm, points_hbm, weight_hbm, pack_ref, agg_ref, newest_ref, points_ref, weight_ref, sems
):
    coarse_count = pack_ref.shape[1] - EXTRA
    point_count = newest_ref.shape[1]
    load_all(
        [
            (basis_hbm.at[basis_hbm.shape[0] - 1], newest_ref),
            (agg_hbm, agg_ref),
            (points_hbm, points_ref),
            (weight_hbm, weight_ref),
        ],
        sems,
    )
    total = pick(members(agg_ref, 0, coarse_count), newest_ref[0]) + pick(
        members(agg_ref, 1, coarse_count), newest_ref[1]
    )
    pack_ref[0, :coarse_count, :] = total
    pack_ref[0, coarse_count:, :] = jnp.concatenate(
        [points_ref[...], weight_ref[...], jnp.zeros((EXTRA - 3, point_count), jnp.float32)], axis=0
    )


def prefetch_kernel(
    masks,
    index_ref,
    pack_hbm,
    agg_hbm,
    basis_hbm,
    jacobi_hbm,
    weight_hbm,
    inverse_hbm,
    inverse_ref,
    member_ref,
    smooth_ref,
    weight_out_ref,
    keep_ref,
    send_ref,
    half_ref,
    agg_ref,
    basis_ref,
    jacobi_ref,
    weight_ref,
    sems,
):
    coarse_count = member_ref.shape[1]
    block_total, _, _, rhs_count = basis_ref.shape
    load_all(
        [
            (basis_hbm, basis_ref),
            (agg_hbm, agg_ref),
            (jacobi_hbm, jacobi_ref),
            (weight_hbm, weight_ref),
            (inverse_hbm, inverse_ref),
        ],
        sems,
    )
    for a in range(2):
        member_ref[a] = members(agg_ref, a, coarse_count)
        smooth_ref[a] = (
            as_column(jacobi_ref[a : a + 1, :], rhs_count) * basis_ref[block_total - 1, a]
        )
    weight = as_column(weight_ref[...], rhs_count)
    weight_out_ref[...] = weight
    right = stacked(basis_ref)
    number = 0
    for i in range(block_total):
        left = jnp.concatenate([basis_ref[i, a] * weight for a in range(2)], axis=0)
        row = dot_first(left, right[:, i * rhs_count :])
        for j in range(i, block_total):
            block = row[:, (j - i) * rhs_count : (j - i + 1) * rhs_count]
            rows = slice(number * rhs_count, (number + 1) * rhs_count)
            half_ref[rows, :] = block * 0.5 if i == j else block
            number += 1
    spread(half_ref, (keep_ref, send_ref), bits_of(index_ref[2], masks))


def part_at(parts, k):
    size = parts[0].shape[0]
    return parts[k // size], k % size


def coarse_kernel(order, ways, z_count, index_ref, near_ref, inverse_ref, *refs):
    narrow_count, coarse_count, _ = inverse_ref.shape
    packs = refs[: len(refs) - ways - 3]
    outs = refs[len(packs) : len(packs) + ways]
    source_ref, target_ref, rhs_ref = refs[len(packs) + ways :]
    for k, offset in enumerate(order):
        first = pl.multiple_of((index_ref[1] ^ offset) * coarse_count, 8)
        ref, row = part_at(packs, k)
        rhs_ref[pl.ds(first, coarse_count), :] = ref[row, :coarse_count, :]
    for k in range(z_count):
        ref, row = part_at(packs, k)
        source_ref[k] = ref[row, coarse_count:, :]
    for k in range(target_ref.shape[0]):
        ref, row = part_at(packs, k * z_count)
        target_ref[k] = ref[row, coarse_count:, :]
    left = jnp.concatenate(
        [inverse_ref[index_ref[0] ^ k] for k in range(narrow_count)], axis=0
    )
    product = dot_rows(left, rhs_ref[...])
    tail = jnp.concatenate([source_ref[k] for k in range(z_count)], axis=0)
    each = z_count * EXTRA // (narrow_count // ways)
    for k in range(narrow_count):
        part = product[k * coarse_count : (k + 1) * coarse_count, :]
        outs[k % ways][k // ways, :coarse_count, :] = part
        first = (k // ways) * each
        outs[k % ways][k // ways, coarse_count:, :] = tail[first : first + each, :]


def coarse_sum_kernel(ways, kept_ref, got_ref, target_ref, *refs):
    outs, source_ref = refs[:ways], refs[ways]
    rows = target_ref.shape[0] * EXTRA
    coarse_count = outs[0].shape[1] - rows
    each = (kept_ref.shape[1] - coarse_count) // EXTRA
    for k in range(kept_ref.shape[0]):
        for j in range(each):
            first = coarse_count + j * EXTRA
            source_ref[k * each + j] = got_ref[k, first : first + EXTRA, :]
    for k in range(outs[0].shape[0]):
        for j in range(ways):
            source = k * ways + j
            outs[j][k, :coarse_count, :] = (
                kept_ref[source, :coarse_count, :] + got_ref[source, :coarse_count, :]
            )
            for t in range(target_ref.shape[0]):
                first = coarse_count + t * EXTRA
                outs[j][k, first : first + EXTRA, :] = target_ref[t]


def precond_kernel(index_ref, member_ref, smooth_ref, *refs):
    parts = refs[:-3]
    precond_ref, pair_ref, next_ref = refs[-3:]
    coarse_count = member_ref.shape[1]
    point_count = smooth_ref.shape[1]
    width = pair_ref.shape[1]
    even = (index_ref[2] & 1) == 0
    coarse_sol = total_of([part[0, :coarse_count, :] for part in parts])
    for a in range(2):
        value = smooth_ref[a] + pick(member_ref[a], coarse_sol, ((0,), (0,)))
        precond_ref[0, a] = value.astype(jnp.bfloat16)
        first = value[:width]
        last = value[point_count - width :]
        pair_ref[a] = jnp.where(even, last, first).astype(jnp.bfloat16)
        next_ref[a] = jnp.where(even, first, last).astype(jnp.bfloat16)


def matrix_kernel(coarse_count, own_ref, other_ref, *refs):
    targets, matrix_ref = refs[:-1], refs[-1]
    point_count = own_ref.shape[2]
    size = (targets[0].shape[1] - coarse_count) // EXTRA
    step = pl.program_id(0)
    first = pl.multiple_of(coarse_count + lax.rem(step, size) * EXTRA, EXTRA)
    target = targets[0][0, pl.ds(first, EXTRA), :]
    for j in range(1, len(targets)):
        target = jnp.where(step // size == j, targets[j][0, pl.ds(first, EXTRA), :], target)
    target_x = as_column(target[0:1, :], point_count)
    target_y = as_column(target[1:2, :], point_count)
    for s in range(matrix_ref.shape[3] // point_count):
        ref, row = part_at((own_ref, other_ref), s)
        source = ref[row]
        delta_x = target_x - source[0:1, :]
        delta_y = target_y - source[1:2, :]
        factor = ELASTIC * source[2:3, :]
        square_x = delta_x * delta_x
        square_y = delta_y * delta_y
        square_dist = square_x + square_y + DELTA2
        inverse = 1.0 / square_dist
        log_part = (-0.5 * (3.0 - 4.0 * NU)) * jnp.log(square_dist)
        lanes = slice(s * point_count, (s + 1) * point_count)
        matrix_ref[0, 0, :, lanes] = (factor * (log_part + square_x * inverse)).astype(jnp.bfloat16)
        matrix_ref[0, 1, :, lanes] = (factor * (delta_x * delta_y * inverse)).astype(jnp.bfloat16)
        matrix_ref[0, 2, :, lanes] = (factor * (log_part + square_y * inverse)).astype(jnp.bfloat16)


def far_kernel(ways, skip, *refs):
    matrix_ref, *refs = refs[skip:]
    fields = refs[: len(refs) - ways - 1]
    outs = refs[len(fields) : len(fields) + ways]
    fields_ref = refs[-1]
    point_count, rhs_count = fields[0].shape[2:]
    step = pl.program_id(0)

    @pl.when(step == 0)
    def _():
        for s in range(fields_ref.shape[0] // point_count):
            ref, row = part_at(fields, s)
            for b in range(2):
                rows = slice(s * point_count, (s + 1) * point_count)
                fields_ref[rows, b * rhs_count : (b + 1) * rhs_count] = ref[row, b]

    mixed = dot16(matrix_ref[0, 1], fields_ref[...])
    out_x = dot16(matrix_ref[0, 0], fields_ref[:, :rhs_count]) + mixed[:, rhs_count:]
    out_y = dot16(matrix_ref[0, 2], fields_ref[:, rhs_count:]) + mixed[:, :rhs_count]
    for j, out_ref in enumerate(outs):

        @pl.when(lax.rem(step, ways) == j)
        def _(out_ref=out_ref):
            out_ref[step // ways, 0] = out_x
            out_ref[step // ways, 1] = out_y


def near_kernel(
    index_ref,
    panel_ref,
    count_ref,
    block_ref,
    own_ref,
    pair_ref,
    next_ref,
    out_ref,
    line_ref,
    gathered_ref,
):
    point_count = own_ref.shape[2]
    width = pair_ref.shape[1]
    even = (index_ref[2] & 1) == 0
    panels_dev, double_nodes, _ = block_ref.shape
    nodes = double_nodes // 2
    slot_total = panel_ref.shape[1]
    for b in range(2):
        pair = pair_ref[b].astype(jnp.float32)
        following = next_ref[b].astype(jnp.float32)
        line_ref[b, :width, :] = jnp.where(even, following, pair).astype(jnp.bfloat16)
        line_ref[b, width : width + point_count, :] = own_ref[0, b]
        line_ref[b, width + point_count :, :] = jnp.where(even, pair, following).astype(
            jnp.bfloat16
        )
    first_panel = index_ref[2] * panels_dev
    lane = lax.broadcasted_iota(jnp.int32, block_ref.shape[1:], 1)
    for p in range(panels_dev):
        for k in range(slot_total):
            first = pl.multiple_of((panel_ref[p, k] - first_panel) * nodes + width, 16)
            for b in range(2):
                row = (k * 2 + b) * nodes
                gathered_ref[p, row : row + nodes, :] = line_ref[b, pl.ds(first, nodes), :]
        blocks = jnp.where(
            lane < count_ref[p] * double_nodes, block_ref[p].astype(jnp.float32), 0.0
        ).astype(jnp.bfloat16)
        near = dot16(blocks, gathered_ref[p])
        for a in range(2):
            rows = slice(p * nodes, (p + 1) * nodes)
            own = own_ref[0, a, rows, :].astype(jnp.float32)
            out_ref[a, rows, :] = 0.5 * own + near[a * nodes : (a + 1) * nodes, :]


def spread(full_ref, outs, own):
    rows = outs[0].shape[1]
    for k in range(len(outs) * outs[0].shape[0]):
        first = pl.multiple_of((own ^ k) * rows, 8)
        outs[k % len(outs)][k // len(outs)] = full_ref[pl.ds(first, rows), :]


def collect(order, parts, full_ref, own, start):
    rows = full_ref.shape[0] // len(order)
    for k, offset in enumerate(order):
        first = pl.multiple_of((own ^ offset) * rows, 8)
        ref, row = part_at(parts, k)
        full_ref[pl.ds(first, rows), :] = ref[row, start : start + rows, :]


def stacked(basis_ref):
    return jnp.concatenate(
        [
            jnp.concatenate([basis_ref[j, a] for j in range(basis_ref.shape[0])], axis=1)
            for a in range(2)
        ],
        axis=0,
    )


def project_kernel(masks, ways, index_ref, half_hbm, weight_ref, basis_ref, base_ref, *refs):
    arrived = refs[: len(refs) - ways - 2]
    image_ref = refs[len(arrived)]
    outs = refs[len(arrived) + 1 : -1]
    full_ref = refs[-1]
    weighted = []
    for a in range(2):
        image = base_ref[a] + total_of([part[0, a] for part in arrived])
        image_ref[a] = image
        weighted.append(image * weight_ref[...])
    image = jnp.concatenate([image_ref[0], image_ref[1]], axis=0)
    left = jnp.concatenate([stacked(basis_ref), image], axis=1)
    full_ref[...] = dot_first(left, jnp.concatenate(weighted, axis=0))
    spread(full_ref, outs, bits_of(index_ref[2], masks))


def factor_kernel(gather, masks, index_ref, basis_ref, image_ref, *refs):
    parts = refs[:-7]
    hess_ref, upper_ref, new_ref, full_ref, half_ref, work_ref, inverse_ref = refs[-7:]
    block_total, _, _, order = basis_ref.shape
    hess_rows = block_total * order
    tile = (ROWS, order)
    lane = lax.broadcasted_iota(jnp.int32, tile, 1)
    row = lax.broadcasted_iota(jnp.int32, tile, 0)
    own = bits_of(index_ref[2], masks)
    collect(gather, parts, full_ref, own, 0)
    collect(gather, parts, half_ref, own, full_ref.shape[0] // len(gather))
    hessenberg = full_ref[:hess_rows, :]
    hess_ref[...] = hessenberg
    rows = []
    number = 0
    for i in range(block_total):
        count = block_total - i
        left = jnp.concatenate(
            [
                half_ref[(number + j) * order : (number + j + 1) * order, :]
                for j in range(count)
            ],
            axis=1,
        )
        rows.append(dot_rows(left, full_ref[i * order : hess_rows, :]))
        number += count
    product = dot_first(hessenberg, jnp.concatenate(rows, axis=0) - hessenberg)
    work_ref[...] = full_ref[hess_rows:, :] + (product + jnp.transpose(product))
    for block in range(order // ROWS):
        start = block * ROWS
        inverse_ref[start : start + ROWS, :] = jnp.where(lane == row + start, 1.0, 0.0)
    for block in range(order // ROWS):
        start = block * ROWS
        own = work_ref[start : start + ROWS, :]
        own_inverse = inverse_ref[start : start + ROWS, :]
        columns = [
            jnp.broadcast_to(own[:, start + m : start + m + 1], tile) for m in range(ROWS)
        ]
        entry = {
            (j, m): jnp.broadcast_to(columns[m][j : j + 1, :], tile)
            for m in range(ROWS)
            for j in range(m, ROWS)
        }
        scale = []
        for m in range(ROWS):
            scale.append(lax.rsqrt(entry[m, m]))
            for j in range(m + 1, ROWS):
                entry[j, m] = entry[j, m] * scale[m]
            for n in range(m + 1, ROWS):
                for j in range(n, ROWS):
                    entry[j, n] = entry[j, n] - entry[j, m] * entry[n, m]
        solved = []
        solved_inverse = []
        for m in range(ROWS):
            upper_row = jnp.broadcast_to(own[m : m + 1, :], tile)
            inverse_row = jnp.broadcast_to(own_inverse[m : m + 1, :], tile)
            for j in range(m):
                upper_row = upper_row - entry[m, j] * solved[j]
                inverse_row = inverse_row - entry[m, j] * solved_inverse[j]
            upper_row = upper_row * scale[m]
            inverse_row = inverse_row * scale[m]
            solved.append(upper_row)
            solved_inverse.append(inverse_row)
        upper_rows = solved[ROWS - 1]
        inverse_rows = solved_inverse[ROWS - 1]
        for m in range(ROWS - 1):
            upper_rows = jnp.where(row == m, solved[m], upper_rows)
            inverse_rows = jnp.where(row == m, solved_inverse[m], inverse_rows)
        upper_ref[start : start + ROWS, :] = jnp.where(lane >= row + start, upper_rows, 0.0)
        inverse_ref[start : start + ROWS, :] = inverse_rows
        for later in range(block + 1, order // ROWS):
            first = later * ROWS
            target = work_ref[first : first + ROWS, :]
            target_inverse = inverse_ref[first : first + ROWS, :]
            multiplier = []
            for m in range(ROWS):
                value = jnp.broadcast_to(target[:, start + m : start + m + 1], tile)
                for j in range(m):
                    value = value - multiplier[j] * entry[m, j]
                multiplier.append(value * scale[m])
            for m in range(ROWS):
                target = target - multiplier[m] * solved[m]
                target_inverse = target_inverse - multiplier[m] * solved_inverse[m]
            work_ref[first : first + ROWS, :] = target
            inverse_ref[first : first + ROWS, :] = target_inverse
    image = jnp.concatenate([image_ref[0], image_ref[1]], axis=0)
    remainder = image - dot_rows(stacked(basis_ref), hessenberg)
    new_ref[...] = dot_rows(remainder, inverse_ref[...], ((1,), (1,)))


def f32(*shape):
    return jax.ShapeDtypeStruct(shape, jnp.float32)


def b16(*shape):
    return jax.ShapeDtypeStruct(shape, jnp.bfloat16)


def call(kernel, out_shape, operands, scalars=0, scratch=(), in_hbm=0):
    many = isinstance(out_shape, (tuple, list))
    free = len(operands) - in_hbm
    operands = list(operands[:free]) + [
        pltpu.with_memory_space_constraint(x, pltpu.HBM) for x in operands[free:]
    ]
    return pl.pallas_call(
        kernel,
        out_shape=out_shape,
        in_specs=[SMEM] * scalars + [ANY if in_hbm else VMEM] * (len(operands) - scalars),
        out_specs=[VMEM] * len(out_shape) if many else VMEM,
        scratch_shapes=list(scratch),
        compiler_params=PARAMS,
    )(*operands)


def body(
    points,
    quad_weight,
    basis,
    jacobi,
    near_panel,
    near_count,
    near_block,
    agg_index,
    coarse_inverse,
):
    block_total, _, point_count, rhs_count = basis.shape
    coarse_count = coarse_inverse.shape[1]
    narrow_count = lax.axis_size("narrow")
    wide_count = lax.axis_size("wide")
    panels_dev, slot_total = near_panel.shape
    nodes = near_block.shape[2] // 2
    width = SPAN * nodes
    pack_rows = coarse_count + EXTRA
    index = jnp.stack(
        [lax.axis_index("narrow"), lax.axis_index("wide"), lax.axis_index(AXES)]
    ).astype(jnp.int32)
    weight_row = quad_weight[None, :]
    low, *high = masks_of(wide_count)
    core, *across = masks_of(narrow_count, wide_count)
    high_groups = in_pairs(high)
    plane_groups = in_pairs([low] + across)
    wide_groups = high_groups + [[low]]
    narrow_groups = [[core]] + in_pairs(across)
    source_groups = high_groups + [[core]]
    high_count = 1 << len(high)
    source_total = 2 * high_count * point_count
    target_count = narrow_count
    pair_row = pltpu.VMEM((2, point_count), jnp.float32)
    one_row = pltpu.VMEM((1, point_count), jnp.float32)
    pair_index = pltpu.VMEM((2, point_count), jnp.int32)
    field = pltpu.VMEM((2, point_count, rhs_count), jnp.float32)

    pack = call(
        restrict_kernel,
        f32(1, pack_rows, point_count),
        (agg_index, basis, points, weight_row),
        0,
        [pair_index, field, pair_row, one_row, pltpu.SemaphoreType.DMA((4,))],
        4,
    )
    half_rows = block_total * (block_total + 1) // 2 * rhs_count
    halving = [[core]] + plane_groups
    masks = [core, low] + across
    inverse, member, smooth, weight, *half_parts = call(
        functools.partial(prefetch_kernel, masks),
        [
            f32(*coarse_inverse.shape),
            f32(2, coarse_count, point_count),
            f32(2, point_count, rhs_count),
            f32(point_count, rhs_count),
        ]
        + [f32(narrow_count, half_rows // (2 * narrow_count), rhs_count)] * 2,
        (index, pack, agg_index, basis, jacobi, weight_row, coarse_inverse),
        1,
        [
            pltpu.VMEM((half_rows, rhs_count), jnp.float32),
            pair_index,
            pltpu.VMEM(basis.shape, jnp.float32),
            pair_row,
            one_row,
            pltpu.SemaphoreType.DMA((5,)),
        ],
        5,
    )
    near_rows = jnp.transpose(near_block, (0, 2, 1, 3)).reshape(
        panels_dev, 2 * nodes, slot_total * 2 * nodes
    )
    packs = flip_each([pack] * (1 << len(wide_groups[0])), wide_groups[0])
    pack = join(packs, (weight,))
    half_send = join(half_parts[1:], (pack,))
    packs = gather_steps(pack, wide_groups[1:])
    source_rows = high_count * EXTRA // (narrow_count // 2)
    target_rows = 2 * EXTRA
    coarse_outs = pl.pallas_call(
        functools.partial(
            coarse_kernel, gather_order(wide_groups), 2, high_count
        ),
        out_shape=[f32(narrow_count // 2, coarse_count + source_rows, rhs_count)] * 2
        + [f32(high_count, EXTRA, point_count), f32(2, EXTRA, point_count)],
        in_specs=[SMEM, ANY, VMEM] + [VMEM] * len(packs),
        out_specs=[VMEM] * 4,
        scratch_shapes=[pltpu.VMEM((wide_count * coarse_count, rhs_count), jnp.float32)],
        compiler_params=PARAMS,
    )(index, near_rows, inverse, *packs)
    own_sources = coarse_outs[2]
    kept, got = flip_each(coarse_outs[:2], [core])
    groups = in_pairs(across)
    ways = 1 << len(groups[0])
    *coarse_parts, other_sources = call(
        functools.partial(coarse_sum_kernel, ways),
        [f32(narrow_count // 2 // ways, coarse_count + target_rows, rhs_count)] * ways
        + [f32(high_count, EXTRA, point_count)],
        (kept, got, coarse_outs[3]),
    )
    half_parts = flip_each([half_parts[0], half_send], [core])
    half_parts = sum_parts(half_parts, 2, coarse_parts[:1])
    half_steps = []
    for number, mask in enumerate([low] + across + high):
        got = flip_each(half_parts, [mask])
        half_steps.append(got[1])
        half_parts = sum_parts(got, 2 if number < len(across) else 1)
        if len(half_parts) == 1:
            half_parts = half_parts * 2
    half_total = half_parts[0]
    coarse_parts = scatter_steps(coarse_parts, groups)
    precond, pair_edge, next_edge = call(
        precond_kernel,
        [b16(1, 2, point_count, rhs_count)] + [b16(2, width, rhs_count)] * 2,
        (index, member, smooth, *coarse_parts),
        1,
    )
    matrix_spec = pl.BlockSpec((1, 3, point_count, source_total), lambda k: (k, 0, 0, 0))
    matrix = pl.pallas_call(
        functools.partial(matrix_kernel, coarse_count),
        out_shape=b16(target_count, 3, point_count, source_total),
        grid=(target_count,),
        in_specs=[VMEM] * (2 + len(coarse_parts)),
        out_specs=matrix_spec,
        compiler_params=PARAMS,
    )(own_sources, other_sources, *coarse_parts)
    device_count = narrow_count * wide_count
    pair_edge = flip(pair_edge, 1)
    pairs = [(i, i + 1) for i in range(1, device_count - 1, 2)]
    next_edge = lax.ppermute(next_edge, AXES, pairs + [(j, i) for i, j in pairs])
    fields = flip_each([precond] * (1 << len(source_groups[0])), source_groups[0])
    after = (matrix, half_steps[0], pair_edge, next_edge)
    fields = gather_steps(join(fields, after), source_groups[1:])

    after = (half_steps[1],)
    ways = 1 << len(plane_groups[0])
    far_parts = pl.pallas_call(
        functools.partial(far_kernel, ways, len(after)),
        out_shape=[f32(target_count // ways, 2, point_count, rhs_count)] * ways,
        grid=(target_count,),
        in_specs=[ANY] * len(after) + [matrix_spec] + [VMEM] * len(fields),
        out_specs=[VMEM] * ways,
        scratch_shapes=[pltpu.VMEM((source_total, 2 * rhs_count), jnp.bfloat16)],
        compiler_params=PARAMS,
    )(*after, matrix, *fields)
    far_parts = scatter_steps(far_parts, plane_groups)
    base = call(
        near_kernel,
        f32(2, point_count, rhs_count),
        (index, near_panel, near_count, near_rows, precond, pair_edge, next_edge),
        3,
        [
            pltpu.VMEM((2, 2 * width + point_count, rhs_count), jnp.bfloat16),
            pltpu.VMEM((panels_dev, slot_total * 2 * nodes, rhs_count), jnp.bfloat16),
        ],
    )

    hess_rows = block_total * rhs_count
    sum_rows = hess_rows + rhs_count
    image, *parts = pl.pallas_call(
        functools.partial(project_kernel, masks, 2),
        out_shape=[f32(2, point_count, rhs_count)]
        + [f32(narrow_count, sum_rows // (2 * narrow_count), rhs_count)] * 2,
        in_specs=[SMEM] + [ANY] + [VMEM] * (3 + len(far_parts)),
        out_specs=[VMEM] * 3,
        scratch_shapes=[pltpu.VMEM((sum_rows, rhs_count), jnp.float32)],
        compiler_params=PARAMS,
    )(index, half_steps[2], weight, basis, base, *far_parts)
    (total,) = sum_parts(scatter_steps(parts, halving), 1, half_steps[3:4])
    total = sum_butterfly(total, high_groups)
    parts = gather_steps(append(total, half_total), halving[::-1])
    hessenberg, upper_factor, new_block = call(
        functools.partial(factor_kernel, gather_order(part_groups(halving)[::-1]), masks),
        [
            f32(hess_rows, rhs_count),
            f32(rhs_count, rhs_count),
            f32(2 * point_count, rhs_count),
        ],
        (index, basis, image, *parts),
        1,
        [
            pltpu.VMEM((sum_rows, rhs_count), jnp.float32),
            pltpu.VMEM((half_rows, rhs_count), jnp.float32),
        ]
        + [pltpu.VMEM((rhs_count, rhs_count), jnp.float32)] * 2,
    )
    return (
        new_block.reshape(2, point_count, rhs_count),
        hessenberg.reshape(block_total, rhs_count, rhs_count),
        upper_factor,
    )


def solution(mesh):
    in_specs = (
        P(None, ("narrow", "wide")),
        P(("narrow", "wide")),
        P(None, None, ("narrow", "wide"), None),
        P(None, ("narrow", "wide")),
        P(("narrow", "wide"), None),
        P(("narrow", "wide")),
        P(("narrow", "wide"), None, None, None),
        P(None, ("narrow", "wide")),
        P(None, "wide", "narrow"),
    )
    out_specs = (P(None, ("narrow", "wide"), None), P(), P())
    return jax.shard_map(body, mesh=mesh, in_specs=in_specs, out_specs=out_specs, check_vma=False)
```

```python
import functools

import jax
import jax.numpy as jnp
from jax import lax
from jax.experimental import pallas as pl
from jax.experimental.pallas import tpu as pltpu
from jax.sharding import PartitionSpec as P

SPAN = 4


NU = 0.3
DELTA2 = 1e-05
ELASTIC = 40.0
AXES = ("narrow", "wide")
EXTRA = 8
ROWS = 8
SMEM = pl.BlockSpec(memory_space=pltpu.SMEM)
VMEM = pl.BlockSpec(memory_space=pltpu.VMEM)
ANY = pl.BlockSpec(memory_space=pl.ANY)
PARAMS = pltpu.CompilerParams(vmem_limit_bytes=48 * 1024 * 1024)


def split(value):
    high = value.astype(jnp.bfloat16)
    return high, (value - high.astype(jnp.float32)).astype(jnp.bfloat16)


def dot16(left, right, contract=((1,), (0,))):
    return lax.dot_general(left, right, (contract, ((), ())), preferred_element_type=jnp.float32)


def dot_rows(left, right, contract=((1,), (0,))):
    left_high, left_low = split(left)
    right_high, right_low = split(right)
    return dot16(left_high, right_high, contract) + (
        dot16(left_high, right_low, contract) + dot16(left_low, right_high, contract)
    )


def dot_first(left, right):
    return dot_rows(left, right, ((0,), (0,)))


def pick(member, value, contract=((1,), (0,))):
    member = member.astype(jnp.bfloat16)
    high, low = split(value)
    lowest = (value - high.astype(jnp.float32) - low.astype(jnp.float32)).astype(jnp.bfloat16)
    return dot16(member, high, contract) + (
        dot16(member, low, contract) + dot16(member, lowest, contract)
    )


def as_column(row, width):
    return jnp.transpose(jnp.broadcast_to(row, (width, row.shape[1])))


def flip(block, mask):
    count = lax.axis_size(AXES)
    return lax.ppermute(block, AXES, [(i, i ^ mask) for i in range(count)])


def masks_of(count, scale=1):
    return [scale << bit for bit in range(count.bit_length() - 1)]


def in_pairs(masks):
    return [masks[k : k + 2] for k in range(0, len(masks), 2)]


def combined(group, number):
    mask = 0
    for bit, part in enumerate(group):
        if number >> bit & 1:
            mask ^= part
    return mask


def flip_each(parts, group):
    return [parts[0]] + [flip(parts[j], combined(group, j)) for j in range(1, 1 << len(group))]


def join_kernel(count, *refs):
    parts, out_ref = refs[-1 - count : -1], refs[-1]
    size = parts[0].shape[0]
    for j, ref in enumerate(parts):
        out_ref[j * size : (j + 1) * size] = ref[...]


def join(parts, after=()):
    shape = (len(parts) * parts[0].shape[0],) + parts[0].shape[1:]
    return pl.pallas_call(
        functools.partial(join_kernel, len(parts)),
        out_shape=jax.ShapeDtypeStruct(shape, parts[0].dtype),
        in_specs=[ANY] * len(after) + [VMEM] * len(parts),
        out_specs=VMEM,
        compiler_params=PARAMS,
    )(*after, *parts)


def gather_steps(held, groups, after=()):
    parts = [held]
    for group in groups:
        if len(parts) > 1:
            held = join(parts, after)
            after = ()
        parts = flip_each([held] * (1 << len(group)), group)
    return parts


def gather_order(groups):
    order = [0]
    for group in groups:
        order = [k ^ combined(group, j) for j in range(1 << len(group)) for k in order]
    return order


def total_of(values):
    while len(values) > 1:
        values = [values[k] + values[k + 1] for k in range(0, len(values), 2)]
    return values[0]


def sum_kernel(count, skip, *refs):
    parts, outs = refs[skip : skip + count], refs[skip + count :]
    for k in range(outs[0].shape[0]):
        for j, out_ref in enumerate(outs):
            out_ref[k] = total_of([part[k * len(outs) + j] for part in parts])


def sum_parts(parts, ways, after=()):
    out = f32(parts[0].shape[0] // ways, *parts[0].shape[1:])
    return pl.pallas_call(
        functools.partial(sum_kernel, len(parts), len(after)),
        out_shape=[out] * ways,
        in_specs=[ANY] * len(after) + [VMEM] * len(parts),
        out_specs=[VMEM] * ways,
        compiler_params=PARAMS,
    )(*after, *parts)


def scatter_steps(parts, groups):
    for number, group in enumerate(groups):
        if number:
            parts = sum_parts(parts, 1 << len(group))
        parts = flip_each(parts, group)
    return parts


def sum_butterfly(total, groups):
    for group in groups:
        (total,) = sum_parts(flip_each([total] * (1 << len(group)), group), 1)
    return total


def append_kernel(left_ref, right_ref, out_ref):
    rows = left_ref.shape[1]
    out_ref[:, :rows, :] = left_ref[...]
    out_ref[:, rows:, :] = right_ref[...]


def append(left, right):
    count, rows, width = left.shape
    shape = f32(count, rows + right.shape[1], width)
    return call(append_kernel, shape, (left, right))


def part_groups(groups):
    bit, found = 0, []
    for group in groups:
        found.append([1 << (bit + k) for k in range(len(group))])
        bit += len(group)
    return found


def bits_of(index, masks):
    packed = 0
    for bit, mask in enumerate(masks):
        packed = packed + (lax.shift_right_logical(index, mask.bit_length() - 1) & 1) * (1 << bit)
    return packed


def members(agg_ref, a, coarse_count):
    ids = lax.broadcasted_iota(jnp.int32, (coarse_count, agg_ref.shape[1]), 0)
    return jnp.where(ids == agg_ref[a : a + 1, :], 1.0, 0.0)


def load_all(pairs, sems):
    copies = [
        pltpu.make_async_copy(source, target, sems.at[k])
        for k, (source, target) in enumerate(pairs)
    ]
    for copy in copies:
        copy.start()
    for copy in copies:
        copy.wait()


def restrict_kernel(
    agg_hbm, basis_hbm, points_hbm, weight_hbm, pack_ref, agg_ref, newest_ref, points_ref, weight_ref, sems
):
    coarse_count = pack_ref.shape[1] - EXTRA
    point_count = newest_ref.shape[1]
    load_all(
        [
            (basis_hbm.at[basis_hbm.shape[0] - 1], newest_ref),
            (agg_hbm, agg_ref),
            (points_hbm, points_ref),
            (weight_hbm, weight_ref),
        ],
        sems,
    )
    total = pick(members(agg_ref, 0, coarse_count), newest_ref[0]) + pick(
        members(agg_ref, 1, coarse_count), newest_ref[1]
    )
    pack_ref[0, :coarse_count, :] = total
    pack_ref[0, coarse_count:, :] = jnp.concatenate(
        [points_ref[...], weight_ref[...], jnp.zeros((EXTRA - 3, point_count), jnp.float32)], axis=0
    )


def prefetch_kernel(
    masks,
    index_ref,
    pack_hbm,
    agg_hbm,
    basis_hbm,
    jacobi_hbm,
    weight_hbm,
    inverse_hbm,
    inverse_ref,
    member_ref,
    smooth_ref,
    weight_out_ref,
    keep_ref,
    send_ref,
    half_ref,
    agg_ref,
    basis_ref,
    jacobi_ref,
    weight_ref,
    sems,
):
    coarse_count = member_ref.shape[1]
    block_total, _, _, rhs_count = basis_ref.shape
    load_all(
        [
            (basis_hbm, basis_ref),
            (agg_hbm, agg_ref),
            (jacobi_hbm, jacobi_ref),
            (weight_hbm, weight_ref),
            (inverse_hbm, inverse_ref),
        ],
        sems,
    )
    for a in range(2):
        member_ref[a] = members(agg_ref, a, coarse_count)
        smooth_ref[a] = (
            as_column(jacobi_ref[a : a + 1, :], rhs_count) * basis_ref[block_total - 1, a]
        )
    weight = as_column(weight_ref[...], rhs_count)
    weight_out_ref[...] = weight
    right = stacked(basis_ref)
    number = 0
    for i in range(block_total):
        left = jnp.concatenate([basis_ref[i, a] * weight for a in range(2)], axis=0)
        row = dot_first(left, right[:, i * rhs_count :])
        for j in range(i, block_total):
            block = row[:, (j - i) * rhs_count : (j - i + 1) * rhs_count]
            rows = slice(number * rhs_count, (number + 1) * rhs_count)
            half_ref[rows, :] = block * 0.5 if i == j else block
            number += 1
    spread(half_ref, (keep_ref, send_ref), bits_of(index_ref[2], masks))


def part_at(parts, k):
    size = parts[0].shape[0]
    return parts[k // size], k % size


def coarse_kernel(order, ways, z_count, index_ref, near_ref, inverse_ref, *refs):
    narrow_count, coarse_count, _ = inverse_ref.shape
    packs = refs[: len(refs) - ways - 3]
    outs = refs[len(packs) : len(packs) + ways]
    source_ref, target_ref, rhs_ref = refs[len(packs) + ways :]
    for k, offset in enumerate(order):
        first = pl.multiple_of((index_ref[1] ^ offset) * coarse_count, 8)
        ref, row = part_at(packs, k)
        rhs_ref[pl.ds(first, coarse_count), :] = ref[row, :coarse_count, :]
    for k in range(z_count):
        ref, row = part_at(packs, k)
        source_ref[k] = ref[row, coarse_count:, :]
    for k in range(target_ref.shape[0]):
        ref, row = part_at(packs, k * z_count)
        target_ref[k] = ref[row, coarse_count:, :]
    left = jnp.concatenate(
        [inverse_ref[index_ref[0] ^ k] for k in range(narrow_count)], axis=0
    )
    product = dot_rows(left, rhs_ref[...])
    tail = jnp.concatenate([source_ref[k] for k in range(z_count)], axis=0)
    each = z_count * EXTRA // (narrow_count // ways)
    for k in range(narrow_count):
        part = product[k * coarse_count : (k + 1) * coarse_count, :]
        outs[k % ways][k // ways, :coarse_count, :] = part
        first = (k // ways) * each
        outs[k % ways][k // ways, coarse_count:, :] = tail[first : first + each, :]


def coarse_sum_kernel(ways, kept_ref, got_ref, target_ref, *refs):
    outs, source_ref = refs[:ways], refs[ways]
    rows = target_ref.shape[0] * EXTRA
    coarse_count = outs[0].shape[1] - rows
    each = (kept_ref.shape[1] - coarse_count) // EXTRA
    for k in range(kept_ref.shape[0]):
        for j in range(each):
            first = coarse_count + j * EXTRA
            source_ref[k * each + j] = got_ref[k, first : first + EXTRA, :]
    for k in range(outs[0].shape[0]):
        for j in range(ways):
            source = k * ways + j
            outs[j][k, :coarse_count, :] = (
                kept_ref[source, :coarse_count, :] + got_ref[source, :coarse_count, :]
            )
            for t in range(target_ref.shape[0]):
                first = coarse_count + t * EXTRA
                outs[j][k, first : first + EXTRA, :] = target_ref[t]


def precond_kernel(index_ref, half_hbm, member_ref, smooth_ref, *refs):
    parts = refs[:-3]
    precond_ref, pair_ref, next_ref = refs[-3:]
    coarse_count = member_ref.shape[1]
    point_count = smooth_ref.shape[1]
    width = pair_ref.shape[1]
    even = (index_ref[2] & 1) == 0
    coarse_sol = total_of([part[0, :coarse_count, :] for part in parts])
    for a in range(2):
        value = smooth_ref[a] + pick(member_ref[a], coarse_sol, ((0,), (0,)))
        precond_ref[0, a] = value.astype(jnp.bfloat16)
        first = value[:width]
        last = value[point_count - width :]
        pair_ref[a] = jnp.where(even, last, first).astype(jnp.bfloat16)
        next_ref[a] = jnp.where(even, first, last).astype(jnp.bfloat16)


def matrix_kernel(coarse_count, own_ref, other_ref, *refs):
    targets, matrix_ref = refs[:-1], refs[-1]
    point_count = own_ref.shape[2]
    size = (targets[0].shape[1] - coarse_count) // EXTRA
    step = pl.program_id(0)
    first = pl.multiple_of(coarse_count + lax.rem(step, size) * EXTRA, EXTRA)
    target = targets[0][0, pl.ds(first, EXTRA), :]
    for j in range(1, len(targets)):
        target = jnp.where(step // size == j, targets[j][0, pl.ds(first, EXTRA), :], target)
    target_x = as_column(target[0:1, :], point_count)
    target_y = as_column(target[1:2, :], point_count)
    for s in range(matrix_ref.shape[3] // point_count):
        ref, row = part_at((own_ref, other_ref), s)
        source = ref[row]
        delta_x = target_x - source[0:1, :]
        delta_y = target_y - source[1:2, :]
        factor = ELASTIC * source[2:3, :]
        square_x = delta_x * delta_x
        square_y = delta_y * delta_y
        square_dist = square_x + square_y + DELTA2
        inverse = 1.0 / square_dist
        log_part = (-0.5 * (3.0 - 4.0 * NU)) * jnp.log(square_dist)
        lanes = slice(s * point_count, (s + 1) * point_count)
        matrix_ref[0, 0, :, lanes] = (factor * (log_part + square_x * inverse)).astype(jnp.bfloat16)
        matrix_ref[0, 1, :, lanes] = (factor * (delta_x * delta_y * inverse)).astype(jnp.bfloat16)
        matrix_ref[0, 2, :, lanes] = (factor * (log_part + square_y * inverse)).astype(jnp.bfloat16)


def far_kernel(ways, skip, *refs):
    matrix_ref, *refs = refs[skip:]
    fields = refs[: len(refs) - ways - 1]
    outs = refs[len(fields) : len(fields) + ways]
    fields_ref = refs[-1]
    point_count, rhs_count = fields[0].shape[2:]
    step = pl.program_id(0)

    @pl.when(step == 0)
    def _():
        for s in range(fields_ref.shape[0] // point_count):
            ref, row = part_at(fields, s)
            for b in range(2):
                rows = slice(s * point_count, (s + 1) * point_count)
                fields_ref[rows, b * rhs_count : (b + 1) * rhs_count] = ref[row, b]

    mixed = dot16(matrix_ref[0, 1], fields_ref[...])
    out_x = dot16(matrix_ref[0, 0], fields_ref[:, :rhs_count]) + mixed[:, rhs_count:]
    out_y = dot16(matrix_ref[0, 2], fields_ref[:, rhs_count:]) + mixed[:, :rhs_count]
    for j, out_ref in enumerate(outs):

        @pl.when(lax.rem(step, ways) == j)
        def _(out_ref=out_ref):
            out_ref[step // ways, 0] = out_x
            out_ref[step // ways, 1] = out_y


def near_kernel(
    index_ref,
    panel_ref,
    count_ref,
    block_ref,
    own_ref,
    pair_ref,
    next_ref,
    out_ref,
    line_ref,
    gathered_ref,
):
    point_count = own_ref.shape[2]
    width = pair_ref.shape[1]
    even = (index_ref[2] & 1) == 0
    panels_dev, double_nodes, _ = block_ref.shape
    nodes = double_nodes // 2
    slot_total = panel_ref.shape[1]
    for b in range(2):
        pair = pair_ref[b].astype(jnp.float32)
        following = next_ref[b].astype(jnp.float32)
        line_ref[b, :width, :] = jnp.where(even, following, pair).astype(jnp.bfloat16)
        line_ref[b, width : width + point_count, :] = own_ref[0, b]
        line_ref[b, width + point_count :, :] = jnp.where(even, pair, following).astype(
            jnp.bfloat16
        )
    first_panel = index_ref[2] * panels_dev
    lane = lax.broadcasted_iota(jnp.int32, block_ref.shape[1:], 1)
    for p in range(panels_dev):
        for k in range(slot_total):
            first = pl.multiple_of((panel_ref[p, k] - first_panel) * nodes + width, 16)
            for b in range(2):
                row = (k * 2 + b) * nodes
                gathered_ref[p, row : row + nodes, :] = line_ref[b, pl.ds(first, nodes), :]
        blocks = jnp.where(
            lane < count_ref[p] * double_nodes, block_ref[p].astype(jnp.float32), 0.0
        ).astype(jnp.bfloat16)
        near = dot16(blocks, gathered_ref[p])
        for a in range(2):
            rows = slice(p * nodes, (p + 1) * nodes)
            own = own_ref[0, a, rows, :].astype(jnp.float32)
            out_ref[a, rows, :] = 0.5 * own + near[a * nodes : (a + 1) * nodes, :]


def spread(full_ref, outs, own):
    rows = outs[0].shape[1]
    for k in range(len(outs) * outs[0].shape[0]):
        first = pl.multiple_of((own ^ k) * rows, 8)
        outs[k % len(outs)][k // len(outs)] = full_ref[pl.ds(first, rows), :]


def collect(order, parts, full_ref, own, start):
    rows = full_ref.shape[0] // len(order)
    for k, offset in enumerate(order):
        first = pl.multiple_of((own ^ offset) * rows, 8)
        ref, row = part_at(parts, k)
        full_ref[pl.ds(first, rows), :] = ref[row, start : start + rows, :]


def stacked(basis_ref):
    return jnp.concatenate(
        [
            jnp.concatenate([basis_ref[j, a] for j in range(basis_ref.shape[0])], axis=1)
            for a in range(2)
        ],
        axis=0,
    )


def project_kernel(masks, ways, index_ref, half_hbm, weight_ref, basis_ref, base_ref, *refs):
    arrived = refs[: len(refs) - ways - 2]
    image_ref = refs[len(arrived)]
    outs = refs[len(arrived) + 1 : -1]
    full_ref = refs[-1]
    weighted = []
    for a in range(2):
        image = base_ref[a] + total_of([part[0, a] for part in arrived])
        image_ref[a] = image
        weighted.append(image * weight_ref[...])
    image = jnp.concatenate([image_ref[0], image_ref[1]], axis=0)
    left = jnp.concatenate([stacked(basis_ref), image], axis=1)
    full_ref[...] = dot_first(left, jnp.concatenate(weighted, axis=0))
    spread(full_ref, outs, bits_of(index_ref[2], masks))


def factor_kernel(gather, masks, index_ref, basis_ref, image_ref, *refs):
    parts = refs[:-7]
    hess_ref, upper_ref, new_ref, full_ref, half_ref, work_ref, inverse_ref = refs[-7:]
    block_total, _, _, order = basis_ref.shape
    hess_rows = block_total * order
    tile = (ROWS, order)
    lane = lax.broadcasted_iota(jnp.int32, tile, 1)
    row = lax.broadcasted_iota(jnp.int32, tile, 0)
    own = bits_of(index_ref[2], masks)
    collect(gather, parts, full_ref, own, 0)
    collect(gather, parts, half_ref, own, full_ref.shape[0] // len(gather))
    hessenberg = full_ref[:hess_rows, :]
    hess_ref[...] = hessenberg
    rows = []
    number = 0
    for i in range(block_total):
        count = block_total - i
        left = jnp.concatenate(
            [
                half_ref[(number + j) * order : (number + j + 1) * order, :]
                for j in range(count)
            ],
            axis=1,
        )
        rows.append(dot_rows(left, full_ref[i * order : hess_rows, :]))
        number += count
    product = dot_first(hessenberg, jnp.concatenate(rows, axis=0) - hessenberg)
    work_ref[...] = full_ref[hess_rows:, :] + (product + jnp.transpose(product))
    for block in range(order // ROWS):
        start = block * ROWS
        inverse_ref[start : start + ROWS, :] = jnp.where(lane == row + start, 1.0, 0.0)
    for block in range(order // ROWS):
        start = block * ROWS
        own = work_ref[start : start + ROWS, :]
        own_inverse = inverse_ref[start : start + ROWS, :]
        columns = [
            jnp.broadcast_to(own[:, start + m : start + m + 1], tile) for m in range(ROWS)
        ]
        entry = {
            (j, m): jnp.broadcast_to(columns[m][j : j + 1, :], tile)
            for m in range(ROWS)
            for j in range(m, ROWS)
        }
        scale = []
        for m in range(ROWS):
            scale.append(lax.rsqrt(entry[m, m]))
            for j in range(m + 1, ROWS):
                entry[j, m] = entry[j, m] * scale[m]
            for n in range(m + 1, ROWS):
                for j in range(n, ROWS):
                    entry[j, n] = entry[j, n] - entry[j, m] * entry[n, m]
        solved = []
        solved_inverse = []
        for m in range(ROWS):
            upper_row = jnp.broadcast_to(own[m : m + 1, :], tile)
            inverse_row = jnp.broadcast_to(own_inverse[m : m + 1, :], tile)
            for j in range(m):
                upper_row = upper_row - entry[m, j] * solved[j]
                inverse_row = inverse_row - entry[m, j] * solved_inverse[j]
            upper_row = upper_row * scale[m]
            inverse_row = inverse_row * scale[m]
            solved.append(upper_row)
            solved_inverse.append(inverse_row)
        upper_rows = solved[ROWS - 1]
        inverse_rows = solved_inverse[ROWS - 1]
        for m in range(ROWS - 1):
            upper_rows = jnp.where(row == m, solved[m], upper_rows)
            inverse_rows = jnp.where(row == m, solved_inverse[m], inverse_rows)
        upper_ref[start : start + ROWS, :] = jnp.where(lane >= row + start, upper_rows, 0.0)
        inverse_ref[start : start + ROWS, :] = inverse_rows
        for later in range(block + 1, order // ROWS):
            first = later * ROWS
            target = work_ref[first : first + ROWS, :]
            target_inverse = inverse_ref[first : first + ROWS, :]
            multiplier = []
            for m in range(ROWS):
                value = jnp.broadcast_to(target[:, start + m : start + m + 1], tile)
                for j in range(m):
                    value = value - multiplier[j] * entry[m, j]
                multiplier.append(value * scale[m])
            for m in range(ROWS):
                target = target - multiplier[m] * solved[m]
                target_inverse = target_inverse - multiplier[m] * solved_inverse[m]
            work_ref[first : first + ROWS, :] = target
            inverse_ref[first : first + ROWS, :] = target_inverse
    image = jnp.concatenate([image_ref[0], image_ref[1]], axis=0)
    remainder = image - dot_rows(stacked(basis_ref), hessenberg)
    new_ref[...] = dot_rows(remainder, inverse_ref[...], ((1,), (1,)))


def f32(*shape):
    return jax.ShapeDtypeStruct(shape, jnp.float32)


def b16(*shape):
    return jax.ShapeDtypeStruct(shape, jnp.bfloat16)


def call(kernel, out_shape, operands, scalars=0, scratch=(), in_hbm=0):
    many = isinstance(out_shape, (tuple, list))
    free = len(operands) - in_hbm
    operands = list(operands[:free]) + [
        pltpu.with_memory_space_constraint(x, pltpu.HBM) for x in operands[free:]
    ]
    return pl.pallas_call(
        kernel,
        out_shape=out_shape,
        in_specs=[SMEM] * scalars + [ANY if in_hbm else VMEM] * (len(operands) - scalars),
        out_specs=[VMEM] * len(out_shape) if many else VMEM,
        scratch_shapes=list(scratch),
        compiler_params=PARAMS,
    )(*operands)


def body(
    points,
    quad_weight,
    basis,
    jacobi,
    near_panel,
    near_count,
    near_block,
    agg_index,
    coarse_inverse,
):
    block_total, _, point_count, rhs_count = basis.shape
    coarse_count = coarse_inverse.shape[1]
    narrow_count = lax.axis_size("narrow")
    wide_count = lax.axis_size("wide")
    panels_dev, slot_total = near_panel.shape
    nodes = near_block.shape[2] // 2
    width = SPAN * nodes
    pack_rows = coarse_count + EXTRA
    index = jnp.stack(
        [lax.axis_index("narrow"), lax.axis_index("wide"), lax.axis_index(AXES)]
    ).astype(jnp.int32)
    weight_row = quad_weight[None, :]
    low, *high = masks_of(wide_count)
    core, *across = masks_of(narrow_count, wide_count)
    high_groups = in_pairs(high)
    plane_groups = in_pairs([low] + across)
    wide_groups = high_groups + [[low]]
    narrow_groups = [[core]] + in_pairs(across)
    source_groups = high_groups + [[core]]
    high_count = 1 << len(high)
    source_total = 2 * high_count * point_count
    target_count = narrow_count
    pair_row = pltpu.VMEM((2, point_count), jnp.float32)
    one_row = pltpu.VMEM((1, point_count), jnp.float32)
    pair_index = pltpu.VMEM((2, point_count), jnp.int32)
    field = pltpu.VMEM((2, point_count, rhs_count), jnp.float32)

    pack = call(
        restrict_kernel,
        f32(1, pack_rows, point_count),
        (agg_index, basis, points, weight_row),
        0,
        [pair_index, field, pair_row, one_row, pltpu.SemaphoreType.DMA((4,))],
        4,
    )
    half_rows = block_total * (block_total + 1) // 2 * rhs_count
    halving = [[core]] + plane_groups
    masks = [core, low] + across
    inverse, member, smooth, weight, *half_parts = call(
        functools.partial(prefetch_kernel, masks),
        [
            f32(*coarse_inverse.shape),
            f32(2, coarse_count, point_count),
            f32(2, point_count, rhs_count),
            f32(point_count, rhs_count),
        ]
        + [f32(narrow_count, half_rows // (2 * narrow_count), rhs_count)] * 2,
        (index, pack, agg_index, basis, jacobi, weight_row, coarse_inverse),
        1,
        [
            pltpu.VMEM((half_rows, rhs_count), jnp.float32),
            pair_index,
            pltpu.VMEM(basis.shape, jnp.float32),
            pair_row,
            one_row,
            pltpu.SemaphoreType.DMA((5,)),
        ],
        5,
    )
    near_rows = jnp.transpose(near_block, (0, 2, 1, 3)).reshape(
        panels_dev, 2 * nodes, slot_total * 2 * nodes
    )
    packs = flip_each([pack] * (1 << len(wide_groups[0])), wide_groups[0])
    pack = join(packs, (weight,))
    half_send = join(half_parts[1:], (pack,))
    packs = gather_steps(pack, wide_groups[1:])
    source_rows = high_count * EXTRA // (narrow_count // 2)
    target_rows = 2 * EXTRA
    coarse_outs = pl.pallas_call(
        functools.partial(
            coarse_kernel, gather_order(wide_groups), 2, high_count
        ),
        out_shape=[f32(narrow_count // 2, coarse_count + source_rows, rhs_count)] * 2
        + [f32(high_count, EXTRA, point_count), f32(2, EXTRA, point_count)],
        in_specs=[SMEM, ANY, VMEM] + [VMEM] * len(packs),
        out_specs=[VMEM] * 4,
        scratch_shapes=[pltpu.VMEM((wide_count * coarse_count, rhs_count), jnp.float32)],
        compiler_params=PARAMS,
    )(index, near_rows, inverse, *packs)
    own_sources = coarse_outs[2]
    kept, got = flip_each(coarse_outs[:2], [core])
    groups = in_pairs(across)
    ways = 1 << len(groups[0])
    *coarse_parts, other_sources = call(
        functools.partial(coarse_sum_kernel, ways),
        [f32(narrow_count // 2 // ways, coarse_count + target_rows, rhs_count)] * ways
        + [f32(high_count, EXTRA, point_count)],
        (kept, got, coarse_outs[3]),
    )
    half_parts = flip_each([half_parts[0], half_send], [core])
    half_parts = sum_parts(half_parts, 2)
    half_steps = []
    for number, mask in enumerate([low] + across + high):
        got = flip_each(half_parts, [mask])
        half_steps.append(got[1])
        half_parts = sum_parts(got, 2 if number < len(across) else 1)
        if len(half_parts) == 1:
            half_parts = half_parts * 2
    half_total = half_parts[0]
    coarse_parts = scatter_steps(coarse_parts, groups)
    precond, pair_edge, next_edge = pl.pallas_call(
        precond_kernel,
        out_shape=[b16(1, 2, point_count, rhs_count)] + [b16(2, width, rhs_count)] * 2,
        in_specs=[SMEM, ANY] + [VMEM] * (2 + len(coarse_parts)),
        out_specs=[VMEM] * 3,
        compiler_params=PARAMS,
    )(index, half_steps[0], member, smooth, *coarse_parts)
    matrix_spec = pl.BlockSpec((1, 3, point_count, source_total), lambda k: (k, 0, 0, 0))
    matrix = pl.pallas_call(
        functools.partial(matrix_kernel, coarse_count),
        out_shape=b16(target_count, 3, point_count, source_total),
        grid=(target_count,),
        in_specs=[VMEM] * (2 + len(coarse_parts)),
        out_specs=matrix_spec,
        compiler_params=PARAMS,
    )(own_sources, other_sources, *coarse_parts)
    device_count = narrow_count * wide_count
    pair_edge = flip(pair_edge, 1)
    pairs = [(i, i + 1) for i in range(1, device_count - 1, 2)]
    next_edge = lax.ppermute(next_edge, AXES, pairs + [(j, i) for i, j in pairs])
    fields = flip_each([precond] * (1 << len(source_groups[0])), source_groups[0])
    after = (matrix, half_steps[1], pair_edge, next_edge)
    fields = gather_steps(join(fields, after), source_groups[1:])

    after = ()
    ways = 1 << len(plane_groups[0])
    far_parts = pl.pallas_call(
        functools.partial(far_kernel, ways, len(after)),
        out_shape=[f32(target_count // ways, 2, point_count, rhs_count)] * ways,
        grid=(target_count,),
        in_specs=[ANY] * len(after) + [matrix_spec] + [VMEM] * len(fields),
        out_specs=[VMEM] * ways,
        scratch_shapes=[pltpu.VMEM((source_total, 2 * rhs_count), jnp.bfloat16)],
        compiler_params=PARAMS,
    )(*after, matrix, *fields)
    far_parts = scatter_steps(far_parts, plane_groups)
    base = call(
        near_kernel,
        f32(2, point_count, rhs_count),
        (index, near_panel, near_count, near_rows, precond, pair_edge, next_edge),
        3,
        [
            pltpu.VMEM((2, 2 * width + point_count, rhs_count), jnp.bfloat16),
            pltpu.VMEM((panels_dev, slot_total * 2 * nodes, rhs_count), jnp.bfloat16),
        ],
    )

    hess_rows = block_total * rhs_count
    sum_rows = hess_rows + rhs_count
    image, *parts = pl.pallas_call(
        functools.partial(project_kernel, masks, 2),
        out_shape=[f32(2, point_count, rhs_count)]
        + [f32(narrow_count, sum_rows // (2 * narrow_count), rhs_count)] * 2,
        in_specs=[SMEM] + [ANY] + [VMEM] * (3 + len(far_parts)),
        out_specs=[VMEM] * 3,
        scratch_shapes=[pltpu.VMEM((sum_rows, rhs_count), jnp.float32)],
        compiler_params=PARAMS,
    )(index, half_steps[2], weight, basis, base, *far_parts)
    (total,) = sum_parts(scatter_steps(parts, halving), 1, half_steps[3:4])
    total = sum_butterfly(total, high_groups)
    parts = gather_steps(append(total, half_total), halving[::-1])
    hessenberg, upper_factor, new_block = call(
        functools.partial(factor_kernel, gather_order(part_groups(halving)[::-1]), masks),
        [
            f32(hess_rows, rhs_count),
            f32(rhs_count, rhs_count),
            f32(2 * point_count, rhs_count),
        ],
        (index, basis, image, *parts),
        1,
        [
            pltpu.VMEM((sum_rows, rhs_count), jnp.float32),
            pltpu.VMEM((half_rows, rhs_count), jnp.float32),
        ]
        + [pltpu.VMEM((rhs_count, rhs_count), jnp.float32)] * 2,
    )
    return (
        new_block.reshape(2, point_count, rhs_count),
        hessenberg.reshape(block_total, rhs_count, rhs_count),
        upper_factor,
    )


def solution(mesh):
    in_specs = (
        P(None, ("narrow", "wide")),
        P(("narrow", "wide")),
        P(None, None, ("narrow", "wide"), None),
        P(None, ("narrow", "wide")),
        P(("narrow", "wide"), None),
        P(("narrow", "wide")),
        P(("narrow", "wide"), None, None, None),
        P(None, ("narrow", "wide")),
        P(None, "wide", "narrow"),
    )
    out_specs = (P(None, ("narrow", "wide"), None), P(), P())
    return jax.shard_map(body, mesh=mesh, in_specs=in_specs, out_specs=out_specs, check_vma=False)
```

```python
import functools

import jax
import jax.numpy as jnp
from jax import lax
from jax.experimental import pallas as pl
from jax.experimental.pallas import tpu as pltpu
from jax.sharding import PartitionSpec as P

SPAN = 4


NU = 0.3
DELTA2 = 1e-05
ELASTIC = 40.0
AXES = ("narrow", "wide")
EXTRA = 8
ROWS = 8
SMEM = pl.BlockSpec(memory_space=pltpu.SMEM)
VMEM = pl.BlockSpec(memory_space=pltpu.VMEM)
ANY = pl.BlockSpec(memory_space=pl.ANY)
PARAMS = pltpu.CompilerParams(vmem_limit_bytes=48 * 1024 * 1024)


def split(value):
    high = value.astype(jnp.bfloat16)
    return high, (value - high.astype(jnp.float32)).astype(jnp.bfloat16)


def dot16(left, right, contract=((1,), (0,))):
    return lax.dot_general(left, right, (contract, ((), ())), preferred_element_type=jnp.float32)


def dot_rows(left, right, contract=((1,), (0,))):
    left_high, left_low = split(left)
    right_high, right_low = split(right)
    return dot16(left_high, right_high, contract) + (
        dot16(left_high, right_low, contract) + dot16(left_low, right_high, contract)
    )


def dot_first(left, right):
    return dot_rows(left, right, ((0,), (0,)))


def pick(member, value, contract=((1,), (0,))):
    member = member.astype(jnp.bfloat16)
    high, low = split(value)
    lowest = (value - high.astype(jnp.float32) - low.astype(jnp.float32)).astype(jnp.bfloat16)
    return dot16(member, high, contract) + (
        dot16(member, low, contract) + dot16(member, lowest, contract)
    )


def as_column(row, width):
    return jnp.transpose(jnp.broadcast_to(row, (width, row.shape[1])))


def flip(block, mask):
    count = lax.axis_size(AXES)
    return lax.ppermute(block, AXES, [(i, i ^ mask) for i in range(count)])


def masks_of(count, scale=1):
    return [scale << bit for bit in range(count.bit_length() - 1)]


def in_pairs(masks):
    return [masks[k : k + 2] for k in range(0, len(masks), 2)]


def combined(group, number):
    mask = 0
    for bit, part in enumerate(group):
        if number >> bit & 1:
            mask ^= part
    return mask


def flip_each(parts, group):
    return [parts[0]] + [flip(parts[j], combined(group, j)) for j in range(1, 1 << len(group))]


def join_kernel(count, *refs):
    parts, out_ref = refs[-1 - count : -1], refs[-1]
    size = parts[0].shape[0]
    for j, ref in enumerate(parts):
        out_ref[j * size : (j + 1) * size] = ref[...]


def join(parts, after=()):
    shape = (len(parts) * parts[0].shape[0],) + parts[0].shape[1:]
    return pl.pallas_call(
        functools.partial(join_kernel, len(parts)),
        out_shape=jax.ShapeDtypeStruct(shape, parts[0].dtype),
        in_specs=[ANY] * len(after) + [VMEM] * len(parts),
        out_specs=VMEM,
        compiler_params=PARAMS,
    )(*after, *parts)


def gather_steps(held, groups, after=()):
    parts = [held]
    for group in groups:
        if len(parts) > 1:
            held = join(parts, after)
            after = ()
        parts = flip_each([held] * (1 << len(group)), group)
    return parts


def gather_order(groups):
    order = [0]
    for group in groups:
        order = [k ^ combined(group, j) for j in range(1 << len(group)) for k in order]
    return order


def total_of(values):
    while len(values) > 1:
        values = [values[k] + values[k + 1] for k in range(0, len(values), 2)]
    return values[0]


def sum_kernel(count, skip, *refs):
    parts, outs = refs[skip : skip + count], refs[skip + count :]
    for k in range(outs[0].shape[0]):
        for j, out_ref in enumerate(outs):
            out_ref[k] = total_of([part[k * len(outs) + j] for part in parts])


def sum_parts(parts, ways, after=()):
    out = f32(parts[0].shape[0] // ways, *parts[0].shape[1:])
    return pl.pallas_call(
        functools.partial(sum_kernel, len(parts), len(after)),
        out_shape=[out] * ways,
        in_specs=[ANY] * len(after) + [VMEM] * len(parts),
        out_specs=[VMEM] * ways,
        compiler_params=PARAMS,
    )(*after, *parts)


def scatter_steps(parts, groups):
    for number, group in enumerate(groups):
        if number:
            parts = sum_parts(parts, 1 << len(group))
        parts = flip_each(parts, group)
    return parts


def sum_butterfly(total, groups):
    for group in groups:
        (total,) = sum_parts(flip_each([total] * (1 << len(group)), group), 1)
    return total


def append_kernel(left_ref, right_ref, out_ref):
    rows = left_ref.shape[1]
    out_ref[:, :rows, :] = left_ref[...]
    out_ref[:, rows:, :] = right_ref[...]


def append(left, right):
    count, rows, width = left.shape
    shape = f32(count, rows + right.shape[1], width)
    return call(append_kernel, shape, (left, right))


def part_groups(groups):
    bit, found = 0, []
    for group in groups:
        found.append([1 << (bit + k) for k in range(len(group))])
        bit += len(group)
    return found


def bits_of(index, masks):
    packed = 0
    for bit, mask in enumerate(masks):
        packed = packed + (lax.shift_right_logical(index, mask.bit_length() - 1) & 1) * (1 << bit)
    return packed


def members(agg_ref, a, coarse_count):
    ids = lax.broadcasted_iota(jnp.int32, (coarse_count, agg_ref.shape[1]), 0)
    return jnp.where(ids == agg_ref[a : a + 1, :], 1.0, 0.0)


def load_all(pairs, sems):
    copies = [
        pltpu.make_async_copy(source, target, sems.at[k])
        for k, (source, target) in enumerate(pairs)
    ]
    for copy in copies:
        copy.start()
    for copy in copies:
        copy.wait()


def restrict_kernel(
    agg_hbm, basis_hbm, points_hbm, weight_hbm, pack_ref, agg_ref, newest_ref, points_ref, weight_ref, sems
):
    coarse_count = pack_ref.shape[1] - EXTRA
    point_count = newest_ref.shape[1]
    load_all(
        [
            (basis_hbm.at[basis_hbm.shape[0] - 1], newest_ref),
            (agg_hbm, agg_ref),
            (points_hbm, points_ref),
            (weight_hbm, weight_ref),
        ],
        sems,
    )
    total = pick(members(agg_ref, 0, coarse_count), newest_ref[0]) + pick(
        members(agg_ref, 1, coarse_count), newest_ref[1]
    )
    pack_ref[0, :coarse_count, :] = total
    pack_ref[0, coarse_count:, :] = jnp.concatenate(
        [points_ref[...], weight_ref[...], jnp.zeros((EXTRA - 3, point_count), jnp.float32)], axis=0
    )


def prefetch_kernel(
    masks,
    index_ref,
    pack_hbm,
    agg_hbm,
    basis_hbm,
    jacobi_hbm,
    weight_hbm,
    inverse_hbm,
    inverse_ref,
    member_ref,
    smooth_ref,
    weight_out_ref,
    keep_ref,
    send_ref,
    half_ref,
    agg_ref,
    basis_ref,
    jacobi_ref,
    weight_ref,
    sems,
):
    coarse_count = member_ref.shape[1]
    block_total, _, _, rhs_count = basis_ref.shape
    load_all(
        [
            (basis_hbm, basis_ref),
            (agg_hbm, agg_ref),
            (jacobi_hbm, jacobi_ref),
            (weight_hbm, weight_ref),
            (inverse_hbm, inverse_ref),
        ],
        sems,
    )
    for a in range(2):
        member_ref[a] = members(agg_ref, a, coarse_count)
        smooth_ref[a] = (
            as_column(jacobi_ref[a : a + 1, :], rhs_count) * basis_ref[block_total - 1, a]
        )
    weight = as_column(weight_ref[...], rhs_count)
    weight_out_ref[...] = weight
    right = stacked(basis_ref)
    number = 0
    for i in range(block_total):
        left = jnp.concatenate([basis_ref[i, a] * weight for a in range(2)], axis=0)
        row = dot_first(left, right[:, i * rhs_count :])
        for j in range(i, block_total):
            block = row[:, (j - i) * rhs_count : (j - i + 1) * rhs_count]
            rows = slice(number * rhs_count, (number + 1) * rhs_count)
            half_ref[rows, :] = block * 0.5 if i == j else block
            number += 1
    spread(half_ref, (keep_ref, send_ref), bits_of(index_ref[2], masks))


def part_at(parts, k):
    size = parts[0].shape[0]
    return parts[k // size], k % size


def coarse_kernel(order, ways, z_count, index_ref, near_ref, inverse_ref, *refs):
    narrow_count, coarse_count, _ = inverse_ref.shape
    packs = refs[: len(refs) - ways - 3]
    outs = refs[len(packs) : len(packs) + ways]
    source_ref, target_ref, rhs_ref = refs[len(packs) + ways :]
    for k, offset in enumerate(order):
        first = pl.multiple_of((index_ref[1] ^ offset) * coarse_count, 8)
        ref, row = part_at(packs, k)
        rhs_ref[pl.ds(first, coarse_count), :] = ref[row, :coarse_count, :]
    for k in range(z_count):
        ref, row = part_at(packs, k)
        source_ref[k] = ref[row, coarse_count:, :]
    for k in range(target_ref.shape[0]):
        ref, row = part_at(packs, k * z_count)
        target_ref[k] = ref[row, coarse_count:, :]
    left = jnp.concatenate(
        [inverse_ref[index_ref[0] ^ k] for k in range(narrow_count)], axis=0
    )
    product = dot_rows(left, rhs_ref[...])
    tail = jnp.concatenate([source_ref[k] for k in range(z_count)], axis=0)
    each = z_count * EXTRA // (narrow_count // ways)
    for k in range(narrow_count):
        part = product[k * coarse_count : (k + 1) * coarse_count, :]
        outs[k % ways][k // ways, :coarse_count, :] = part
        first = (k // ways) * each
        outs[k % ways][k // ways, coarse_count:, :] = tail[first : first + each, :]


def coarse_sum_kernel(ways, kept_ref, got_ref, target_ref, *refs):
    outs, source_ref = refs[:ways], refs[ways]
    rows = target_ref.shape[0] * EXTRA
    coarse_count = outs[0].shape[1] - rows
    each = (kept_ref.shape[1] - coarse_count) // EXTRA
    for k in range(kept_ref.shape[0]):
        for j in range(each):
            first = coarse_count + j * EXTRA
            source_ref[k * each + j] = got_ref[k, first : first + EXTRA, :]
    for k in range(outs[0].shape[0]):
        for j in range(ways):
            source = k * ways + j
            outs[j][k, :coarse_count, :] = (
                kept_ref[source, :coarse_count, :] + got_ref[source, :coarse_count, :]
            )
            for t in range(target_ref.shape[0]):
                first = coarse_count + t * EXTRA
                outs[j][k, first : first + EXTRA, :] = target_ref[t]


def precond_kernel(index_ref, half_hbm, member_ref, smooth_ref, *refs):
    parts = refs[:-3]
    precond_ref, pair_ref, next_ref = refs[-3:]
    coarse_count = member_ref.shape[1]
    point_count = smooth_ref.shape[1]
    width = pair_ref.shape[1]
    even = (index_ref[2] & 1) == 0
    coarse_sol = total_of([part[0, :coarse_count, :] for part in parts])
    for a in range(2):
        value = smooth_ref[a] + pick(member_ref[a], coarse_sol, ((0,), (0,)))
        precond_ref[0, a] = value.astype(jnp.bfloat16)
        first = value[:width]
        last = value[point_count - width :]
        pair_ref[a] = jnp.where(even, last, first).astype(jnp.bfloat16)
        next_ref[a] = jnp.where(even, first, last).astype(jnp.bfloat16)


def matrix_kernel(coarse_count, own_ref, other_ref, *refs):
    targets, matrix_ref = refs[:-1], refs[-1]
    point_count = own_ref.shape[2]
    size = (targets[0].shape[1] - coarse_count) // EXTRA
    step = pl.program_id(0)
    first = pl.multiple_of(coarse_count + lax.rem(step, size) * EXTRA, EXTRA)
    target = targets[0][0, pl.ds(first, EXTRA), :]
    for j in range(1, len(targets)):
        target = jnp.where(step // size == j, targets[j][0, pl.ds(first, EXTRA), :], target)
    target_x = as_column(target[0:1, :], point_count)
    target_y = as_column(target[1:2, :], point_count)
    for s in range(matrix_ref.shape[3] // point_count):
        ref, row = part_at((own_ref, other_ref), s)
        source = ref[row]
        delta_x = target_x - source[0:1, :]
        delta_y = target_y - source[1:2, :]
        factor = ELASTIC * source[2:3, :]
        square_x = delta_x * delta_x
        square_y = delta_y * delta_y
        square_dist = square_x + square_y + DELTA2
        inverse = 1.0 / square_dist
        log_part = (-0.5 * (3.0 - 4.0 * NU)) * jnp.log(square_dist)
        lanes = slice(s * point_count, (s + 1) * point_count)
        matrix_ref[0, 0, :, lanes] = (factor * (log_part + square_x * inverse)).astype(jnp.bfloat16)
        matrix_ref[0, 1, :, lanes] = (factor * (delta_x * delta_y * inverse)).astype(jnp.bfloat16)
        matrix_ref[0, 2, :, lanes] = (factor * (log_part + square_y * inverse)).astype(jnp.bfloat16)


def far_kernel(ways, matrix_ref, field_ref, *refs):
    earlier, outs, fields_ref = refs[: -1 - ways], refs[-1 - ways : -1], refs[-1]
    point_count, rhs_count = field_ref.shape[2:]
    step = pl.program_id(0)

    @pl.when(step == 0)
    def _():
        for s in range(field_ref.shape[0]):
            for b in range(2):
                rows = slice(s * point_count, (s + 1) * point_count)
                fields_ref[rows, b * rhs_count : (b + 1) * rhs_count] = field_ref[s, b]

    mixed = dot16(matrix_ref[0, 1], fields_ref[...])
    out_x = dot16(matrix_ref[0, 0], fields_ref[:, :rhs_count]) + mixed[:, rhs_count:]
    out_y = dot16(matrix_ref[0, 2], fields_ref[:, rhs_count:]) + mixed[:, :rhs_count]
    for j, out_ref in enumerate(outs):

        @pl.when(lax.rem(step, ways) == j)
        def _(j=j, out_ref=out_ref):
            row = step // ways
            if earlier:
                out_ref[row, 0] = out_x + earlier[j][row, 0]
                out_ref[row, 1] = out_y + earlier[j][row, 1]
            else:
                out_ref[row, 0] = out_x
                out_ref[row, 1] = out_y


def near_kernel(
    index_ref,
    panel_ref,
    count_ref,
    block_ref,
    own_ref,
    pair_ref,
    next_ref,
    out_ref,
    line_ref,
    gathered_ref,
):
    point_count = own_ref.shape[2]
    width = pair_ref.shape[1]
    even = (index_ref[2] & 1) == 0
    panels_dev, double_nodes, _ = block_ref.shape
    nodes = double_nodes // 2
    slot_total = panel_ref.shape[1]
    for b in range(2):
        pair = pair_ref[b].astype(jnp.float32)
        following = next_ref[b].astype(jnp.float32)
        line_ref[b, :width, :] = jnp.where(even, following, pair).astype(jnp.bfloat16)
        line_ref[b, width : width + point_count, :] = own_ref[0, b]
        line_ref[b, width + point_count :, :] = jnp.where(even, pair, following).astype(
            jnp.bfloat16
        )
    first_panel = index_ref[2] * panels_dev
    lane = lax.broadcasted_iota(jnp.int32, block_ref.shape[1:], 1)
    for p in range(panels_dev):
        for k in range(slot_total):
            first = pl.multiple_of((panel_ref[p, k] - first_panel) * nodes + width, 16)
            for b in range(2):
                row = (k * 2 + b) * nodes
                gathered_ref[p, row : row + nodes, :] = line_ref[b, pl.ds(first, nodes), :]
        blocks = jnp.where(
            lane < count_ref[p] * double_nodes, block_ref[p].astype(jnp.float32), 0.0
        ).astype(jnp.bfloat16)
        near = dot16(blocks, gathered_ref[p])
        for a in range(2):
            rows = slice(p * nodes, (p + 1) * nodes)
            own = own_ref[0, a, rows, :].astype(jnp.float32)
            out_ref[a, rows, :] = 0.5 * own + near[a * nodes : (a + 1) * nodes, :]


def spread(full_ref, outs, own):
    rows = outs[0].shape[1]
    for k in range(len(outs) * outs[0].shape[0]):
        first = pl.multiple_of((own ^ k) * rows, 8)
        outs[k % len(outs)][k // len(outs)] = full_ref[pl.ds(first, rows), :]


def collect(order, parts, full_ref, own, start):
    rows = full_ref.shape[0] // len(order)
    for k, offset in enumerate(order):
        first = pl.multiple_of((own ^ offset) * rows, 8)
        ref, row = part_at(parts, k)
        full_ref[pl.ds(first, rows), :] = ref[row, start : start + rows, :]


def stacked(basis_ref):
    return jnp.concatenate(
        [
            jnp.concatenate([basis_ref[j, a] for j in range(basis_ref.shape[0])], axis=1)
            for a in range(2)
        ],
        axis=0,
    )


def project_kernel(masks, ways, index_ref, half_hbm, weight_ref, basis_ref, base_ref, *refs):
    arrived = refs[: len(refs) - ways - 2]
    image_ref = refs[len(arrived)]
    outs = refs[len(arrived) + 1 : -1]
    full_ref = refs[-1]
    weighted = []
    for a in range(2):
        image = base_ref[a] + total_of([part[0, a] for part in arrived])
        image_ref[a] = image
        weighted.append(image * weight_ref[...])
    image = jnp.concatenate([image_ref[0], image_ref[1]], axis=0)
    left = jnp.concatenate([stacked(basis_ref), image], axis=1)
    full_ref[...] = dot_first(left, jnp.concatenate(weighted, axis=0))
    spread(full_ref, outs, bits_of(index_ref[2], masks))


def factor_kernel(gather, masks, index_ref, basis_ref, image_ref, *refs):
    parts = refs[:-7]
    hess_ref, upper_ref, new_ref, full_ref, half_ref, work_ref, inverse_ref = refs[-7:]
    block_total, _, _, order = basis_ref.shape
    hess_rows = block_total * order
    tile = (ROWS, order)
    lane = lax.broadcasted_iota(jnp.int32, tile, 1)
    row = lax.broadcasted_iota(jnp.int32, tile, 0)
    own = bits_of(index_ref[2], masks)
    collect(gather, parts, full_ref, own, 0)
    collect(gather, parts, half_ref, own, full_ref.shape[0] // len(gather))
    hessenberg = full_ref[:hess_rows, :]
    hess_ref[...] = hessenberg
    rows = []
    number = 0
    for i in range(block_total):
        count = block_total - i
        left = jnp.concatenate(
            [
                half_ref[(number + j) * order : (number + j + 1) * order, :]
                for j in range(count)
            ],
            axis=1,
        )
        rows.append(dot_rows(left, full_ref[i * order : hess_rows, :]))
        number += count
    product = dot_first(hessenberg, jnp.concatenate(rows, axis=0) - hessenberg)
    work_ref[...] = full_ref[hess_rows:, :] + (product + jnp.transpose(product))
    for block in range(order // ROWS):
        start = block * ROWS
        inverse_ref[start : start + ROWS, :] = jnp.where(lane == row + start, 1.0, 0.0)
    for block in range(order // ROWS):
        start = block * ROWS
        own = work_ref[start : start + ROWS, :]
        own_inverse = inverse_ref[start : start + ROWS, :]
        columns = [
            jnp.broadcast_to(own[:, start + m : start + m + 1], tile) for m in range(ROWS)
        ]
        entry = {
            (j, m): jnp.broadcast_to(columns[m][j : j + 1, :], tile)
            for m in range(ROWS)
            for j in range(m, ROWS)
        }
        scale = []
        for m in range(ROWS):
            scale.append(lax.rsqrt(entry[m, m]))
            for j in range(m + 1, ROWS):
                entry[j, m] = entry[j, m] * scale[m]
            for n in range(m + 1, ROWS):
                for j in range(n, ROWS):
                    entry[j, n] = entry[j, n] - entry[j, m] * entry[n, m]
        solved = []
        solved_inverse = []
        for m in range(ROWS):
            upper_row = jnp.broadcast_to(own[m : m + 1, :], tile)
            inverse_row = jnp.broadcast_to(own_inverse[m : m + 1, :], tile)
            for j in range(m):
                upper_row = upper_row - entry[m, j] * solved[j]
                inverse_row = inverse_row - entry[m, j] * solved_inverse[j]
            upper_row = upper_row * scale[m]
            inverse_row = inverse_row * scale[m]
            solved.append(upper_row)
            solved_inverse.append(inverse_row)
        upper_rows = solved[ROWS - 1]
        inverse_rows = solved_inverse[ROWS - 1]
        for m in range(ROWS - 1):
            upper_rows = jnp.where(row == m, solved[m], upper_rows)
            inverse_rows = jnp.where(row == m, solved_inverse[m], inverse_rows)
        upper_ref[start : start + ROWS, :] = jnp.where(lane >= row + start, upper_rows, 0.0)
        inverse_ref[start : start + ROWS, :] = inverse_rows
        for later in range(block + 1, order // ROWS):
            first = later * ROWS
            target = work_ref[first : first + ROWS, :]
            target_inverse = inverse_ref[first : first + ROWS, :]
            multiplier = []
            for m in range(ROWS):
                value = jnp.broadcast_to(target[:, start + m : start + m + 1], tile)
                for j in range(m):
                    value = value - multiplier[j] * entry[m, j]
                multiplier.append(value * scale[m])
            for m in range(ROWS):
                target = target - multiplier[m] * solved[m]
                target_inverse = target_inverse - multiplier[m] * solved_inverse[m]
            work_ref[first : first + ROWS, :] = target
            inverse_ref[first : first + ROWS, :] = target_inverse
    image = jnp.concatenate([image_ref[0], image_ref[1]], axis=0)
    remainder = image - dot_rows(stacked(basis_ref), hessenberg)
    new_ref[...] = dot_rows(remainder, inverse_ref[...], ((1,), (1,)))


def f32(*shape):
    return jax.ShapeDtypeStruct(shape, jnp.float32)


def b16(*shape):
    return jax.ShapeDtypeStruct(shape, jnp.bfloat16)


def call(kernel, out_shape, operands, scalars=0, scratch=(), in_hbm=0):
    many = isinstance(out_shape, (tuple, list))
    free = len(operands) - in_hbm
    operands = list(operands[:free]) + [
        pltpu.with_memory_space_constraint(x, pltpu.HBM) for x in operands[free:]
    ]
    return pl.pallas_call(
        kernel,
        out_shape=out_shape,
        in_specs=[SMEM] * scalars + [ANY if in_hbm else VMEM] * (len(operands) - scalars),
        out_specs=[VMEM] * len(out_shape) if many else VMEM,
        scratch_shapes=list(scratch),
        compiler_params=PARAMS,
    )(*operands)


def body(
    points,
    quad_weight,
    basis,
    jacobi,
    near_panel,
    near_count,
    near_block,
    agg_index,
    coarse_inverse,
):
    block_total, _, point_count, rhs_count = basis.shape
    coarse_count = coarse_inverse.shape[1]
    narrow_count = lax.axis_size("narrow")
    wide_count = lax.axis_size("wide")
    panels_dev, slot_total = near_panel.shape
    nodes = near_block.shape[2] // 2
    width = SPAN * nodes
    pack_rows = coarse_count + EXTRA
    index = jnp.stack(
        [lax.axis_index("narrow"), lax.axis_index("wide"), lax.axis_index(AXES)]
    ).astype(jnp.int32)
    weight_row = quad_weight[None, :]
    low, *high = masks_of(wide_count)
    core, *across = masks_of(narrow_count, wide_count)
    high_groups = in_pairs(high)
    plane_groups = in_pairs([low] + across)
    wide_groups = high_groups + [[low]]
    narrow_groups = [[core]] + in_pairs(across)
    source_groups = high_groups + [[core]]
    high_count = 1 << len(high)
    source_total = 2 * high_count * point_count
    target_count = narrow_count
    pair_row = pltpu.VMEM((2, point_count), jnp.float32)
    one_row = pltpu.VMEM((1, point_count), jnp.float32)
    pair_index = pltpu.VMEM((2, point_count), jnp.int32)
    field = pltpu.VMEM((2, point_count, rhs_count), jnp.float32)

    pack = call(
        restrict_kernel,
        f32(1, pack_rows, point_count),
        (agg_index, basis, points, weight_row),
        0,
        [pair_index, field, pair_row, one_row, pltpu.SemaphoreType.DMA((4,))],
        4,
    )
    half_rows = block_total * (block_total + 1) // 2 * rhs_count
    halving = [[core]] + plane_groups
    masks = [core, low] + across
    inverse, member, smooth, weight, *half_parts = call(
        functools.partial(prefetch_kernel, masks),
        [
            f32(*coarse_inverse.shape),
            f32(2, coarse_count, point_count),
            f32(2, point_count, rhs_count),
            f32(point_count, rhs_count),
        ]
        + [f32(narrow_count, half_rows // (2 * narrow_count), rhs_count)] * 2,
        (index, pack, agg_index, basis, jacobi, weight_row, coarse_inverse),
        1,
        [
            pltpu.VMEM((half_rows, rhs_count), jnp.float32),
            pair_index,
            pltpu.VMEM(basis.shape, jnp.float32),
            pair_row,
            one_row,
            pltpu.SemaphoreType.DMA((5,)),
        ],
        5,
    )
    near_rows = jnp.transpose(near_block, (0, 2, 1, 3)).reshape(
        panels_dev, 2 * nodes, slot_total * 2 * nodes
    )
    packs = flip_each([pack] * (1 << len(wide_groups[0])), wide_groups[0])
    pack = join(packs, (weight,))
    half_send = join(half_parts[1:], (pack,))
    packs = gather_steps(pack, wide_groups[1:])
    source_rows = high_count * EXTRA // (narrow_count // 2)
    target_rows = 2 * EXTRA
    coarse_outs = pl.pallas_call(
        functools.partial(
            coarse_kernel, gather_order(wide_groups), 2, high_count
        ),
        out_shape=[f32(narrow_count // 2, coarse_count + source_rows, rhs_count)] * 2
        + [f32(high_count, EXTRA, point_count), f32(2, EXTRA, point_count)],
        in_specs=[SMEM, ANY, VMEM] + [VMEM] * len(packs),
        out_specs=[VMEM] * 4,
        scratch_shapes=[pltpu.VMEM((wide_count * coarse_count, rhs_count), jnp.float32)],
        compiler_params=PARAMS,
    )(index, near_rows, inverse, *packs)
    own_sources = coarse_outs[2]
    kept, got = flip_each(coarse_outs[:2], [core])
    groups = in_pairs(across)
    ways = 1 << len(groups[0])
    *coarse_parts, other_sources = call(
        functools.partial(coarse_sum_kernel, ways),
        [f32(narrow_count // 2 // ways, coarse_count + target_rows, rhs_count)] * ways
        + [f32(high_count, EXTRA, point_count)],
        (kept, got, coarse_outs[3]),
    )
    half_parts = flip_each([half_parts[0], half_send], [core])
    half_parts = sum_parts(half_parts, 2)
    half_steps = []
    for number, mask in enumerate([low] + across + high):
        got = flip_each(half_parts, [mask])
        half_steps.append(got[1])
        half_parts = sum_parts(got, 2 if number < len(across) else 1)
        if len(half_parts) == 1:
            half_parts = half_parts * 2
    half_total = half_parts[0]
    coarse_parts = scatter_steps(coarse_parts, groups)
    precond, pair_edge, next_edge = pl.pallas_call(
        precond_kernel,
        out_shape=[b16(1, 2, point_count, rhs_count)] + [b16(2, width, rhs_count)] * 2,
        in_specs=[SMEM, ANY] + [VMEM] * (2 + len(coarse_parts)),
        out_specs=[VMEM] * 3,
        compiler_params=PARAMS,
    )(index, half_steps[0], member, smooth, *coarse_parts)
    matrix_spec = pl.BlockSpec((1, 3, point_count, source_total), lambda k: (k, 0, 0, 0))
    matrix = pl.pallas_call(
        functools.partial(matrix_kernel, coarse_count),
        out_shape=b16(target_count, 3, point_count, source_total),
        grid=(target_count,),
        in_specs=[VMEM] * (2 + len(coarse_parts)),
        out_specs=matrix_spec,
        compiler_params=PARAMS,
    )(own_sources, other_sources, *coarse_parts)
    device_count = narrow_count * wide_count
    pair_edge = flip(pair_edge, 1)
    pairs = [(i, i + 1) for i in range(1, device_count - 1, 2)]
    next_edge = lax.ppermute(next_edge, AXES, pairs + [(j, i) for i, j in pairs])
    fields = flip_each([precond] * (1 << len(source_groups[0])), source_groups[0])
    after = (matrix, half_steps[1], next_edge)
    fields = gather_steps(join(fields, after), source_groups[1:])

    ways = 1 << len(plane_groups[0])
    far_parts = []
    for number, field in enumerate(fields):
        far_parts = pl.pallas_call(
            functools.partial(far_kernel, ways),
            out_shape=[f32(target_count // ways, 2, point_count, rhs_count)] * ways,
            grid=(target_count,),
            in_specs=[
                pl.BlockSpec(
                    (1, 3, point_count, source_total // 2),
                    lambda k, number=number: (k, 0, 0, number),
                )
            ]
            + [VMEM] * (1 + len(far_parts)),
            out_specs=[VMEM] * ways,
            scratch_shapes=[pltpu.VMEM((source_total // 2, 2 * rhs_count), jnp.bfloat16)],
            compiler_params=PARAMS,
        )(matrix, field, *far_parts)
    far_parts = scatter_steps(far_parts, plane_groups)
    base = call(
        near_kernel,
        f32(2, point_count, rhs_count),
        (index, near_panel, near_count, near_rows, precond, pair_edge, next_edge),
        3,
        [
            pltpu.VMEM((2, 2 * width + point_count, rhs_count), jnp.bfloat16),
            pltpu.VMEM((panels_dev, slot_total * 2 * nodes, rhs_count), jnp.bfloat16),
        ],
    )

    hess_rows = block_total * rhs_count
    sum_rows = hess_rows + rhs_count
    image, *parts = pl.pallas_call(
        functools.partial(project_kernel, masks, 2),
        out_shape=[f32(2, point_count, rhs_count)]
        + [f32(narrow_count, sum_rows // (2 * narrow_count), rhs_count)] * 2,
        in_specs=[SMEM] + [ANY] + [VMEM] * (3 + len(far_parts)),
        out_specs=[VMEM] * 3,
        scratch_shapes=[pltpu.VMEM((sum_rows, rhs_count), jnp.float32)],
        compiler_params=PARAMS,
    )(index, half_steps[2], weight, basis, base, *far_parts)
    (total,) = sum_parts(scatter_steps(parts, halving), 1, half_steps[3:4])
    total = sum_butterfly(total, high_groups)
    parts = gather_steps(append(total, half_total), halving[::-1])
    hessenberg, upper_factor, new_block = call(
        functools.partial(factor_kernel, gather_order(part_groups(halving)[::-1]), masks),
        [
            f32(hess_rows, rhs_count),
            f32(rhs_count, rhs_count),
            f32(2 * point_count, rhs_count),
        ],
        (index, basis, image, *parts),
        1,
        [
            pltpu.VMEM((sum_rows, rhs_count), jnp.float32),
            pltpu.VMEM((half_rows, rhs_count), jnp.float32),
        ]
        + [pltpu.VMEM((rhs_count, rhs_count), jnp.float32)] * 2,
    )
    return (
        new_block.reshape(2, point_count, rhs_count),
        hessenberg.reshape(block_total, rhs_count, rhs_count),
        upper_factor,
    )


def solution(mesh):
    in_specs = (
        P(None, ("narrow", "wide")),
        P(("narrow", "wide")),
        P(None, None, ("narrow", "wide"), None),
        P(None, ("narrow", "wide")),
        P(("narrow", "wide"), None),
        P(("narrow", "wide")),
        P(("narrow", "wide"), None, None, None),
        P(None, ("narrow", "wide")),
        P(None, "wide", "narrow"),
    )
    out_specs = (P(None, ("narrow", "wide"), None), P(), P())
    return jax.shard_map(body, mesh=mesh, in_specs=in_specs, out_specs=out_specs, check_vma=False)
```

```python
import functools

import jax
import jax.numpy as jnp
from jax import lax
from jax.experimental import pallas as pl
from jax.experimental.pallas import tpu as pltpu
from jax.sharding import PartitionSpec as P

SPAN = 4


NU = 0.3
DELTA2 = 1e-05
ELASTIC = 40.0
AXES = ("narrow", "wide")
EXTRA = 8
ROWS = 8
SMEM = pl.BlockSpec(memory_space=pltpu.SMEM)
VMEM = pl.BlockSpec(memory_space=pltpu.VMEM)
ANY = pl.BlockSpec(memory_space=pl.ANY)
PARAMS = pltpu.CompilerParams(vmem_limit_bytes=48 * 1024 * 1024)


def split(value):
    high = value.astype(jnp.bfloat16)
    return high, (value - high.astype(jnp.float32)).astype(jnp.bfloat16)


def dot16(left, right, contract=((1,), (0,))):
    return lax.dot_general(left, right, (contract, ((), ())), preferred_element_type=jnp.float32)


def dot_rows(left, right, contract=((1,), (0,))):
    left_high, left_low = split(left)
    right_high, right_low = split(right)
    return dot16(left_high, right_high, contract) + (
        dot16(left_high, right_low, contract) + dot16(left_low, right_high, contract)
    )


def dot_first(left, right):
    return dot_rows(left, right, ((0,), (0,)))


def pick(member, value, contract=((1,), (0,))):
    member = member.astype(jnp.bfloat16)
    high, low = split(value)
    lowest = (value - high.astype(jnp.float32) - low.astype(jnp.float32)).astype(jnp.bfloat16)
    return dot16(member, high, contract) + (
        dot16(member, low, contract) + dot16(member, lowest, contract)
    )


def as_column(row, width):
    return jnp.transpose(jnp.broadcast_to(row, (width, row.shape[1])))


def flip(block, mask):
    count = lax.axis_size(AXES)
    return lax.ppermute(block, AXES, [(i, i ^ mask) for i in range(count)])


def masks_of(count, scale=1):
    return [scale << bit for bit in range(count.bit_length() - 1)]


def in_pairs(masks):
    return [masks[k : k + 2] for k in range(0, len(masks), 2)]


def combined(group, number):
    mask = 0
    for bit, part in enumerate(group):
        if number >> bit & 1:
            mask ^= part
    return mask


def flip_each(parts, group):
    return [parts[0]] + [flip(parts[j], combined(group, j)) for j in range(1, 1 << len(group))]


def farthest_first(parts):
    return [parts[0], *parts[:0:-1]]


def join_kernel(count, *refs):
    parts, out_ref = farthest_first(refs[-1 - count : -1]), refs[-1]
    size = parts[0].shape[0]
    for j, ref in enumerate(parts):
        out_ref[j * size : (j + 1) * size] = ref[...]


def join(parts, after=()):
    shape = (len(parts) * parts[0].shape[0],) + parts[0].shape[1:]
    return pl.pallas_call(
        functools.partial(join_kernel, len(parts)),
        out_shape=jax.ShapeDtypeStruct(shape, parts[0].dtype),
        in_specs=[ANY] * len(after) + [VMEM] * len(parts),
        out_specs=VMEM,
        compiler_params=PARAMS,
    )(*after, *farthest_first(parts))


def gather_steps(held, groups, after=()):
    parts = [held]
    for group in groups:
        if len(parts) > 1:
            held = join(parts, after)
            after = ()
        parts = flip_each([held] * (1 << len(group)), group)
    return parts


def gather_order(groups):
    order = [0]
    for group in groups:
        order = [k ^ combined(group, j) for j in range(1 << len(group)) for k in order]
    return order


def total_of(values):
    while len(values) > 1:
        values = [values[k] + values[k + 1] for k in range(0, len(values), 2)]
    return values[0]


def sum_kernel(count, skip, *refs):
    parts, outs = refs[skip : skip + count], refs[skip + count :]
    for k in range(outs[0].shape[0]):
        for j, out_ref in enumerate(outs):
            out_ref[k] = total_of([part[k * len(outs) + j] for part in parts])


def sum_parts(parts, ways, after=()):
    out = f32(parts[0].shape[0] // ways, *parts[0].shape[1:])
    return pl.pallas_call(
        functools.partial(sum_kernel, len(parts), len(after)),
        out_shape=[out] * ways,
        in_specs=[ANY] * len(after) + [VMEM] * len(parts),
        out_specs=[VMEM] * ways,
        compiler_params=PARAMS,
    )(*after, *farthest_first(parts))


def scatter_steps(parts, groups):
    for number, group in enumerate(groups):
        if number:
            parts = sum_parts(parts, 1 << len(group))
        parts = flip_each(parts, group)
    return parts


def sum_butterfly(total, groups):
    for group in groups:
        (total,) = sum_parts(flip_each([total] * (1 << len(group)), group), 1)
    return total


def append_kernel(left_ref, right_ref, out_ref):
    rows = left_ref.shape[1]
    out_ref[:, :rows, :] = left_ref[...]
    out_ref[:, rows:, :] = right_ref[...]


def append(left, right):
    count, rows, width = left.shape
    shape = f32(count, rows + right.shape[1], width)
    return call(append_kernel, shape, (left, right))


def part_groups(groups):
    bit, found = 0, []
    for group in groups:
        found.append([1 << (bit + k) for k in range(len(group))])
        bit += len(group)
    return found


def bits_of(index, masks):
    packed = 0
    for bit, mask in enumerate(masks):
        packed = packed + (lax.shift_right_logical(index, mask.bit_length() - 1) & 1) * (1 << bit)
    return packed


def members(agg_ref, a, coarse_count):
    ids = lax.broadcasted_iota(jnp.int32, (coarse_count, agg_ref.shape[1]), 0)
    return jnp.where(ids == agg_ref[a : a + 1, :], 1.0, 0.0)


def load_all(pairs, sems):
    copies = [
        pltpu.make_async_copy(source, target, sems.at[k])
        for k, (source, target) in enumerate(pairs)
    ]
    for copy in copies:
        copy.start()
    for copy in copies:
        copy.wait()


def restrict_kernel(
    agg_hbm, basis_hbm, points_hbm, weight_hbm, pack_ref, agg_ref, newest_ref, points_ref, weight_ref, sems
):
    coarse_count = pack_ref.shape[1] - EXTRA
    point_count = newest_ref.shape[1]
    load_all(
        [
            (basis_hbm.at[basis_hbm.shape[0] - 1], newest_ref),
            (agg_hbm, agg_ref),
            (points_hbm, points_ref),
            (weight_hbm, weight_ref),
        ],
        sems,
    )
    total = pick(members(agg_ref, 0, coarse_count), newest_ref[0]) + pick(
        members(agg_ref, 1, coarse_count), newest_ref[1]
    )
    pack_ref[0, :coarse_count, :] = total
    pack_ref[0, coarse_count:, :] = jnp.concatenate(
        [points_ref[...], weight_ref[...], jnp.zeros((EXTRA - 3, point_count), jnp.float32)], axis=0
    )


def prefetch_kernel(
    masks,
    index_ref,
    pack_hbm,
    agg_hbm,
    basis_hbm,
    jacobi_hbm,
    weight_hbm,
    inverse_hbm,
    inverse_ref,
    member_ref,
    smooth_ref,
    weight_out_ref,
    keep_ref,
    send_ref,
    half_ref,
    agg_ref,
    basis_ref,
    jacobi_ref,
    weight_ref,
    sems,
):
    coarse_count = member_ref.shape[1]
    block_total, _, _, rhs_count = basis_ref.shape
    load_all(
        [
            (basis_hbm, basis_ref),
            (agg_hbm, agg_ref),
            (jacobi_hbm, jacobi_ref),
            (weight_hbm, weight_ref),
            (inverse_hbm, inverse_ref),
        ],
        sems,
    )
    for a in range(2):
        member_ref[a] = members(agg_ref, a, coarse_count)
        smooth_ref[a] = (
            as_column(jacobi_ref[a : a + 1, :], rhs_count) * basis_ref[block_total - 1, a]
        )
    weight = as_column(weight_ref[...], rhs_count)
    weight_out_ref[...] = weight
    right = stacked(basis_ref)
    number = 0
    for i in range(block_total):
        left = jnp.concatenate([basis_ref[i, a] * weight for a in range(2)], axis=0)
        row = dot_first(left, right[:, i * rhs_count :])
        for j in range(i, block_total):
            block = row[:, (j - i) * rhs_count : (j - i + 1) * rhs_count]
            rows = slice(number * rhs_count, (number + 1) * rhs_count)
            half_ref[rows, :] = block * 0.5 if i == j else block
            number += 1
    spread(half_ref, (keep_ref, send_ref), bits_of(index_ref[2], masks))


def part_at(parts, k):
    size = parts[0].shape[0]
    return parts[k // size], k % size


def coarse_kernel(order, ways, z_count, index_ref, near_ref, inverse_ref, *refs):
    narrow_count, coarse_count, _ = inverse_ref.shape
    packs = refs[: len(refs) - ways - 3]
    outs = refs[len(packs) : len(packs) + ways]
    source_ref, target_ref, rhs_ref = refs[len(packs) + ways :]
    for k, offset in enumerate(order):
        first = pl.multiple_of((index_ref[1] ^ offset) * coarse_count, 8)
        ref, row = part_at(packs, k)
        rhs_ref[pl.ds(first, coarse_count), :] = ref[row, :coarse_count, :]
    for k in range(z_count):
        ref, row = part_at(packs, k)
        source_ref[k] = ref[row, coarse_count:, :]
    for k in range(target_ref.shape[0]):
        ref, row = part_at(packs, k * z_count)
        target_ref[k] = ref[row, coarse_count:, :]
    left = jnp.concatenate(
        [inverse_ref[index_ref[0] ^ k] for k in range(narrow_count)], axis=0
    )
    product = dot_rows(left, rhs_ref[...])
    tail = jnp.concatenate([source_ref[k] for k in range(z_count)], axis=0)
    each = z_count * EXTRA // (narrow_count // ways)
    for k in range(narrow_count):
        part = product[k * coarse_count : (k + 1) * coarse_count, :]
        outs[k % ways][k // ways, :coarse_count, :] = part
        first = (k // ways) * each
        outs[k % ways][k // ways, coarse_count:, :] = tail[first : first + each, :]


def coarse_sum_kernel(ways, kept_ref, got_ref, target_ref, *refs):
    outs, source_ref = refs[:ways], refs[ways]
    rows = target_ref.shape[0] * EXTRA
    coarse_count = outs[0].shape[1] - rows
    each = (kept_ref.shape[1] - coarse_count) // EXTRA
    for k in range(kept_ref.shape[0]):
        for j in range(each):
            first = coarse_count + j * EXTRA
            source_ref[k * each + j] = got_ref[k, first : first + EXTRA, :]
    for k in range(outs[0].shape[0]):
        for j in range(ways):
            source = k * ways + j
            outs[j][k, :coarse_count, :] = (
                kept_ref[source, :coarse_count, :] + got_ref[source, :coarse_count, :]
            )
            for t in range(target_ref.shape[0]):
                first = coarse_count + t * EXTRA
                outs[j][k, first : first + EXTRA, :] = target_ref[t]


def precond_kernel(index_ref, half_hbm, member_ref, smooth_ref, *refs):
    parts = refs[:-3]
    precond_ref, pair_ref, next_ref = refs[-3:]
    coarse_count = member_ref.shape[1]
    point_count = smooth_ref.shape[1]
    width = pair_ref.shape[1]
    even = (index_ref[2] & 1) == 0
    coarse_sol = total_of([part[0, :coarse_count, :] for part in parts])
    for a in range(2):
        value = smooth_ref[a] + pick(member_ref[a], coarse_sol, ((0,), (0,)))
        precond_ref[0, a] = value.astype(jnp.bfloat16)
        first = value[:width]
        last = value[point_count - width :]
        pair_ref[a] = jnp.where(even, last, first).astype(jnp.bfloat16)
        next_ref[a] = jnp.where(even, first, last).astype(jnp.bfloat16)


def matrix_kernel(coarse_count, own_ref, other_ref, *refs):
    targets, matrix_ref = refs[:-1], refs[-1]
    point_count = own_ref.shape[2]
    size = (targets[0].shape[1] - coarse_count) // EXTRA
    step = pl.program_id(0)
    first = pl.multiple_of(coarse_count + lax.rem(step, size) * EXTRA, EXTRA)
    target = targets[0][0, pl.ds(first, EXTRA), :]
    for j in range(1, len(targets)):
        target = jnp.where(step // size == j, targets[j][0, pl.ds(first, EXTRA), :], target)
    target_x = as_column(target[0:1, :], point_count)
    target_y = as_column(target[1:2, :], point_count)
    for s in range(matrix_ref.shape[3] // point_count):
        ref, row = part_at((own_ref, other_ref), s)
        source = ref[row]
        delta_x = target_x - source[0:1, :]
        delta_y = target_y - source[1:2, :]
        factor = ELASTIC * source[2:3, :]
        square_x = delta_x * delta_x
        square_y = delta_y * delta_y
        square_dist = square_x + square_y + DELTA2
        inverse = 1.0 / square_dist
        log_part = (-0.5 * (3.0 - 4.0 * NU)) * jnp.log(square_dist)
        lanes = slice(s * point_count, (s + 1) * point_count)
        matrix_ref[0, 0, :, lanes] = (factor * (log_part + square_x * inverse)).astype(jnp.bfloat16)
        matrix_ref[0, 1, :, lanes] = (factor * (delta_x * delta_y * inverse)).astype(jnp.bfloat16)
        matrix_ref[0, 2, :, lanes] = (factor * (log_part + square_y * inverse)).astype(jnp.bfloat16)


def far_kernel(ways, matrix_ref, field_ref, *refs):
    earlier, outs, fields_ref = refs[: -1 - ways], refs[-1 - ways : -1], refs[-1]
    point_count, rhs_count = field_ref.shape[2:]
    step = pl.program_id(0)

    @pl.when(step == 0)
    def _():
        for s in range(field_ref.shape[0]):
            for b in range(2):
                rows = slice(s * point_count, (s + 1) * point_count)
                fields_ref[rows, b * rhs_count : (b + 1) * rhs_count] = field_ref[s, b]

    mixed = dot16(matrix_ref[0, 1], fields_ref[...])
    out_x = dot16(matrix_ref[0, 0], fields_ref[:, :rhs_count]) + mixed[:, rhs_count:]
    out_y = dot16(matrix_ref[0, 2], fields_ref[:, rhs_count:]) + mixed[:, :rhs_count]
    for j, out_ref in enumerate(outs):

        @pl.when(lax.rem(step, ways) == j)
        def _(j=j, out_ref=out_ref):
            row = step // ways
            if earlier:
                out_ref[row, 0] = out_x + earlier[j][row, 0]
                out_ref[row, 1] = out_y + earlier[j][row, 1]
            else:
                out_ref[row, 0] = out_x
                out_ref[row, 1] = out_y


def near_kernel(
    index_ref,
    panel_ref,
    count_ref,
    block_ref,
    own_ref,
    pair_ref,
    next_ref,
    out_ref,
    line_ref,
    gathered_ref,
):
    point_count = own_ref.shape[2]
    width = pair_ref.shape[1]
    even = (index_ref[2] & 1) == 0
    panels_dev, double_nodes, _ = block_ref.shape
    nodes = double_nodes // 2
    slot_total = panel_ref.shape[1]
    for b in range(2):
        pair = pair_ref[b].astype(jnp.float32)
        following = next_ref[b].astype(jnp.float32)
        line_ref[b, :width, :] = jnp.where(even, following, pair).astype(jnp.bfloat16)
        line_ref[b, width : width + point_count, :] = own_ref[0, b]
        line_ref[b, width + point_count :, :] = jnp.where(even, pair, following).astype(
            jnp.bfloat16
        )
    first_panel = index_ref[2] * panels_dev
    lane = lax.broadcasted_iota(jnp.int32, block_ref.shape[1:], 1)
    for p in range(panels_dev):
        for k in range(slot_total):
            first = pl.multiple_of((panel_ref[p, k] - first_panel) * nodes + width, 16)
            for b in range(2):
                row = (k * 2 + b) * nodes
                gathered_ref[p, row : row + nodes, :] = line_ref[b, pl.ds(first, nodes), :]
        blocks = jnp.where(
            lane < count_ref[p] * double_nodes, block_ref[p].astype(jnp.float32), 0.0
        ).astype(jnp.bfloat16)
        near = dot16(blocks, gathered_ref[p])
        for a in range(2):
            rows = slice(p * nodes, (p + 1) * nodes)
            own = own_ref[0, a, rows, :].astype(jnp.float32)
            out_ref[a, rows, :] = 0.5 * own + near[a * nodes : (a + 1) * nodes, :]


def spread(full_ref, outs, own):
    rows = outs[0].shape[1]
    for k in range(len(outs) * outs[0].shape[0]):
        first = pl.multiple_of((own ^ k) * rows, 8)
        outs[k % len(outs)][k // len(outs)] = full_ref[pl.ds(first, rows), :]


def collect(order, parts, full_ref, own, start):
    rows = full_ref.shape[0] // len(order)
    for k, offset in enumerate(order):
        first = pl.multiple_of((own ^ offset) * rows, 8)
        ref, row = part_at(parts, k)
        full_ref[pl.ds(first, rows), :] = ref[row, start : start + rows, :]


def stacked(basis_ref):
    return jnp.concatenate(
        [
            jnp.concatenate([basis_ref[j, a] for j in range(basis_ref.shape[0])], axis=1)
            for a in range(2)
        ],
        axis=0,
    )


def project_kernel(masks, ways, index_ref, half_hbm, weight_ref, basis_ref, base_ref, *refs):
    arrived = refs[: len(refs) - ways - 2]
    image_ref = refs[len(arrived)]
    outs = refs[len(arrived) + 1 : -1]
    full_ref = refs[-1]
    weighted = []
    for a in range(2):
        image = base_ref[a] + total_of([part[0, a] for part in arrived])
        image_ref[a] = image
        weighted.append(image * weight_ref[...])
    image = jnp.concatenate([image_ref[0], image_ref[1]], axis=0)
    left = jnp.concatenate([stacked(basis_ref), image], axis=1)
    full_ref[...] = dot_first(left, jnp.concatenate(weighted, axis=0))
    spread(full_ref, outs, bits_of(index_ref[2], masks))


def factor_kernel(gather, masks, index_ref, basis_ref, image_ref, *refs):
    parts = refs[:-7]
    hess_ref, upper_ref, new_ref, full_ref, half_ref, work_ref, inverse_ref = refs[-7:]
    block_total, _, _, order = basis_ref.shape
    hess_rows = block_total * order
    tile = (ROWS, order)
    lane = lax.broadcasted_iota(jnp.int32, tile, 1)
    row = lax.broadcasted_iota(jnp.int32, tile, 0)
    own = bits_of(index_ref[2], masks)
    collect(gather, parts, full_ref, own, 0)
    collect(gather, parts, half_ref, own, full_ref.shape[0] // len(gather))
    hessenberg = full_ref[:hess_rows, :]
    hess_ref[...] = hessenberg
    rows = []
    number = 0
    for i in range(block_total):
        count = block_total - i
        left = jnp.concatenate(
            [
                half_ref[(number + j) * order : (number + j + 1) * order, :]
                for j in range(count)
            ],
            axis=1,
        )
        rows.append(dot_rows(left, full_ref[i * order : hess_rows, :]))
        number += count
    product = dot_first(hessenberg, jnp.concatenate(rows, axis=0) - hessenberg)
    work_ref[...] = full_ref[hess_rows:, :] + (product + jnp.transpose(product))
    for block in range(order // ROWS):
        start = block * ROWS
        inverse_ref[start : start + ROWS, :] = jnp.where(lane == row + start, 1.0, 0.0)
    for block in range(order // ROWS):
        start = block * ROWS
        own = work_ref[start : start + ROWS, :]
        own_inverse = inverse_ref[start : start + ROWS, :]
        columns = [
            jnp.broadcast_to(own[:, start + m : start + m + 1], tile) for m in range(ROWS)
        ]
        entry = {
            (j, m): jnp.broadcast_to(columns[m][j : j + 1, :], tile)
            for m in range(ROWS)
            for j in range(m, ROWS)
        }
        scale = []
        for m in range(ROWS):
            scale.append(lax.rsqrt(entry[m, m]))
            for j in range(m + 1, ROWS):
                entry[j, m] = entry[j, m] * scale[m]
            for n in range(m + 1, ROWS):
                for j in range(n, ROWS):
                    entry[j, n] = entry[j, n] - entry[j, m] * entry[n, m]
        solved = []
        solved_inverse = []
        for m in range(ROWS):
            upper_row = jnp.broadcast_to(own[m : m + 1, :], tile)
            inverse_row = jnp.broadcast_to(own_inverse[m : m + 1, :], tile)
            for j in range(m):
                upper_row = upper_row - entry[m, j] * solved[j]
                inverse_row = inverse_row - entry[m, j] * solved_inverse[j]
            upper_row = upper_row * scale[m]
            inverse_row = inverse_row * scale[m]
            solved.append(upper_row)
            solved_inverse.append(inverse_row)
        upper_rows = solved[ROWS - 1]
        inverse_rows = solved_inverse[ROWS - 1]
        for m in range(ROWS - 1):
            upper_rows = jnp.where(row == m, solved[m], upper_rows)
            inverse_rows = jnp.where(row == m, solved_inverse[m], inverse_rows)
        upper_ref[start : start + ROWS, :] = jnp.where(lane >= row + start, upper_rows, 0.0)
        inverse_ref[start : start + ROWS, :] = inverse_rows
        for later in range(block + 1, order // ROWS):
            first = later * ROWS
            target = work_ref[first : first + ROWS, :]
            target_inverse = inverse_ref[first : first + ROWS, :]
            multiplier = []
            for m in range(ROWS):
                value = jnp.broadcast_to(target[:, start + m : start + m + 1], tile)
                for j in range(m):
                    value = value - multiplier[j] * entry[m, j]
                multiplier.append(value * scale[m])
            for m in range(ROWS):
                target = target - multiplier[m] * solved[m]
                target_inverse = target_inverse - multiplier[m] * solved_inverse[m]
            work_ref[first : first + ROWS, :] = target
            inverse_ref[first : first + ROWS, :] = target_inverse
    image = jnp.concatenate([image_ref[0], image_ref[1]], axis=0)
    remainder = image - dot_rows(stacked(basis_ref), hessenberg)
    new_ref[...] = dot_rows(remainder, inverse_ref[...], ((1,), (1,)))


def f32(*shape):
    return jax.ShapeDtypeStruct(shape, jnp.float32)


def b16(*shape):
    return jax.ShapeDtypeStruct(shape, jnp.bfloat16)


def call(kernel, out_shape, operands, scalars=0, scratch=(), in_hbm=0):
    many = isinstance(out_shape, (tuple, list))
    free = len(operands) - in_hbm
    operands = list(operands[:free]) + [
        pltpu.with_memory_space_constraint(x, pltpu.HBM) for x in operands[free:]
    ]
    return pl.pallas_call(
        kernel,
        out_shape=out_shape,
        in_specs=[SMEM] * scalars + [ANY if in_hbm else VMEM] * (len(operands) - scalars),
        out_specs=[VMEM] * len(out_shape) if many else VMEM,
        scratch_shapes=list(scratch),
        compiler_params=PARAMS,
    )(*operands)


def body(
    points,
    quad_weight,
    basis,
    jacobi,
    near_panel,
    near_count,
    near_block,
    agg_index,
    coarse_inverse,
):
    block_total, _, point_count, rhs_count = basis.shape
    coarse_count = coarse_inverse.shape[1]
    narrow_count = lax.axis_size("narrow")
    wide_count = lax.axis_size("wide")
    panels_dev, slot_total = near_panel.shape
    nodes = near_block.shape[2] // 2
    width = SPAN * nodes
    pack_rows = coarse_count + EXTRA
    index = jnp.stack(
        [lax.axis_index("narrow"), lax.axis_index("wide"), lax.axis_index(AXES)]
    ).astype(jnp.int32)
    weight_row = quad_weight[None, :]
    low, *high = masks_of(wide_count)
    core, *across = masks_of(narrow_count, wide_count)
    high_groups = in_pairs(high)
    plane_groups = in_pairs([low] + across)
    wide_groups = high_groups + [[low]]
    narrow_groups = [[core]] + in_pairs(across)
    source_groups = high_groups + [[core]]
    high_count = 1 << len(high)
    source_total = 2 * high_count * point_count
    target_count = narrow_count
    pair_row = pltpu.VMEM((2, point_count), jnp.float32)
    one_row = pltpu.VMEM((1, point_count), jnp.float32)
    pair_index = pltpu.VMEM((2, point_count), jnp.int32)
    field = pltpu.VMEM((2, point_count, rhs_count), jnp.float32)

    pack = call(
        restrict_kernel,
        f32(1, pack_rows, point_count),
        (agg_index, basis, points, weight_row),
        0,
        [pair_index, field, pair_row, one_row, pltpu.SemaphoreType.DMA((4,))],
        4,
    )
    half_rows = block_total * (block_total + 1) // 2 * rhs_count
    halving = [[core]] + plane_groups
    masks = [core, low] + across
    inverse, member, smooth, weight, *half_parts = call(
        functools.partial(prefetch_kernel, masks),
        [
            f32(*coarse_inverse.shape),
            f32(2, coarse_count, point_count),
            f32(2, point_count, rhs_count),
            f32(point_count, rhs_count),
        ]
        + [f32(narrow_count, half_rows // (2 * narrow_count), rhs_count)] * 2,
        (index, pack, agg_index, basis, jacobi, weight_row, coarse_inverse),
        1,
        [
            pltpu.VMEM((half_rows, rhs_count), jnp.float32),
            pair_index,
            pltpu.VMEM(basis.shape, jnp.float32),
            pair_row,
            one_row,
            pltpu.SemaphoreType.DMA((5,)),
        ],
        5,
    )
    near_rows = jnp.transpose(near_block, (0, 2, 1, 3)).reshape(
        panels_dev, 2 * nodes, slot_total * 2 * nodes
    )
    packs = flip_each([pack] * (1 << len(wide_groups[0])), wide_groups[0])
    pack = join(packs, (weight,))
    half_send = join(half_parts[1:], (pack,))
    packs = gather_steps(pack, wide_groups[1:])
    source_rows = high_count * EXTRA // (narrow_count // 2)
    target_rows = 2 * EXTRA
    coarse_outs = pl.pallas_call(
        functools.partial(
            coarse_kernel, gather_order(wide_groups), 2, high_count
        ),
        out_shape=[f32(narrow_count // 2, coarse_count + source_rows, rhs_count)] * 2
        + [f32(high_count, EXTRA, point_count), f32(2, EXTRA, point_count)],
        in_specs=[SMEM, ANY, VMEM] + [VMEM] * len(packs),
        out_specs=[VMEM] * 4,
        scratch_shapes=[pltpu.VMEM((wide_count * coarse_count, rhs_count), jnp.float32)],
        compiler_params=PARAMS,
    )(index, near_rows, inverse, *packs)
    own_sources = coarse_outs[2]
    kept, got = flip_each(coarse_outs[:2], [core])
    groups = in_pairs(across)
    ways = 1 << len(groups[0])
    *coarse_parts, other_sources = call(
        functools.partial(coarse_sum_kernel, ways),
        [f32(narrow_count // 2 // ways, coarse_count + target_rows, rhs_count)] * ways
        + [f32(high_count, EXTRA, point_count)],
        (kept, got, coarse_outs[3]),
    )
    half_parts = flip_each([half_parts[0], half_send], [core])
    half_parts = sum_parts(half_parts, 2)
    half_steps = []
    for number, mask in enumerate([low] + across + high):
        got = flip_each(half_parts, [mask])
        half_steps.append(got[1])
        half_parts = sum_parts(got, 2 if number < len(across) else 1)
        if len(half_parts) == 1:
            half_parts = half_parts * 2
    half_total = half_parts[0]
    coarse_parts = scatter_steps(coarse_parts, groups)
    precond, pair_edge, next_edge = pl.pallas_call(
        precond_kernel,
        out_shape=[b16(1, 2, point_count, rhs_count)] + [b16(2, width, rhs_count)] * 2,
        in_specs=[SMEM, ANY] + [VMEM] * (2 + len(coarse_parts)),
        out_specs=[VMEM] * 3,
        compiler_params=PARAMS,
    )(index, half_steps[0], member, smooth, *coarse_parts)
    matrix_spec = pl.BlockSpec((1, 3, point_count, source_total), lambda k: (k, 0, 0, 0))
    matrix = pl.pallas_call(
        functools.partial(matrix_kernel, coarse_count),
        out_shape=b16(target_count, 3, point_count, source_total),
        grid=(target_count,),
        in_specs=[VMEM] * (2 + len(coarse_parts)),
        out_specs=matrix_spec,
        compiler_params=PARAMS,
    )(own_sources, other_sources, *coarse_parts)
    device_count = narrow_count * wide_count
    pair_edge = flip(pair_edge, 1)
    pairs = [(i, i + 1) for i in range(1, device_count - 1, 2)]
    next_edge = lax.ppermute(next_edge, AXES, pairs + [(j, i) for i, j in pairs])
    fields = flip_each([precond] * (1 << len(source_groups[0])), source_groups[0])
    after = (matrix, half_steps[1], next_edge)
    fields = gather_steps(join(fields, after), source_groups[1:])

    ways = 1 << len(plane_groups[0])
    far_parts = []
    for number, field in enumerate(fields):
        far_parts = pl.pallas_call(
            functools.partial(far_kernel, ways),
            out_shape=[f32(target_count // ways, 2, point_count, rhs_count)] * ways,
            grid=(target_count,),
            in_specs=[
                pl.BlockSpec(
                    (1, 3, point_count, source_total // 2),
                    lambda k, number=number: (k, 0, 0, number),
                )
            ]
            + [VMEM] * (1 + len(far_parts)),
            out_specs=[VMEM] * ways,
            scratch_shapes=[pltpu.VMEM((source_total // 2, 2 * rhs_count), jnp.bfloat16)],
            compiler_params=PARAMS,
        )(matrix, field, *far_parts)
    far_parts = scatter_steps(far_parts, plane_groups)
    base = call(
        near_kernel,
        f32(2, point_count, rhs_count),
        (index, near_panel, near_count, near_rows, precond, pair_edge, next_edge),
        3,
        [
            pltpu.VMEM((2, 2 * width + point_count, rhs_count), jnp.bfloat16),
            pltpu.VMEM((panels_dev, slot_total * 2 * nodes, rhs_count), jnp.bfloat16),
        ],
    )

    hess_rows = block_total * rhs_count
    sum_rows = hess_rows + rhs_count
    image, *parts = pl.pallas_call(
        functools.partial(project_kernel, masks, 2),
        out_shape=[f32(2, point_count, rhs_count)]
        + [f32(narrow_count, sum_rows // (2 * narrow_count), rhs_count)] * 2,
        in_specs=[SMEM] + [ANY] + [VMEM] * (3 + len(far_parts)),
        out_specs=[VMEM] * 3,
        scratch_shapes=[pltpu.VMEM((sum_rows, rhs_count), jnp.float32)],
        compiler_params=PARAMS,
    )(index, half_steps[2], weight, basis, base, *farthest_first(far_parts))
    (total,) = sum_parts(scatter_steps(parts, halving), 1, half_steps[3:4])
    total = sum_butterfly(total, high_groups)
    parts = gather_steps(append(total, half_total), halving[::-1])
    hessenberg, upper_factor, new_block = call(
        functools.partial(factor_kernel, gather_order(part_groups(halving)[::-1]), masks),
        [
            f32(hess_rows, rhs_count),
            f32(rhs_count, rhs_count),
            f32(2 * point_count, rhs_count),
        ],
        (index, basis, image, *parts),
        1,
        [
            pltpu.VMEM((sum_rows, rhs_count), jnp.float32),
            pltpu.VMEM((half_rows, rhs_count), jnp.float32),
        ]
        + [pltpu.VMEM((rhs_count, rhs_count), jnp.float32)] * 2,
    )
    return (
        new_block.reshape(2, point_count, rhs_count),
        hessenberg.reshape(block_total, rhs_count, rhs_count),
        upper_factor,
    )


def solution(mesh):
    in_specs = (
        P(None, ("narrow", "wide")),
        P(("narrow", "wide")),
        P(None, None, ("narrow", "wide"), None),
        P(None, ("narrow", "wide")),
        P(("narrow", "wide"), None),
        P(("narrow", "wide")),
        P(("narrow", "wide"), None, None, None),
        P(None, ("narrow", "wide")),
        P(None, "wide", "narrow"),
    )
    out_specs = (P(None, ("narrow", "wide"), None), P(), P())
    return jax.shard_map(body, mesh=mesh, in_specs=in_specs, out_specs=out_specs, check_vma=False)
```

```python
import functools

import jax
import jax.numpy as jnp
from jax import lax
from jax.experimental import pallas as pl
from jax.experimental.pallas import tpu as pltpu
from jax.sharding import PartitionSpec as P

SPAN = 4


NU = 0.3
DELTA2 = 1e-05
ELASTIC = 40.0
AXES = ("narrow", "wide")
EXTRA = 8
WHOLE_BYTES = 8 * 1024 * 1024
ROWS = 8
SMEM = pl.BlockSpec(memory_space=pltpu.SMEM)
VMEM = pl.BlockSpec(memory_space=pltpu.VMEM)
ANY = pl.BlockSpec(memory_space=pl.ANY)
PARAMS = pltpu.CompilerParams(vmem_limit_bytes=48 * 1024 * 1024)


def split(value):
    high = value.astype(jnp.bfloat16)
    return high, (value - high.astype(jnp.float32)).astype(jnp.bfloat16)


def dot16(left, right, contract=((1,), (0,))):
    return lax.dot_general(left, right, (contract, ((), ())), preferred_element_type=jnp.float32)


def dot_rows(left, right, contract=((1,), (0,))):
    left_high, left_low = split(left)
    right_high, right_low = split(right)
    return dot16(left_high, right_high, contract) + (
        dot16(left_high, right_low, contract) + dot16(left_low, right_high, contract)
    )


def dot_first(left, right):
    return dot_rows(left, right, ((0,), (0,)))


def pick(member, value, contract=((1,), (0,))):
    member = member.astype(jnp.bfloat16)
    high, low = split(value)
    lowest = (value - high.astype(jnp.float32) - low.astype(jnp.float32)).astype(jnp.bfloat16)
    return dot16(member, high, contract) + (
        dot16(member, low, contract) + dot16(member, lowest, contract)
    )


def as_column(row, width):
    return jnp.transpose(jnp.broadcast_to(row, (width, row.shape[1])))


def flip(block, mask):
    count = lax.axis_size(AXES)
    return lax.ppermute(block, AXES, [(i, i ^ mask) for i in range(count)])


def masks_of(count, scale=1):
    return [scale << bit for bit in range(count.bit_length() - 1)]


def in_pairs(masks):
    return [masks[k : k + 2] for k in range(0, len(masks), 2)]


def combined(group, number):
    mask = 0
    for bit, part in enumerate(group):
        if number >> bit & 1:
            mask ^= part
    return mask


def flip_each(parts, group):
    return [parts[0]] + [flip(parts[j], combined(group, j)) for j in range(1, 1 << len(group))]


def farthest_first(parts):
    return [parts[0], *parts[:0:-1]]


def join_kernel(count, *refs):
    parts, out_ref = farthest_first(refs[-1 - count : -1]), refs[-1]
    size = parts[0].shape[0]
    for j, ref in enumerate(parts):
        out_ref[j * size : (j + 1) * size] = ref[...]


def join(parts, after=()):
    shape = (len(parts) * parts[0].shape[0],) + parts[0].shape[1:]
    return pl.pallas_call(
        functools.partial(join_kernel, len(parts)),
        out_shape=jax.ShapeDtypeStruct(shape, parts[0].dtype),
        in_specs=[ANY] * len(after) + [VMEM] * len(parts),
        out_specs=VMEM,
        compiler_params=PARAMS,
    )(*after, *farthest_first(parts))


def gather_steps(held, groups, after=()):
    parts = [held]
    for group in groups:
        if len(parts) > 1:
            held = join(parts, after)
            after = ()
        parts = flip_each([held] * (1 << len(group)), group)
    return parts


def gather_order(groups):
    order = [0]
    for group in groups:
        order = [k ^ combined(group, j) for j in range(1 << len(group)) for k in order]
    return order


def total_of(values):
    while len(values) > 1:
        values = [values[k] + values[k + 1] for k in range(0, len(values), 2)]
    return values[0]


def sum_kernel(count, skip, *refs):
    parts, outs = refs[skip : skip + count], refs[skip + count :]
    for k in range(outs[0].shape[0]):
        for j, out_ref in enumerate(outs):
            out_ref[k] = total_of([part[k * len(outs) + j] for part in parts])


def sum_parts(parts, ways, after=()):
    out = f32(parts[0].shape[0] // ways, *parts[0].shape[1:])
    return pl.pallas_call(
        functools.partial(sum_kernel, len(parts), len(after)),
        out_shape=[out] * ways,
        in_specs=[ANY] * len(after) + [VMEM] * len(parts),
        out_specs=[VMEM] * ways,
        compiler_params=PARAMS,
    )(*after, *farthest_first(parts))


def scatter_steps(parts, groups):
    for number, group in enumerate(groups):
        if number:
            parts = sum_parts(parts, 1 << len(group))
        parts = flip_each(parts, group)
    return parts


def sum_butterfly(total, groups):
    for group in groups:
        (total,) = sum_parts(flip_each([total] * (1 << len(group)), group), 1)
    return total


def append_kernel(left_ref, right_ref, out_ref):
    rows = left_ref.shape[1]
    out_ref[:, :rows, :] = left_ref[...]
    out_ref[:, rows:, :] = right_ref[...]


def append(left, right):
    count, rows, width = left.shape
    shape = f32(count, rows + right.shape[1], width)
    return call(append_kernel, shape, (left, right))


def part_groups(groups):
    bit, found = 0, []
    for group in groups:
        found.append([1 << (bit + k) for k in range(len(group))])
        bit += len(group)
    return found


def bits_of(index, masks):
    packed = 0
    for bit, mask in enumerate(masks):
        packed = packed + (lax.shift_right_logical(index, mask.bit_length() - 1) & 1) * (1 << bit)
    return packed


def members(agg_ref, a, coarse_count):
    ids = lax.broadcasted_iota(jnp.int32, (coarse_count, agg_ref.shape[1]), 0)
    return jnp.where(ids == agg_ref[a : a + 1, :], 1.0, 0.0)


def load_all(pairs, sems):
    copies = [
        pltpu.make_async_copy(source, target, sems.at[k])
        for k, (source, target) in enumerate(pairs)
    ]
    for copy in copies:
        copy.start()
    for copy in copies:
        copy.wait()


def restrict_kernel(
    agg_hbm, basis_hbm, points_hbm, weight_hbm, pack_ref, agg_ref, newest_ref, points_ref, weight_ref, sems
):
    coarse_count = pack_ref.shape[1] - EXTRA
    point_count = newest_ref.shape[1]
    load_all(
        [
            (basis_hbm.at[basis_hbm.shape[0] - 1], newest_ref),
            (agg_hbm, agg_ref),
            (points_hbm, points_ref),
            (weight_hbm, weight_ref),
        ],
        sems,
    )
    total = pick(members(agg_ref, 0, coarse_count), newest_ref[0]) + pick(
        members(agg_ref, 1, coarse_count), newest_ref[1]
    )
    pack_ref[0, :coarse_count, :] = total
    pack_ref[0, coarse_count:, :] = jnp.concatenate(
        [points_ref[...], weight_ref[...], jnp.zeros((EXTRA - 3, point_count), jnp.float32)], axis=0
    )


def prefetch_kernel(
    masks,
    index_ref,
    pack_hbm,
    agg_hbm,
    basis_hbm,
    jacobi_hbm,
    weight_hbm,
    inverse_hbm,
    inverse_ref,
    member_ref,
    smooth_ref,
    weight_out_ref,
    keep_ref,
    send_ref,
    half_ref,
    agg_ref,
    basis_ref,
    jacobi_ref,
    weight_ref,
    sems,
):
    coarse_count = member_ref.shape[1]
    block_total, _, _, rhs_count = basis_ref.shape
    load_all(
        [
            (basis_hbm, basis_ref),
            (agg_hbm, agg_ref),
            (jacobi_hbm, jacobi_ref),
            (weight_hbm, weight_ref),
            (inverse_hbm, inverse_ref),
        ],
        sems,
    )
    for a in range(2):
        member_ref[a] = members(agg_ref, a, coarse_count)
        smooth_ref[a] = (
            as_column(jacobi_ref[a : a + 1, :], rhs_count) * basis_ref[block_total - 1, a]
        )
    weight = as_column(weight_ref[...], rhs_count)
    weight_out_ref[...] = weight
    right = stacked(basis_ref)
    number = 0
    for i in range(block_total):
        left = jnp.concatenate([basis_ref[i, a] * weight for a in range(2)], axis=0)
        row = dot_first(left, right[:, i * rhs_count :])
        for j in range(i, block_total):
            block = row[:, (j - i) * rhs_count : (j - i + 1) * rhs_count]
            rows = slice(number * rhs_count, (number + 1) * rhs_count)
            half_ref[rows, :] = block * 0.5 if i == j else block
            number += 1
    spread(half_ref, (keep_ref, send_ref), bits_of(index_ref[2], masks))


def part_at(parts, k):
    size = parts[0].shape[0]
    return parts[k // size], k % size


def coarse_kernel(order, ways, z_count, index_ref, near_ref, inverse_ref, *refs):
    narrow_count, coarse_count, _ = inverse_ref.shape
    packs = refs[: len(refs) - ways - 3]
    outs = refs[len(packs) : len(packs) + ways]
    source_ref, target_ref, rhs_ref = refs[len(packs) + ways :]
    for k, offset in enumerate(order):
        first = pl.multiple_of((index_ref[1] ^ offset) * coarse_count, 8)
        ref, row = part_at(packs, k)
        rhs_ref[pl.ds(first, coarse_count), :] = ref[row, :coarse_count, :]
    for k in range(z_count):
        ref, row = part_at(packs, k)
        source_ref[k] = ref[row, coarse_count:, :]
    for k in range(target_ref.shape[0]):
        ref, row = part_at(packs, k * z_count)
        target_ref[k] = ref[row, coarse_count:, :]
    left = jnp.concatenate(
        [inverse_ref[index_ref[0] ^ k] for k in range(narrow_count)], axis=0
    )
    product = dot_rows(left, rhs_ref[...])
    tail = jnp.concatenate([source_ref[k] for k in range(z_count)], axis=0)
    each = z_count * EXTRA // (narrow_count // ways)
    for k in range(narrow_count):
        part = product[k * coarse_count : (k + 1) * coarse_count, :]
        outs[k % ways][k // ways, :coarse_count, :] = part
        first = (k // ways) * each
        outs[k % ways][k // ways, coarse_count:, :] = tail[first : first + each, :]


def coarse_sum_kernel(ways, kept_ref, got_ref, target_ref, *refs):
    outs, source_ref = refs[:ways], refs[ways]
    rows = target_ref.shape[0] * EXTRA
    coarse_count = outs[0].shape[1] - rows
    each = (kept_ref.shape[1] - coarse_count) // EXTRA
    for k in range(kept_ref.shape[0]):
        for j in range(each):
            first = coarse_count + j * EXTRA
            source_ref[k * each + j] = got_ref[k, first : first + EXTRA, :]
    for k in range(outs[0].shape[0]):
        for j in range(ways):
            source = k * ways + j
            outs[j][k, :coarse_count, :] = (
                kept_ref[source, :coarse_count, :] + got_ref[source, :coarse_count, :]
            )
            for t in range(target_ref.shape[0]):
                first = coarse_count + t * EXTRA
                outs[j][k, first : first + EXTRA, :] = target_ref[t]


def precond_kernel(index_ref, half_hbm, member_ref, smooth_ref, *refs):
    parts = refs[:-3]
    precond_ref, pair_ref, next_ref = refs[-3:]
    coarse_count = member_ref.shape[1]
    point_count = smooth_ref.shape[1]
    width = pair_ref.shape[1]
    even = (index_ref[2] & 1) == 0
    coarse_sol = total_of([part[0, :coarse_count, :] for part in parts])
    for a in range(2):
        value = smooth_ref[a] + pick(member_ref[a], coarse_sol, ((0,), (0,)))
        precond_ref[0, a] = value.astype(jnp.bfloat16)
        first = value[:width]
        last = value[point_count - width :]
        pair_ref[a] = jnp.where(even, last, first).astype(jnp.bfloat16)
        next_ref[a] = jnp.where(even, first, last).astype(jnp.bfloat16)


def matrix_kernel(coarse_count, own_ref, other_ref, *refs):
    targets, matrix_ref = refs[:-1], refs[-1]
    point_count = own_ref.shape[2]
    size = (targets[0].shape[1] - coarse_count) // EXTRA
    step = pl.program_id(0)
    first = pl.multiple_of(coarse_count + lax.rem(step, size) * EXTRA, EXTRA)
    target = targets[0][0, pl.ds(first, EXTRA), :]
    for j in range(1, len(targets)):
        target = jnp.where(step // size == j, targets[j][0, pl.ds(first, EXTRA), :], target)
    target_x = as_column(target[0:1, :], point_count)
    target_y = as_column(target[1:2, :], point_count)
    for s in range(matrix_ref.shape[3] // point_count):
        ref, row = part_at((own_ref, other_ref), s)
        source = ref[row]
        delta_x = target_x - source[0:1, :]
        delta_y = target_y - source[1:2, :]
        factor = ELASTIC * source[2:3, :]
        square_x = delta_x * delta_x
        square_y = delta_y * delta_y
        square_dist = square_x + square_y + DELTA2
        inverse = 1.0 / square_dist
        log_part = (-0.5 * (3.0 - 4.0 * NU)) * jnp.log(square_dist)
        lanes = slice(s * point_count, (s + 1) * point_count)
        matrix_ref[0, 0, :, lanes] = (factor * (log_part + square_x * inverse)).astype(jnp.bfloat16)
        matrix_ref[0, 1, :, lanes] = (factor * (delta_x * delta_y * inverse)).astype(jnp.bfloat16)
        matrix_ref[0, 2, :, lanes] = (factor * (log_part + square_y * inverse)).astype(jnp.bfloat16)


def far_kernel(ways, matrix_ref, field_ref, *refs):
    earlier, outs, fields_ref = refs[: -1 - ways], refs[-1 - ways : -1], refs[-1]
    point_count, rhs_count = field_ref.shape[2:]
    step = pl.program_id(0)

    @pl.when(step == 0)
    def _():
        for s in range(field_ref.shape[0]):
            for b in range(2):
                rows = slice(s * point_count, (s + 1) * point_count)
                fields_ref[rows, b * rhs_count : (b + 1) * rhs_count] = field_ref[s, b]

    mixed = dot16(matrix_ref[0, 1], fields_ref[...])
    out_x = dot16(matrix_ref[0, 0], fields_ref[:, :rhs_count]) + mixed[:, rhs_count:]
    out_y = dot16(matrix_ref[0, 2], fields_ref[:, rhs_count:]) + mixed[:, :rhs_count]
    for j, out_ref in enumerate(outs):

        @pl.when(lax.rem(step, ways) == j)
        def _(j=j, out_ref=out_ref):
            row = step // ways
            if earlier:
                out_ref[row, 0] = out_x + earlier[j][row, 0]
                out_ref[row, 1] = out_y + earlier[j][row, 1]
            else:
                out_ref[row, 0] = out_x
                out_ref[row, 1] = out_y


def far_whole_kernel(ways, number, matrix_ref, field_ref, *refs):
    earlier, outs, fields_ref = refs[: -1 - ways], refs[-1 - ways : -1], refs[-1]
    point_count, rhs_count = field_ref.shape[2:]
    for s in range(field_ref.shape[0]):
        for b in range(2):
            rows = slice(s * point_count, (s + 1) * point_count)
            fields_ref[rows, b * rhs_count : (b + 1) * rhs_count] = field_ref[s, b]
    size = fields_ref.shape[0]
    lanes = slice(number * size, (number + 1) * size)
    for k in range(matrix_ref.shape[0]):
        mixed = dot16(matrix_ref[k, 1, :, lanes], fields_ref[...])
        out_x = dot16(matrix_ref[k, 0, :, lanes], fields_ref[:, :rhs_count])
        out_y = dot16(matrix_ref[k, 2, :, lanes], fields_ref[:, rhs_count:])
        sums = [out_x + mixed[:, rhs_count:], out_y + mixed[:, :rhs_count]]
        for a in range(2):
            if earlier:
                sums[a] = sums[a] + earlier[k % ways][k // ways, a]
            outs[k % ways][k // ways, a] = sums[a]


def near_kernel(
    index_ref,
    panel_ref,
    count_ref,
    block_ref,
    own_ref,
    pair_ref,
    next_ref,
    out_ref,
    line_ref,
    gathered_ref,
):
    point_count = own_ref.shape[2]
    width = pair_ref.shape[1]
    even = (index_ref[2] & 1) == 0
    panels_dev, double_nodes, _ = block_ref.shape
    nodes = double_nodes // 2
    slot_total = panel_ref.shape[1]
    for b in range(2):
        pair = pair_ref[b].astype(jnp.float32)
        following = next_ref[b].astype(jnp.float32)
        line_ref[b, :width, :] = jnp.where(even, following, pair).astype(jnp.bfloat16)
        line_ref[b, width : width + point_count, :] = own_ref[0, b]
        line_ref[b, width + point_count :, :] = jnp.where(even, pair, following).astype(
            jnp.bfloat16
        )
    first_panel = index_ref[2] * panels_dev
    lane = lax.broadcasted_iota(jnp.int32, block_ref.shape[1:], 1)
    for p in range(panels_dev):
        for k in range(slot_total):
            first = pl.multiple_of((panel_ref[p, k] - first_panel) * nodes + width, 16)
            for b in range(2):
                row = (k * 2 + b) * nodes
                gathered_ref[p, row : row + nodes, :] = line_ref[b, pl.ds(first, nodes), :]
        blocks = jnp.where(
            lane < count_ref[p] * double_nodes, block_ref[p].astype(jnp.float32), 0.0
        ).astype(jnp.bfloat16)
        near = dot16(blocks, gathered_ref[p])
        for a in range(2):
            rows = slice(p * nodes, (p + 1) * nodes)
            own = own_ref[0, a, rows, :].astype(jnp.float32)
            out_ref[a, rows, :] = 0.5 * own + near[a * nodes : (a + 1) * nodes, :]


def spread(full_ref, outs, own):
    rows = outs[0].shape[1]
    for k in range(len(outs) * outs[0].shape[0]):
        first = pl.multiple_of((own ^ k) * rows, 8)
        outs[k % len(outs)][k // len(outs)] = full_ref[pl.ds(first, rows), :]


def collect(order, parts, full_ref, own, start):
    rows = full_ref.shape[0] // len(order)
    for k, offset in enumerate(order):
        first = pl.multiple_of((own ^ offset) * rows, 8)
        ref, row = part_at(parts, k)
        full_ref[pl.ds(first, rows), :] = ref[row, start : start + rows, :]


def stacked(basis_ref):
    return jnp.concatenate(
        [
            jnp.concatenate([basis_ref[j, a] for j in range(basis_ref.shape[0])], axis=1)
            for a in range(2)
        ],
        axis=0,
    )


def project_kernel(masks, ways, index_ref, half_hbm, weight_ref, basis_ref, base_ref, *refs):
    arrived = refs[: len(refs) - ways - 2]
    image_ref = refs[len(arrived)]
    outs = refs[len(arrived) + 1 : -1]
    full_ref = refs[-1]
    weighted = []
    for a in range(2):
        image = base_ref[a] + total_of([part[0, a] for part in arrived])
        image_ref[a] = image
        weighted.append(image * weight_ref[...])
    image = jnp.concatenate([image_ref[0], image_ref[1]], axis=0)
    left = jnp.concatenate([stacked(basis_ref), image], axis=1)
    full_ref[...] = dot_first(left, jnp.concatenate(weighted, axis=0))
    spread(full_ref, outs, bits_of(index_ref[2], masks))


def factor_kernel(gather, masks, index_ref, basis_ref, image_ref, *refs):
    parts = refs[:-7]
    hess_ref, upper_ref, new_ref, full_ref, half_ref, work_ref, inverse_ref = refs[-7:]
    block_total, _, _, order = basis_ref.shape
    hess_rows = block_total * order
    tile = (ROWS, order)
    lane = lax.broadcasted_iota(jnp.int32, tile, 1)
    row = lax.broadcasted_iota(jnp.int32, tile, 0)
    own = bits_of(index_ref[2], masks)
    collect(gather, parts, full_ref, own, 0)
    collect(gather, parts, half_ref, own, full_ref.shape[0] // len(gather))
    hessenberg = full_ref[:hess_rows, :]
    hess_ref[...] = hessenberg
    rows = []
    number = 0
    for i in range(block_total):
        count = block_total - i
        left = jnp.concatenate(
            [
                half_ref[(number + j) * order : (number + j + 1) * order, :]
                for j in range(count)
            ],
            axis=1,
        )
        rows.append(dot_rows(left, full_ref[i * order : hess_rows, :]))
        number += count
    product = dot_first(hessenberg, jnp.concatenate(rows, axis=0) - hessenberg)
    work_ref[...] = full_ref[hess_rows:, :] + (product + jnp.transpose(product))
    for block in range(order // ROWS):
        start = block * ROWS
        inverse_ref[start : start + ROWS, :] = jnp.where(lane == row + start, 1.0, 0.0)
    for block in range(order // ROWS):
        start = block * ROWS
        own = work_ref[start : start + ROWS, :]
        own_inverse = inverse_ref[start : start + ROWS, :]
        columns = [
            jnp.broadcast_to(own[:, start + m : start + m + 1], tile) for m in range(ROWS)
        ]
        entry = {
            (j, m): jnp.broadcast_to(columns[m][j : j + 1, :], tile)
            for m in range(ROWS)
            for j in range(m, ROWS)
        }
        scale = []
        for m in range(ROWS):
            scale.append(lax.rsqrt(entry[m, m]))
            for j in range(m + 1, ROWS):
                entry[j, m] = entry[j, m] * scale[m]
            for n in range(m + 1, ROWS):
                for j in range(n, ROWS):
                    entry[j, n] = entry[j, n] - entry[j, m] * entry[n, m]
        solved = []
        solved_inverse = []
        for m in range(ROWS):
            upper_row = jnp.broadcast_to(own[m : m + 1, :], tile)
            inverse_row = jnp.broadcast_to(own_inverse[m : m + 1, :], tile)
            for j in range(m):
                upper_row = upper_row - entry[m, j] * solved[j]
                inverse_row = inverse_row - entry[m, j] * solved_inverse[j]
            upper_row = upper_row * scale[m]
            inverse_row = inverse_row * scale[m]
            solved.append(upper_row)
            solved_inverse.append(inverse_row)
        upper_rows = solved[ROWS - 1]
        inverse_rows = solved_inverse[ROWS - 1]
        for m in range(ROWS - 1):
            upper_rows = jnp.where(row == m, solved[m], upper_rows)
            inverse_rows = jnp.where(row == m, solved_inverse[m], inverse_rows)
        upper_ref[start : start + ROWS, :] = jnp.where(lane >= row + start, upper_rows, 0.0)
        inverse_ref[start : start + ROWS, :] = inverse_rows
        for later in range(block + 1, order // ROWS):
            first = later * ROWS
            target = work_ref[first : first + ROWS, :]
            target_inverse = inverse_ref[first : first + ROWS, :]
            multiplier = []
            for m in range(ROWS):
                value = jnp.broadcast_to(target[:, start + m : start + m + 1], tile)
                for j in range(m):
                    value = value - multiplier[j] * entry[m, j]
                multiplier.append(value * scale[m])
            for m in range(ROWS):
                target = target - multiplier[m] * solved[m]
                target_inverse = target_inverse - multiplier[m] * solved_inverse[m]
            work_ref[first : first + ROWS, :] = target
            inverse_ref[first : first + ROWS, :] = target_inverse
    image = jnp.concatenate([image_ref[0], image_ref[1]], axis=0)
    remainder = image - dot_rows(stacked(basis_ref), hessenberg)
    new_ref[...] = dot_rows(remainder, inverse_ref[...], ((1,), (1,)))


def f32(*shape):
    return jax.ShapeDtypeStruct(shape, jnp.float32)


def b16(*shape):
    return jax.ShapeDtypeStruct(shape, jnp.bfloat16)


def call(kernel, out_shape, operands, scalars=0, scratch=(), in_hbm=0):
    many = isinstance(out_shape, (tuple, list))
    free = len(operands) - in_hbm
    operands = list(operands[:free]) + [
        pltpu.with_memory_space_constraint(x, pltpu.HBM) for x in operands[free:]
    ]
    return pl.pallas_call(
        kernel,
        out_shape=out_shape,
        in_specs=[SMEM] * scalars + [ANY if in_hbm else VMEM] * (len(operands) - scalars),
        out_specs=[VMEM] * len(out_shape) if many else VMEM,
        scratch_shapes=list(scratch),
        compiler_params=PARAMS,
    )(*operands)


def body(
    points,
    quad_weight,
    basis,
    jacobi,
    near_panel,
    near_count,
    near_block,
    agg_index,
    coarse_inverse,
):
    block_total, _, point_count, rhs_count = basis.shape
    coarse_count = coarse_inverse.shape[1]
    narrow_count = lax.axis_size("narrow")
    wide_count = lax.axis_size("wide")
    panels_dev, slot_total = near_panel.shape
    nodes = near_block.shape[2] // 2
    width = SPAN * nodes
    pack_rows = coarse_count + EXTRA
    index = jnp.stack(
        [lax.axis_index("narrow"), lax.axis_index("wide"), lax.axis_index(AXES)]
    ).astype(jnp.int32)
    weight_row = quad_weight[None, :]
    low, *high = masks_of(wide_count)
    core, *across = masks_of(narrow_count, wide_count)
    high_groups = in_pairs(high)
    plane_groups = in_pairs([low] + across)
    wide_groups = high_groups + [[low]]
    narrow_groups = [[core]] + in_pairs(across)
    source_groups = high_groups + [[core]]
    high_count = 1 << len(high)
    source_total = 2 * high_count * point_count
    target_count = narrow_count
    pair_row = pltpu.VMEM((2, point_count), jnp.float32)
    one_row = pltpu.VMEM((1, point_count), jnp.float32)
    pair_index = pltpu.VMEM((2, point_count), jnp.int32)
    field = pltpu.VMEM((2, point_count, rhs_count), jnp.float32)

    pack = call(
        restrict_kernel,
        f32(1, pack_rows, point_count),
        (agg_index, basis, points, weight_row),
        0,
        [pair_index, field, pair_row, one_row, pltpu.SemaphoreType.DMA((4,))],
        4,
    )
    half_rows = block_total * (block_total + 1) // 2 * rhs_count
    halving = [[core]] + plane_groups
    masks = [core, low] + across
    inverse, member, smooth, weight, *half_parts = call(
        functools.partial(prefetch_kernel, masks),
        [
            f32(*coarse_inverse.shape),
            f32(2, coarse_count, point_count),
            f32(2, point_count, rhs_count),
            f32(point_count, rhs_count),
        ]
        + [f32(narrow_count, half_rows // (2 * narrow_count), rhs_count)] * 2,
        (index, pack, agg_index, basis, jacobi, weight_row, coarse_inverse),
        1,
        [
            pltpu.VMEM((half_rows, rhs_count), jnp.float32),
            pair_index,
            pltpu.VMEM(basis.shape, jnp.float32),
            pair_row,
            one_row,
            pltpu.SemaphoreType.DMA((5,)),
        ],
        5,
    )
    near_rows = jnp.transpose(near_block, (0, 2, 1, 3)).reshape(
        panels_dev, 2 * nodes, slot_total * 2 * nodes
    )
    packs = flip_each([pack] * (1 << len(wide_groups[0])), wide_groups[0])
    pack = join(packs, (weight,))
    half_send = join(half_parts[1:], (pack,))
    packs = gather_steps(pack, wide_groups[1:])
    source_rows = high_count * EXTRA // (narrow_count // 2)
    target_rows = 2 * EXTRA
    coarse_outs = pl.pallas_call(
        functools.partial(
            coarse_kernel, gather_order(wide_groups), 2, high_count
        ),
        out_shape=[f32(narrow_count // 2, coarse_count + source_rows, rhs_count)] * 2
        + [f32(high_count, EXTRA, point_count), f32(2, EXTRA, point_count)],
        in_specs=[SMEM, ANY, VMEM] + [VMEM] * len(packs),
        out_specs=[VMEM] * 4,
        scratch_shapes=[pltpu.VMEM((wide_count * coarse_count, rhs_count), jnp.float32)],
        compiler_params=PARAMS,
    )(index, near_rows, inverse, *packs)
    own_sources = coarse_outs[2]
    kept, got = flip_each(coarse_outs[:2], [core])
    groups = in_pairs(across)
    ways = 1 << len(groups[0])
    *coarse_parts, other_sources = call(
        functools.partial(coarse_sum_kernel, ways),
        [f32(narrow_count // 2 // ways, coarse_count + target_rows, rhs_count)] * ways
        + [f32(high_count, EXTRA, point_count)],
        (kept, got, coarse_outs[3]),
    )
    half_parts = flip_each([half_parts[0], half_send], [core])
    half_parts = sum_parts(half_parts, 2)
    half_steps = []
    for number, mask in enumerate([low] + across + high):
        got = flip_each(half_parts, [mask])
        half_steps.append(got[1])
        half_parts = sum_parts(got, 2 if number < len(across) else 1)
        if len(half_parts) == 1:
            half_parts = half_parts * 2
    half_total = half_parts[0]
    coarse_parts = scatter_steps(coarse_parts, groups)
    precond, pair_edge, next_edge = pl.pallas_call(
        precond_kernel,
        out_shape=[b16(1, 2, point_count, rhs_count)] + [b16(2, width, rhs_count)] * 2,
        in_specs=[SMEM, ANY] + [VMEM] * (2 + len(coarse_parts)),
        out_specs=[VMEM] * 3,
        compiler_params=PARAMS,
    )(index, half_steps[0], member, smooth, *coarse_parts)
    matrix_spec = pl.BlockSpec((1, 3, point_count, source_total), lambda k: (k, 0, 0, 0))
    matrix = pl.pallas_call(
        functools.partial(matrix_kernel, coarse_count),
        out_shape=b16(target_count, 3, point_count, source_total),
        grid=(target_count,),
        in_specs=[VMEM] * (2 + len(coarse_parts)),
        out_specs=matrix_spec,
        compiler_params=PARAMS,
    )(own_sources, other_sources, *coarse_parts)
    device_count = narrow_count * wide_count
    pair_edge = flip(pair_edge, 1)
    pairs = [(i, i + 1) for i in range(1, device_count - 1, 2)]
    next_edge = lax.ppermute(next_edge, AXES, pairs + [(j, i) for i, j in pairs])
    fields = flip_each([precond] * (1 << len(source_groups[0])), source_groups[0])
    after = (matrix, half_steps[1], next_edge)
    fields = gather_steps(join(fields, after), source_groups[1:])

    ways = 1 << len(plane_groups[0])
    far_parts = []
    far_out = [f32(target_count // ways, 2, point_count, rhs_count)] * ways
    far_scratch = [pltpu.VMEM((source_total // 2, 2 * rhs_count), jnp.bfloat16)]
    for number, field in enumerate(fields):
        if matrix.size * 2 <= WHOLE_BYTES:
            kernel = functools.partial(far_whole_kernel, ways, number)
            far_parts = call(kernel, far_out, (matrix, field, *far_parts), 0, far_scratch)
            continue
        far_parts = pl.pallas_call(
            functools.partial(far_kernel, ways),
            out_shape=far_out,
            grid=(target_count,),
            in_specs=[
                pl.BlockSpec(
                    (1, 3, point_count, source_total // 2),
                    lambda k, number=number: (k, 0, 0, number),
                )
            ]
            + [VMEM] * (1 + len(far_parts)),
            out_specs=[VMEM] * ways,
            scratch_shapes=far_scratch,
            compiler_params=PARAMS,
        )(matrix, field, *far_parts)
    far_parts = scatter_steps(far_parts, plane_groups)
    base = call(
        near_kernel,
        f32(2, point_count, rhs_count),
        (index, near_panel, near_count, near_rows, precond, pair_edge, next_edge),
        3,
        [
            pltpu.VMEM((2, 2 * width + point_count, rhs_count), jnp.bfloat16),
            pltpu.VMEM((panels_dev, slot_total * 2 * nodes, rhs_count), jnp.bfloat16),
        ],
    )

    hess_rows = block_total * rhs_count
    sum_rows = hess_rows + rhs_count
    image, *parts = pl.pallas_call(
        functools.partial(project_kernel, masks, 2),
        out_shape=[f32(2, point_count, rhs_count)]
        + [f32(narrow_count, sum_rows // (2 * narrow_count), rhs_count)] * 2,
        in_specs=[SMEM] + [ANY] + [VMEM] * (3 + len(far_parts)),
        out_specs=[VMEM] * 3,
        scratch_shapes=[pltpu.VMEM((sum_rows, rhs_count), jnp.float32)],
        compiler_params=PARAMS,
    )(index, half_steps[2], weight, basis, base, *farthest_first(far_parts))
    (total,) = sum_parts(scatter_steps(parts, halving), 1, half_steps[3:4])
    total = sum_butterfly(total, high_groups)
    parts = gather_steps(append(total, half_total), halving[::-1])
    hessenberg, upper_factor, new_block = call(
        functools.partial(factor_kernel, gather_order(part_groups(halving)[::-1]), masks),
        [
            f32(hess_rows, rhs_count),
            f32(rhs_count, rhs_count),
            f32(2 * point_count, rhs_count),
        ],
        (index, basis, image, *parts),
        1,
        [
            pltpu.VMEM((sum_rows, rhs_count), jnp.float32),
            pltpu.VMEM((half_rows, rhs_count), jnp.float32),
        ]
        + [pltpu.VMEM((rhs_count, rhs_count), jnp.float32)] * 2,
    )
    return (
        new_block.reshape(2, point_count, rhs_count),
        hessenberg.reshape(block_total, rhs_count, rhs_count),
        upper_factor,
    )


def solution(mesh):
    in_specs = (
        P(None, ("narrow", "wide")),
        P(("narrow", "wide")),
        P(None, None, ("narrow", "wide"), None),
        P(None, ("narrow", "wide")),
        P(("narrow", "wide"), None),
        P(("narrow", "wide")),
        P(("narrow", "wide"), None, None, None),
        P(None, ("narrow", "wide")),
        P(None, "wide", "narrow"),
    )
    out_specs = (P(None, ("narrow", "wide"), None), P(), P())
    return jax.shard_map(body, mesh=mesh, in_specs=in_specs, out_specs=out_specs, check_vma=False)
```
